32 devices in a mesh: wide: 8 (over y, x, core), narrow: 4 (over z).
Axes of the slice: x: 2, y: 2, z: 4, core: 2. Of those that a mesh axis runs over, the one named last changes fastest.
Arguments:
- amplitudes: bfloat16 [256, 4, 4096], P('wide', None, 'narrow'), may hold values from -6 to 6
- amp_tiles: int32 [8, 4], replicated, may hold values from 0 to 7, all different within a row
- integrals: bfloat16 [8, 2, 4096, 4096], P('wide', None, None, 'narrow'), may hold values from -0.09375 to 0.09375
- cd_tiles: int32 [8, 2], replicated, may hold values from 0 to 7, all different within a row
- q_owner: int32 [8], replicated, may hold values from 0 to 7, each once
Outputs:
- residual: bfloat16 [256, 8, 4096], P('wide', None, 'narrow')
The draws below stay inside these ranges and needn't reach their ends.
Inputs may be any that keep to these rules, and one draw needn't show every extreme that they name: `amp_tiles`: within a row, the 4 tiles are different. `cd_tiles`: within a row, the 2 tiles are different; every tile is named by some row. `q_owner`: each owner index appears once.
All inputs are finite; a program needn't handle non-finite values.
Results may differ from the reference program's by a relative error of at most 0.017.
Values may be sent and summed in bfloat16 or wider, within the bound.
No kernel may reach another device: no remote copies, remote signals or barrier semaphores. Data moves between devices by JAX's collectives and lax.ppermute only.
A program may use at most 64 MiB of HBM per device.

```python
import jax
import jax.numpy as jnp
from jax import lax

KV = 2
PAIR = 4096
NS = 8
NBLK = 8
TW = 4
OCC_PAIRS = 256
N_NARROW = 4


def shard_levels(rng, extent, shards, least, high):
    factor_of, own = 1.0, jax.random.fold_in(rng, 6)
    for axis_at, shards_of in shards:
        draws = jnp.exp(jax.random.uniform(jax.random.fold_in(own, axis_at), (shards_of,), jnp.float32, least / len(shards), high / len(shards)))
        factor_of = factor_of * jnp.repeat(draws, extent[axis_at] // shards_of).reshape([-1 if axis == axis_at else 1 for axis in range(len(extent))])
    return factor_of


def different_ones(stream_key, rows, amount, top, lift):
    sequence = jax.random.permutation(jax.random.fold_in(stream_key, 1), amount)
    favour = sequence
    for power in range(3):
        favour = favour * favour // amount
    favour = favour * lift // amount
    lots = jax.random.randint(jax.random.fold_in(stream_key, 2), (rows, amount), 0, 4096) + favour
    holders = jax.random.permutation(jax.random.fold_in(stream_key, 3), rows)[jnp.arange(amount) % rows]
    lots = jnp.where(jnp.arange(rows)[:, None] == holders[None, :], 1 << 14, lots)
    merit = lots * amount + jnp.arange(amount)
    return lax.top_k(merit.astype(jnp.int32), top)[1].astype(jnp.int32)


def centred(own_key, shape, width, limit, cuts=(), held_as=jnp.bfloat16):
    entries = jax.random.normal(own_key, shape, jnp.float32) * width
    if len(cuts) > 0:
        entries = shard_levels(own_key, shape, cuts, -0.22, 0.18) * entries
    return jnp.clip(entries, min=-limit, max=limit).astype(held_as)


def setup_inputs(seed: int = 0) -> dict:
    keys = jax.random.split(jax.random.key(seed), 6)
    amplitudes = centred(keys[0], (OCC_PAIRS, TW, PAIR), 1.0, 6.0, ((0, 8), (2, 4)))
    amp_tiles = different_ones(keys[1], NBLK, NS, TW, 8192)
    integrals = centred(keys[2], (NS, KV, PAIR, PAIR), (KV * PAIR // 2) ** -0.5, 0.09375, ((0, 8), (3, 4)))
    cd_tiles = different_ones(keys[3], NS, NS, KV, 0)
    q_owner = jax.random.permutation(keys[4], NS).astype(jnp.int32)
    return dict(amplitudes=amplitudes, amp_tiles=amp_tiles, integrals=integrals, cd_tiles=cd_tiles, q_owner=q_owner)


def reference(amplitudes, amp_tiles, integrals, cd_tiles, q_owner):
    nblk = amp_tiles.shape[0]
    rows_dev = amplitudes.shape[0] // nblk
    tile_width = amp_tiles.shape[1]
    block_amps = amplitudes.reshape(nblk, rows_dev, tile_width, PAIR).astype(jnp.float32)

    def one_tile(tile):
        owner_slot = q_owner[tile]
        tile_ints = integrals[owner_slot].astype(jnp.float32).reshape(KV, PAIR, N_NARROW, PAIR // N_NARROW)
        wanted = cd_tiles[tile]
        picker = (amp_tiles[:, :, None] == wanted[None, None, :]).astype(jnp.float32)
        chosen = jnp.einsum("btk,brtc->brkc", picker, block_amps, precision=lax.Precision.HIGHEST)
        chosen = chosen.reshape(nblk * rows_dev, KV, N_NARROW, PAIR // N_NARROW)
        parts = jnp.einsum("rkjc,kpjc->jrp", chosen, tile_ints, precision=lax.Precision.HIGHEST)
        rounded = lax.optimization_barrier(parts.astype(jnp.bfloat16)).astype(jnp.float32)
        return jnp.sum(rounded, axis=0).astype(jnp.bfloat16)

    stacked = lax.map(one_tile, jnp.arange(q_owner.shape[0], dtype=jnp.int32))
    return jnp.transpose(stacked, (1, 0, 2))
```

```python
import functools

import jax
import jax.numpy as jnp
from jax import lax
from jax.experimental import pallas as pl
from jax.experimental.pallas import tpu as pltpu
from jax.sharding import PartitionSpec as P

PART = 512


def pick_kernel(peers, amp_tiles, cd_tiles, q_owner, amps, *rest):
    outs, held, slots = rest[:peers], rest[peers], rest[peers + 1]
    rows, width, _ = amps.shape
    wants = cd_tiles.shape[1]
    me = lax.axis_index("wide")

    def look(q, carry):
        peer = q_owner[q] ^ me
        for k in range(wants):
            slot = jnp.int32(width)
            for t in range(width):
                slot = jnp.where(amp_tiles[me, t] == cd_tiles[q, k], t, slot)
            slots[peer, k] = slot
        return carry

    lax.fori_loop(0, peers, look, 0)
    for t in range(width):
        held[t] = amps[:, t, :]
    held[width] = jnp.zeros_like(held[width])
    for j in range(peers):
        for k in range(wants):
            outs[j][k] = held[slots[j, k]]


def pick(amplitudes, amp_tiles, cd_tiles, q_owner):
    rows, width, depth = amplitudes.shape
    peers, wants = cd_tiles.shape
    smem = pl.BlockSpec(memory_space=pltpu.SMEM)
    vmem = pl.BlockSpec(memory_space=pltpu.VMEM)
    return pl.pallas_call(
        functools.partial(pick_kernel, peers),
        out_shape=[jax.ShapeDtypeStruct((wants, rows, depth), jnp.bfloat16)] * peers,
        in_specs=[smem, smem, smem, vmem],
        out_specs=[vmem] * peers,
        scratch_shapes=[
            pltpu.VMEM((width + 1, rows, depth), jnp.bfloat16),
            pltpu.SMEM((peers, wants), jnp.int32),
        ],
        compiler_params=pltpu.CompilerParams(vmem_limit_bytes=48 << 20),
        name="pick",
    )(amp_tiles, cd_tiles, q_owner, amplitudes)


def product_kernel(count, flip, *refs):
    picked, ints, out, left = refs[:count], refs[count], refs[count + 1], refs[count + 2]
    rows = picked[0].shape[1]

    @pl.when(pl.program_id(0) == 0)
    def _():
        for i, ref in enumerate(picked):
            for k in range(ref.shape[0]):
                left[k, i * rows : (i + 1) * rows, :] = ref[k]

    total = None
    for k in range(left.shape[0]):
        term = lax.dot_general(
            left[k], ints[0, k], (((1,), (1,)), ((), ())), preferred_element_type=jnp.float32
        )
        total = term if total is None else total + term
    out[...] = total.astype(jnp.bfloat16)


def product(flip, picked, ints, near, shards):
    wants, rows, depth = picked[0].shape
    pairs = ints.shape[2]
    share = pairs // shards
    part = min(PART, share)
    steps = share // part
    count = len(picked)

    def at(i, flip):
        shard = jnp.where(flip[0] == 0, near, shards - 1 - near)
        return (0, 0, shard * steps + i, 0)

    return pl.pallas_call(
        functools.partial(product_kernel, count),
        out_shape=jax.ShapeDtypeStruct((count * rows, share), jnp.bfloat16),
        grid_spec=pltpu.PrefetchScalarGridSpec(
            num_scalar_prefetch=1,
            grid=(steps,),
            in_specs=[pl.BlockSpec((wants, rows, depth), lambda i, flip: (0, 0, 0))] * count
            + [pl.BlockSpec((1, wants, part, depth), at)],
            out_specs=pl.BlockSpec((count * rows, part), lambda i, flip: (0, i)),
            scratch_shapes=[pltpu.VMEM((wants, count * rows, depth), jnp.bfloat16)],
        ),
        compiler_params=pltpu.CompilerParams(vmem_limit_bytes=48 << 20),
        cost_estimate=pl.CostEstimate(
            flops=2 * count * rows * wants * depth * share,
            bytes_accessed=2 * wants * depth * share + 2 * count * rows * (share + wants * depth),
            transcendentals=0,
        ),
        name="product",
    )(flip, *picked, ints)


def add(*terms):
    return sum(t.astype(jnp.float32) for t in terms).astype(jnp.bfloat16)


def line_sum(own, place, devices):
    last = []
    held = {}
    for d in range(devices - 1, 0, -1):
        for i in range(d):
            near = d if i < devices // 2 else devices - 1 - d
            value = own[near] if i == 0 else add(own[near], held[i - 1, d])
            held[i, d] = lax.ppermute(
                value, "narrow", [(i, i + 1), (devices - 1 - i, devices - 2 - i)]
            )
        last.append(held[d - 1, d])
    mine = own[0]
    for e in range(1, devices // 2):
        mine = jnp.where(place == e, own[e], mine)
    return add(mine, *last)


def order_kernel(peers, q_owner, *refs):
    shares, out, held = refs[:peers], refs[peers], refs[peers + 1]
    me = lax.axis_index("wide")

    def tile_of(j):
        def look(q, found):
            return jnp.where(q_owner[q] == me ^ j, q, found)

        return lax.fori_loop(0, peers, look, jnp.int32(0))

    for j in range(peers):
        held[tile_of(j)] = shares[j][...]
    for q in range(peers):
        out[:, q, :] = held[q]


def order(q_owner, shares):
    peers = len(shares)
    rows, share = shares[0].shape
    vmem = pl.BlockSpec(memory_space=pltpu.VMEM)
    return pl.pallas_call(
        functools.partial(order_kernel, peers),
        out_shape=jax.ShapeDtypeStruct((rows, peers, share), jnp.bfloat16),
        in_specs=[pl.BlockSpec(memory_space=pltpu.SMEM)] + [vmem] * peers,
        out_specs=vmem,
        scratch_shapes=[pltpu.VMEM((peers, rows, share), jnp.bfloat16)],
        compiler_params=pltpu.CompilerParams(vmem_limit_bytes=48 << 20),
        name="order",
    )(q_owner, *shares)


def on_device(amplitudes, amp_tiles, integrals, cd_tiles, q_owner):
    peers = lax.axis_size("wide")
    devices = lax.axis_size("narrow")
    rows = amplitudes.shape[0]
    at = lax.axis_index("narrow")
    place = jnp.minimum(at, devices - 1 - at)
    flip = jnp.where(at < devices // 2, 0, 1).astype(jnp.int32).reshape(1)

    def swap(value, j):
        return lax.ppermute(value, "wide", [(w, w ^ j) for w in range(peers)])

    picked = pick(amplitudes, amp_tiles, cd_tiles, q_owner)
    picked = [swap(p, j) if j else p for j, p in enumerate(picked)]
    shares = []
    for first, end in ((0, 2), (2, peers)):
        group = picked[first:end]
        own = [None] * devices
        for near in range(devices - 1, -1, -1):
            own[near] = product(flip, group, integrals, near, devices)
        total = line_sum(own, place, devices)
        for j in range(first, end):
            block = lax.slice_in_dim(total, (j - first) * rows, (j - first + 1) * rows)
            shares.append(swap(block, j) if j else block)
    return order(q_owner, shares)


def solution(mesh):
    placed = (P("wide", None, "narrow"), P(), P("wide", None, None, "narrow"), P(), P())
    return jax.shard_map(
        on_device, mesh=mesh, in_specs=placed, out_specs=P("wide", None, "narrow"), check_vma=False
    )
```

```python
import functools

import jax
import jax.numpy as jnp
from jax import lax
from jax.experimental import pallas as pl
from jax.experimental.pallas import tpu as pltpu
from jax.sharding import PartitionSpec as P

PART = 512
LIMIT = 56 << 20


def pick_kernel(peers, amp_tiles, cd_tiles, q_owner, amps, *rest):
    outs, held, slots = rest[: peers // 2], rest[peers // 2], rest[peers // 2 + 1]
    width = amps.shape[1]
    wants = cd_tiles.shape[0]
    me = lax.axis_index("wide")

    def look(q, carry):
        peer = q_owner[q] ^ me
        for k in range(wants):
            slot = jnp.int32(width)
            for t in range(width):
                slot = jnp.where(amp_tiles[t, me] == cd_tiles[k, q], t, slot)
            slots[peer, k] = slot
        return carry

    lax.fori_loop(0, peers, look, 0)
    for t in range(width):
        held[t] = amps[:, t, :]
    held[width] = jnp.zeros_like(held[width])
    for j in range(peers):
        for k in range(wants):
            outs[j // 2][j % 2, k] = held[slots[j, k]]


def pick(amplitudes, amp_tiles, cd_tiles, q_owner):
    rows, width, depth = amplitudes.shape
    peers, wants = cd_tiles.shape
    smem = pl.BlockSpec(memory_space=pltpu.SMEM)
    vmem = pl.BlockSpec(memory_space=pltpu.VMEM)
    return pl.pallas_call(
        functools.partial(pick_kernel, peers),
        out_shape=[jax.ShapeDtypeStruct((2, wants, rows, depth), jnp.bfloat16)] * (peers // 2),
        in_specs=[smem, smem, smem, vmem],
        out_specs=[vmem] * (peers // 2),
        scratch_shapes=[
            pltpu.VMEM((width + 1, rows, depth), jnp.bfloat16),
            pltpu.SMEM((peers, wants), jnp.int32),
        ],
        compiler_params=pltpu.CompilerParams(vmem_limit_bytes=LIMIT),
        name="pick",
    )(amp_tiles.T, cd_tiles.T, q_owner, amplitudes)


def product_kernel(whole, halves, chunks, rows, steps, shard, *refs):
    refs = list(refs)
    picked = [refs.pop(0) for _ in range(len(halves))]
    ints = refs.pop(0)
    outs = [refs.pop(0) for _ in range(chunks)]
    turned, padded = refs
    wants, depth, lanes = turned.shape

    @pl.when((pl.program_id(0) == 0) & (pl.program_id(1) == 0))
    def _():
        padded[...] = jnp.zeros_like(padded)
        for k in range(wants):
            for i, (ref, half) in enumerate(zip(picked, halves)):
                block = ref[k] if half is None else ref[half, k]
                padded[i * rows : (i + 1) * rows, :] = block
            turned[k] = padded[...].T

    total = None
    for k in range(wants):
        term = jnp.dot(ints[0, k], turned[k], preferred_element_type=jnp.float32)
        total = term if total is None else total + term
    total = total.T.astype(jnp.bfloat16)
    each = len(halves) * rows // chunks
    for c in range(chunks):
        outs[c][0] = total[c * each : (c + 1) * each]


def product(shard, picked, ints, rows, chunks):
    arrays, halves = [p for p, _ in picked], [h for _, h in picked]
    _, wants, pairs, depth = ints.shape
    devices = lax.axis_size("narrow")
    share = pairs // devices
    part = min(PART, share)
    steps = share // part
    count = len(picked)
    lanes = -(-count * rows // 128) * 128
    each = count * rows // chunks
    shares = shard.shape[0]

    def full(array):
        return pl.BlockSpec(array.shape, lambda s, i, shard: (0,) * array.ndim)

    return pl.pallas_call(
        functools.partial(product_kernel, None, halves, chunks, rows, steps),
        out_shape=[jax.ShapeDtypeStruct((shares, each, share), jnp.bfloat16)] * chunks,
        grid_spec=pltpu.PrefetchScalarGridSpec(
            num_scalar_prefetch=1,
            grid=(shares, steps),
            in_specs=[full(a) for a in arrays]
            + [pl.BlockSpec((1, wants, part, depth), lambda s, i, shard: (0, 0, shard[s] * steps + i, 0))],
            out_specs=[pl.BlockSpec((1, each, part), lambda s, i, shard: (s, 0, i))] * chunks,
            scratch_shapes=[
                pltpu.VMEM((wants, depth, lanes), jnp.bfloat16),
                pltpu.VMEM((lanes, depth), jnp.bfloat16),
            ],
        ),
        compiler_params=pltpu.CompilerParams(vmem_limit_bytes=LIMIT),
        cost_estimate=pl.CostEstimate(
            flops=2 * 256 * wants * depth * share * shares,
            bytes_accessed=2 * wants * depth * share * shares,
            transcendentals=0,
        ),
        name="product",
    )(shard, *arrays, ints)


def add(*terms):
    return sum(t.astype(jnp.float32) for t in terms).astype(jnp.bfloat16)


def order_kernel(peers, halves, q_owner, *refs):
    shares, out, held = refs[:peers], refs[peers], refs[peers + 1]
    me = lax.axis_index("wide")

    def tile_of(j):
        def look(q, found):
            return jnp.where(q_owner[q] == me ^ j, q, found)

        return lax.fori_loop(0, peers, look, jnp.int32(0))

    for j in range(peers):
        held[tile_of(j)] = shares[j][...] if halves[j] is None else shares[j][halves[j]]
    for q in range(peers):
        out[:, q, :] = held[q]


def order(q_owner, shares, rows):
    peers = len(shares)
    share = shares[0][0].shape[-1]
    vmem = pl.BlockSpec(memory_space=pltpu.VMEM)
    return pl.pallas_call(
        functools.partial(order_kernel, peers, [h for _, h in shares]),
        out_shape=jax.ShapeDtypeStruct((rows, peers, share), jnp.bfloat16),
        in_specs=[pl.BlockSpec(memory_space=pltpu.SMEM)] + [vmem] * peers,
        out_specs=vmem,
        scratch_shapes=[pltpu.VMEM((peers, rows, share), jnp.bfloat16)],
        compiler_params=pltpu.CompilerParams(vmem_limit_bytes=LIMIT),
        name="order",
    )(q_owner, *[s for s, _ in shares])


def on_device(amplitudes, amp_tiles, integrals, cd_tiles, q_owner):
    peers = lax.axis_size("wide")
    devices = lax.axis_size("narrow")
    rows = amplitudes.shape[0]
    at = lax.axis_index("narrow")

    gray = at ^ (at >> 1)
    code = jnp.arange(devices, dtype=jnp.int32) ^ gray
    shard, shift = code, code >> 1
    for _ in range(devices.bit_length() - 2):
        shard, shift = shard ^ shift, shift >> 1
    odd, even = shard[1::2], shard[0::2]

    def swap(value, j):
        return lax.ppermute(value, "wide", [(w, w ^ j) for w in range(peers)])

    def swap_line(value, mask):
        return lax.ppermute(value, "narrow", [(n, n ^ mask) for n in range(devices)])

    picked = pick(amplitudes, amp_tiles, cd_tiles, q_owner)
    mate = swap(picked[0][1], 1)
    arrived = [None] + [swap(picked[g], 2 * g) for g in range(1, peers // 2)]
    handed = [None] + [swap(arrived[g][1], 1) for g in range(1, peers // 2)]
    first = [(picked[0], 0), (mate, None)]
    rest = [pair for g in range(1, peers // 2) for pair in ((arrived[g], 0), (handed[g], None))]

    def totals(group, chunks):
        away = product(odd, group, integrals, rows, chunks)
        keep = product(even, group, integrals, rows, chunks)
        results = []
        for c in range(chunks):
            terms = {2 * i: [keep[c][i]] for i in range(devices // 2)}
            message, names = away[c], list(range(1, devices, 2))
            step = 0
            while True:
                got = swap_line(message, (2 << step) - 1)
                for i, r in enumerate(names):
                    terms[r ^ (1 << step)].append(got[i])
                step += 1
                if 1 << step == devices:
                    break
                names = [r for r in sorted(terms) if r >> step & 1]
                message = jnp.stack([add(*terms.pop(r)) for r in names])
            results.append(add(*terms[0]).reshape(2, rows, -1))
        return results

    own, = totals(first, 1)
    shares = [(own, 0), (swap(own[1], 1), None)]
    for g, total in enumerate(totals(rest, peers // 2 - 1), 1):
        got = swap(total, 2 * g)
        shares += [(got, 0), (swap(got[1], 1), None)]
    return order(q_owner, shares, rows)


def solution(mesh):
    placed = (P("wide", None, "narrow"), P(), P("wide", None, None, "narrow"), P(), P())
    return jax.shard_map(
        on_device, mesh=mesh, in_specs=placed, out_specs=P("wide", None, "narrow"), check_vma=False
    )
```

```python
import functools

import jax
import jax.numpy as jnp
from jax import lax
from jax.experimental import pallas as pl
from jax.experimental.pallas import tpu as pltpu
from jax.sharding import PartitionSpec as P

PART = 512
PIECE = 256
LIMIT = 48 << 20


def pick_kernel(peers, amp_tiles, cd_tiles, q_owner, amps, *rest):
    own, mate, *outs = rest[: peers // 2 + 1]
    held, slots = rest[peers // 2 + 1 :]
    width = amps.shape[1]
    wants = cd_tiles.shape[0]
    me = lax.axis_index("wide")

    def look(q, carry):
        peer = q_owner[q] ^ me
        for k in range(wants):
            slot = jnp.int32(width)
            for t in range(width):
                slot = jnp.where(amp_tiles[t, me] == cd_tiles[k, q], t, slot)
            slots[peer, k] = slot
        return carry

    lax.fori_loop(0, peers, look, 0)
    for t in range(width):
        held[t] = amps[:, t, :]
    held[width] = jnp.zeros_like(held[width])
    for j in range(peers):
        for k in range(wants):
            into = (own, mate)[j].at[k] if j < 2 else outs[j // 2 - 1].at[j % 2, k]
            into[...] = held[slots[j, k]]


def pick(amplitudes, amp_tiles, cd_tiles, q_owner):
    rows, width, depth = amplitudes.shape
    peers, wants = cd_tiles.shape
    smem = pl.BlockSpec(memory_space=pltpu.SMEM)
    vmem = pl.BlockSpec(memory_space=pltpu.VMEM)
    return pl.pallas_call(
        functools.partial(pick_kernel, peers),
        out_shape=[jax.ShapeDtypeStruct((wants, rows, depth), jnp.bfloat16)] * 2
        + [jax.ShapeDtypeStruct((2, wants, rows, depth), jnp.bfloat16)] * (peers // 2 - 1),
        in_specs=[smem, smem, smem, vmem],
        out_specs=[vmem] * (peers // 2 + 1),
        scratch_shapes=[
            pltpu.VMEM((width + 1, rows, depth), jnp.bfloat16),
            pltpu.SMEM((peers, wants), jnp.int32),
        ],
        compiler_params=pltpu.CompilerParams(vmem_limit_bytes=LIMIT),
        name="pick",
    )(amp_tiles.T, cd_tiles.T, q_owner, amplitudes)


def product_kernel(halves, chunks, rows, order, shard, *refs):
    refs = list(refs)
    picked = [refs.pop(0) for _ in range(len(halves))]
    ints = refs.pop(0)
    outs = [refs.pop(0) for _ in range(chunks)]
    buffer, turned, padded, sems = refs
    shares, wants, share, depth = buffer.shape
    pieces = sems.shape[2]
    piece = share // pieces

    def copy(s, k, p):
        start = pl.multiple_of(shard[order[s]] * share, share) + p * piece
        return pltpu.make_async_copy(
            ints.at[0, k, pl.ds(start, piece), :], buffer.at[s, k, pl.ds(p * piece, piece), :], sems.at[s, k, p]
        )

    for s in range(shares):
        for p in range(pieces):
            for k in range(wants):
                copy(s, k, p).start()

    padded[...] = jnp.zeros_like(padded)
    for k in range(wants):
        for i, (ref, half) in enumerate(zip(picked, halves)):
            padded[i * rows : (i + 1) * rows, :] = ref[k] if half is None else ref[half, k]
        turned[k] = padded[...].T

    each = len(halves) * rows // chunks
    part = min(PART, share)
    for s in range(shares):
        for i in range(share // part):
            at = slice(i * part, (i + 1) * part)
            for p in range(i * part // piece, (i + 1) * part // piece):
                for k in range(wants):
                    copy(s, k, p).wait()
            total = None
            for k in range(wants):
                term = jnp.dot(buffer[s, k, at, :], turned[k], preferred_element_type=jnp.float32)
                total = term if total is None else total + term
            total = total.T.astype(jnp.bfloat16)
            for c in range(chunks):
                outs[c][s, :, at] = total[c * each : (c + 1) * each]


def product(shard, order, picked, ints, rows, chunks):
    arrays, halves = [p for p, _ in picked], [h for _, h in picked]
    _, wants, pairs, depth = ints.shape
    share = pairs // shard.shape[0]
    count = len(picked)
    lanes = -(-count * rows // 128) * 128
    each = count * rows // chunks
    shares = len(order)
    pieces = max(1, share // PIECE)
    vmem = pl.BlockSpec(memory_space=pltpu.VMEM)
    return pl.pallas_call(
        functools.partial(product_kernel, halves, chunks, rows, order),
        out_shape=[jax.ShapeDtypeStruct((shares, each, share), jnp.bfloat16)] * chunks,
        in_specs=[pl.BlockSpec(memory_space=pltpu.SMEM)] + [vmem] * count + [pl.BlockSpec(memory_space=pl.ANY)],
        out_specs=[vmem] * chunks,
        scratch_shapes=[
            pltpu.VMEM((shares, wants, share, depth), jnp.bfloat16),
            pltpu.VMEM((wants, depth, lanes), jnp.bfloat16),
            pltpu.VMEM((lanes, depth), jnp.bfloat16),
            pltpu.SemaphoreType.DMA((shares, wants, pieces)),
        ],
        compiler_params=pltpu.CompilerParams(vmem_limit_bytes=LIMIT),
        cost_estimate=pl.CostEstimate(
            flops=2 * 256 * wants * depth * share * shares,
            bytes_accessed=2 * wants * depth * share * shares,
            transcendentals=0,
        ),
        name="product",
    )(shard, *arrays, ints)


def add(*terms):
    return sum(t.astype(jnp.float32) for t in terms).astype(jnp.bfloat16)


def order_kernel(peers, halves, q_owner, *refs):
    shares, out, held = refs[:peers], refs[peers], refs[peers + 1]
    me = lax.axis_index("wide")

    def tile_of(j):
        def look(q, found):
            return jnp.where(q_owner[q] == me ^ j, q, found)

        return lax.fori_loop(0, peers, look, jnp.int32(0))

    for j in range(peers):
        held[tile_of(j)] = shares[j][...] if halves[j] is None else shares[j][halves[j]]
    for q in range(peers):
        out[:, q, :] = held[q]


def order(q_owner, shares, rows):
    peers = len(shares)
    share = shares[0][0].shape[-1]
    vmem = pl.BlockSpec(memory_space=pltpu.VMEM)
    return pl.pallas_call(
        functools.partial(order_kernel, peers, [h for _, h in shares]),
        out_shape=jax.ShapeDtypeStruct((rows, peers, share), jnp.bfloat16),
        in_specs=[pl.BlockSpec(memory_space=pltpu.SMEM)] + [vmem] * peers,
        out_specs=vmem,
        scratch_shapes=[pltpu.VMEM((peers, rows, share), jnp.bfloat16)],
        compiler_params=pltpu.CompilerParams(vmem_limit_bytes=LIMIT),
        name="order",
    )(q_owner, *[s for s, _ in shares])


def on_device(amplitudes, amp_tiles, integrals, cd_tiles, q_owner):
    peers = lax.axis_size("wide")
    devices = lax.axis_size("narrow")
    rows = amplitudes.shape[0]
    at = lax.axis_index("narrow")

    gray = at ^ (at >> 1)
    code = jnp.arange(devices, dtype=jnp.int32) ^ gray
    shard, shift = code, code >> 1
    for _ in range(devices.bit_length() - 2):
        shard, shift = shard ^ shift, shift >> 1
    odd, even = tuple(range(1, devices, 2)), tuple(range(0, devices, 2))

    def swap(value, j):
        return lax.ppermute(value, "wide", [(w, w ^ j) for w in range(peers)])

    def swap_line(value, mask):
        return lax.ppermute(value, "narrow", [(n, n ^ mask) for n in range(devices)])

    mine, mate, *picked = pick(amplitudes, amp_tiles, cd_tiles, q_owner)
    mate = swap(mate, 1)
    arrived = [None] + [swap(picked[g - 1], 2 * g) for g in range(1, peers // 2)]
    handed = [None] + [swap(arrived[g][1], 1) for g in range(1, peers // 2)]
    first = [(mine, None), (mate, None)]
    rest = [pair for g in range(1, peers // 2) for pair in ((arrived[g], 0), (handed[g], None))]

    def totals(group, chunks):
        away = product(shard, odd, group, integrals, rows, chunks)
        keep = product(shard, even, group, integrals, rows, chunks)
        results = []
        for c in range(chunks):
            terms = {2 * i: [keep[c][i]] for i in range(devices // 2)}
            message, names = away[c], list(range(1, devices, 2))
            step = 0
            while True:
                got = swap_line(message, (2 << step) - 1)
                for i, r in enumerate(names):
                    terms[r ^ (1 << step)].append(got[i])
                step += 1
                if 1 << step == devices:
                    break
                names = [r for r in sorted(terms) if r >> step & 1]
                message = jnp.stack([add(*terms.pop(r)) for r in names])
            results.append(add(*terms[0]).reshape(2, rows, -1))
        return results

    own, = totals(first, 1)
    shares = [(own, 0), (swap(own[1], 1), None)]
    for g, total in enumerate(totals(rest, peers // 2 - 1), 1):
        got = swap(total, 2 * g)
        shares += [(got, 0), (swap(got[1], 1), None)]
    return order(q_owner, shares, rows)


def solution(mesh):
    placed = (P("wide", None, "narrow"), P(), P("wide", None, None, "narrow"), P(), P())
    return jax.shard_map(
        on_device, mesh=mesh, in_specs=placed, out_specs=P("wide", None, "narrow"), check_vma=False
    )
```

```python
import functools

import jax
import jax.numpy as jnp
from jax import lax
from jax.experimental import pallas as pl
from jax.experimental.pallas import tpu as pltpu
from jax.sharding import PartitionSpec as P

PART = 512
PIECE = 256
LIMIT = 48 << 20


def pick_kernel(peers, *refs):
    given, own, mate, *outs = refs[:4], *refs[4 : peers // 2 + 5]
    amp_tiles, cd_tiles, q_owner, amps, held, slots, sems = refs[peers // 2 + 5 :]
    copies = [
        pltpu.make_async_copy(source, target, sems.at[i])
        for i, (source, target) in enumerate(zip(given, (amp_tiles, cd_tiles, q_owner, amps)))
    ]
    for copy in copies:
        copy.start()
    for copy in copies[:3]:
        copy.wait()
    width = amps.shape[1]
    wants = cd_tiles.shape[0]
    me = lax.axis_index("wide")

    def look(q, carry):
        peer = q_owner[q] ^ me
        for k in range(wants):
            slot = jnp.int32(width)
            for t in range(width):
                slot = jnp.where(amp_tiles[t, me] == cd_tiles[k, q], t, slot)
            slots[peer, k] = slot
        return carry

    lax.fori_loop(0, peers, look, 0)
    copies[3].wait()
    for t in range(width):
        held[t] = amps[:, t, :]
    held[width] = jnp.zeros_like(held[width])
    for j in range(peers):
        for k in range(wants):
            into = (own, mate)[j].at[k] if j < 2 else outs[j // 2 - 1].at[j % 2, k]
            into[...] = held[slots[j, k]]


def pick(amplitudes, amp_tiles, cd_tiles, q_owner):
    rows, width, depth = amplitudes.shape
    peers, wants = cd_tiles.shape
    vmem = pl.BlockSpec(memory_space=pltpu.VMEM)
    return pl.pallas_call(
        functools.partial(pick_kernel, peers),
        out_shape=[jax.ShapeDtypeStruct((wants, rows, depth), jnp.bfloat16)] * 2
        + [jax.ShapeDtypeStruct((2, wants, rows, depth), jnp.bfloat16)] * (peers // 2 - 1),
        in_specs=[pl.BlockSpec(memory_space=pltpu.HBM)] * 4,
        out_specs=[vmem] * (peers // 2 + 1),
        scratch_shapes=[
            pltpu.SMEM((width, amp_tiles.shape[0]), jnp.int32),
            pltpu.SMEM((wants, peers), jnp.int32),
            pltpu.SMEM((peers,), jnp.int32),
            pltpu.VMEM(amplitudes.shape, jnp.bfloat16),
            pltpu.VMEM((width + 1, rows, depth), jnp.bfloat16),
            pltpu.SMEM((peers, wants), jnp.int32),
            pltpu.SemaphoreType.DMA((4,)),
        ],
        compiler_params=pltpu.CompilerParams(vmem_limit_bytes=60 << 20),
        name="pick",
    )(amp_tiles.T, cd_tiles.T, q_owner, amplitudes)


def product_kernel(halves, chunks, rows, order, shard, *refs):
    refs = list(refs)
    picked = [refs.pop(0) for _ in range(len(halves))]
    ints = refs.pop(0)
    outs = [refs.pop(0) for _ in range(chunks)]
    buffer, left, sems = refs
    shares, wants, share, depth = buffer.shape
    pieces = sems.shape[2]
    piece = share // pieces

    def copy(s, k, p):
        start = pl.multiple_of(shard[order[s]] * share, share) + p * piece
        return pltpu.make_async_copy(
            ints.at[0, k, pl.ds(start, piece), :], buffer.at[s, k, pl.ds(p * piece, piece), :], sems.at[s, k, p]
        )

    for s in range(shares):
        for p in range(pieces):
            for k in range(wants):
                copy(s, k, p).start()

    for k in range(wants):
        for i, (ref, half) in enumerate(zip(picked, halves)):
            left[k, i * rows : (i + 1) * rows, :] = ref[k] if half is None else ref[half, k]

    each = len(halves) * rows // chunks
    part = min(PART, share)
    for s in range(shares):
        for i in range(share // part):
            at = slice(i * part, (i + 1) * part)
            for p in range(i * part // piece, (i + 1) * part // piece):
                for k in range(wants):
                    copy(s, k, p).wait()
            total = None
            for k in range(wants):
                term = lax.dot_general(
                    left[k], buffer[s, k, at, :], (((1,), (1,)), ((), ())), preferred_element_type=jnp.float32
                )
                total = term if total is None else total + term
            total = total.astype(jnp.bfloat16)
            for c in range(chunks):
                outs[c][s, :, at] = total[c * each : (c + 1) * each]


def product(shard, order, picked, ints, rows, chunks):
    arrays, halves = [p for p, _ in picked], [h for _, h in picked]
    _, wants, pairs, depth = ints.shape
    share = pairs // shard.shape[0]
    count = len(picked)
    each = count * rows // chunks
    shares = len(order)
    pieces = max(1, share // PIECE)
    vmem = pl.BlockSpec(memory_space=pltpu.VMEM)
    return pl.pallas_call(
        functools.partial(product_kernel, halves, chunks, rows, order),
        out_shape=[jax.ShapeDtypeStruct((shares, each, share), jnp.bfloat16)] * chunks,
        in_specs=[pl.BlockSpec(memory_space=pltpu.SMEM)] + [vmem] * count + [pl.BlockSpec(memory_space=pltpu.HBM)],
        out_specs=[vmem] * chunks,
        scratch_shapes=[
            pltpu.VMEM((shares, wants, share, depth), jnp.bfloat16),
            pltpu.VMEM((wants, count * rows, depth), jnp.bfloat16),
            pltpu.SemaphoreType.DMA((shares, wants, pieces)),
        ],
        compiler_params=pltpu.CompilerParams(vmem_limit_bytes=LIMIT),
        cost_estimate=pl.CostEstimate(
            flops=2 * 256 * wants * depth * share * shares,
            bytes_accessed=2 * wants * depth * share * shares,
            transcendentals=0,
        ),
        name="product",
    )(shard, *arrays, ints)


def add(*terms):
    return sum(t.astype(jnp.float32) for t in terms).astype(jnp.bfloat16)


def order_kernel(halves, place, *refs):
    shares, out, held = refs[: len(halves)], refs[-2], refs[-1]
    rows = held.shape[0] // len(halves)
    for j, (share, half) in enumerate(zip(shares, halves)):
        held[j * rows : (j + 1) * rows, :] = share[...] if half is None else share[half]
    out[...] = jnp.dot(place[...], held[...], preferred_element_type=jnp.float32).astype(jnp.bfloat16)


def order(place, shares):
    size, share = place.shape[0], shares[0][0].shape[-1]
    vmem = pl.BlockSpec(memory_space=pltpu.VMEM)
    return pl.pallas_call(
        functools.partial(order_kernel, [h for _, h in shares]),
        out_shape=jax.ShapeDtypeStruct((size, share), jnp.bfloat16),
        in_specs=[vmem] * (1 + len(shares)),
        out_specs=vmem,
        scratch_shapes=[pltpu.VMEM((size, share), jnp.bfloat16)],
        compiler_params=pltpu.CompilerParams(vmem_limit_bytes=LIMIT),
        name="order",
    )(place, *[s for s, _ in shares])


def on_device(amplitudes, amp_tiles, integrals, cd_tiles, q_owner):
    peers = lax.axis_size("wide")
    devices = lax.axis_size("narrow")
    rows = amplitudes.shape[0]
    at = lax.axis_index("narrow")

    gray = at ^ (at >> 1)
    code = jnp.arange(devices, dtype=jnp.int32) ^ gray
    shard, shift = code, code >> 1
    for _ in range(devices.bit_length() - 2):
        shard, shift = shard ^ shift, shift >> 1
    odd, even = tuple(range(1, devices, 2)), tuple(range(0, devices, 2))

    def swap(value, j):
        return lax.ppermute(value, "wide", [(w, w ^ j) for w in range(peers)])

    def swap_line(value, mask):
        return lax.ppermute(value, "narrow", [(n, n ^ mask) for n in range(devices)])

    mine, mate, *picked = pick(amplitudes, amp_tiles, cd_tiles, q_owner)
    mate = swap(mate, 1)
    arrived = [None] + [swap(picked[g - 1], 2 * g) for g in range(1, peers // 2)]
    handed = [None] + [swap(arrived[g][1], 1) for g in range(1, peers // 2)]
    first = [(mine, None), (mate, None)]
    rest = [pair for g in range(1, peers // 2) for pair in ((arrived[g], 0), (handed[g], None))]

    wide = jnp.arange(peers * rows, dtype=jnp.int32)
    source = (q_owner ^ lax.axis_index("wide"))[None, :] * rows + jnp.arange(rows, dtype=jnp.int32)[:, None]
    place = (source.reshape(-1, 1) == wide[None, :]).astype(jnp.bfloat16)

    def totals(group, chunks, beside=None):
        away = product(shard, odd, group, integrals, rows, chunks)
        keep = product(shard, even, group, integrals, rows, chunks)
        if beside is not None:
            keep, beside = lax.optimization_barrier((keep, beside))
        results = []
        for c in range(chunks):
            terms = {2 * i: [keep[c][i]] for i in range(devices // 2)}
            message, names = away[c], list(range(1, devices, 2))
            step = 0
            while True:
                got = swap_line(message, (2 << step) - 1)
                for i, r in enumerate(names):
                    terms[r ^ (1 << step)].append(got[i])
                step += 1
                if 1 << step == devices:
                    break
                names = [r for r in sorted(terms) if r >> step & 1]
                message = jnp.stack([add(*terms.pop(r)) for r in names])
            results.append(add(*terms[0]).reshape(2, rows, -1))
        return results, beside

    (own,), place = totals(first, 1, place)
    shares = [(own, 0), (swap(own[1], 1), None)]
    for g, total in enumerate(totals(rest, peers // 2 - 1)[0], 1):
        got = swap(total, 2 * g)
        shares += [(got, 0), (swap(got[1], 1), None)]
    return order(place, shares).reshape(rows, peers, -1)


def solution(mesh):
    placed = (P("wide", None, "narrow"), P(), P("wide", None, None, "narrow"), P(), P())
    return jax.shard_map(
        on_device, mesh=mesh, in_specs=placed, out_specs=P("wide", None, "narrow"), check_vma=False
    )
```

```python
import functools

import jax
import jax.numpy as jnp
from jax import lax
from jax.experimental import pallas as pl
from jax.experimental.pallas import tpu as pltpu
from jax.sharding import PartitionSpec as P

PART = 512
PIECE = 256
LIMIT = 48 << 20
WHOLE = 60 << 20


def pick_kernel(peers, *refs):
    given, outs = refs[:4], refs[4 : 4 + peers]
    amp_tiles, cd_tiles, q_owner, amps, held, slots, sems = refs[4 + peers :]
    copies = [
        pltpu.make_async_copy(source, target, sems.at[i])
        for i, (source, target) in enumerate(zip(given, (amp_tiles, cd_tiles, q_owner, amps)))
    ]
    for copy in copies:
        copy.start()
    for copy in copies[:3]:
        copy.wait()
    width = amps.shape[1]
    wants = cd_tiles.shape[0]
    me = lax.axis_index("wide")

    def look(q, carry):
        peer = q_owner[q] ^ me
        for k in range(wants):
            slot = jnp.int32(width)
            for t in range(width):
                slot = jnp.where(amp_tiles[t, me] == cd_tiles[k, q], t, slot)
            slots[peer, k] = slot
        return carry

    lax.fori_loop(0, peers, look, 0)
    copies[3].wait()
    for t in range(width):
        held[t] = amps[:, t, :]
    held[width] = jnp.zeros_like(held[width])
    for j in range(peers):
        for k in range(wants):
            outs[j][k] = held[slots[j, k]]


def pick(amplitudes, amp_tiles, cd_tiles, q_owner):
    rows, width, depth = amplitudes.shape
    peers, wants = cd_tiles.shape
    return pl.pallas_call(
        functools.partial(pick_kernel, peers),
        out_shape=[jax.ShapeDtypeStruct((wants, rows, depth), jnp.bfloat16)] * peers,
        in_specs=[pl.BlockSpec(memory_space=pltpu.HBM)] * 4,
        out_specs=[pl.BlockSpec(memory_space=pltpu.VMEM)] * peers,
        scratch_shapes=[
            pltpu.SMEM((width, amp_tiles.shape[0]), jnp.int32),
            pltpu.SMEM((wants, peers), jnp.int32),
            pltpu.SMEM((peers,), jnp.int32),
            pltpu.VMEM(amplitudes.shape, jnp.bfloat16),
            pltpu.VMEM((width + 1, rows, depth), jnp.bfloat16),
            pltpu.SMEM((peers, wants), jnp.int32),
            pltpu.SemaphoreType.DMA((4,)),
        ],
        compiler_params=pltpu.CompilerParams(vmem_limit_bytes=WHOLE),
        name="pick",
    )(amp_tiles.T, cd_tiles.T, q_owner, amplitudes)


def product_kernel(count, chunks, others, order, shard, *refs):
    picked, ints, outs = refs[:count], refs[count], refs[count + 1 + others : count + 1 + others + chunks]
    buffer, left, sems, row_sems = refs[-4:]
    shares, wants, share, depth = buffer.shape
    rows = picked[0].shape[1]
    pieces = sems.shape[2]
    piece = share // pieces

    def copy(s, k, p):
        start = pl.multiple_of(shard[order[s]] * share, share) + p * piece
        return pltpu.make_async_copy(
            ints.at[0, k, pl.ds(start, piece), :], buffer.at[s, k, pl.ds(p * piece, piece), :], sems.at[s, k, p]
        )

    placing = [
        pltpu.make_async_copy(ref.at[k], left.at[k, i * rows : (i + 1) * rows, :], row_sems.at[k, i])
        for k in range(wants)
        for i, ref in enumerate(picked)
    ]
    for row_copy in placing:
        row_copy.start()
    for s in range(shares):
        for p in range(pieces):
            for k in range(wants):
                copy(s, k, p).start()
    for row_copy in placing:
        row_copy.wait()

    each = count * rows // chunks
    part = min(PART, share)
    for s in range(shares):
        for i in range(share // part):
            at = slice(i * part, (i + 1) * part)
            for p in range(i * part // piece, (i + 1) * part // piece):
                for k in range(wants):
                    copy(s, k, p).wait()
            total = None
            for k in range(wants):
                term = lax.dot_general(
                    left[k], buffer[s, k, at, :], (((1,), (1,)), ((), ())), preferred_element_type=jnp.float32
                )
                total = term if total is None else total + term
            total = total.astype(jnp.bfloat16)
            for c in range(chunks):
                outs[c][s, :, at] = total[c * each : (c + 1) * each]


def product(shard, order, picked, ints, chunks, passed, after, limit):
    _, wants, pairs, depth = ints.shape
    rows = picked[0].shape[1]
    share = pairs // shard.shape[0]
    count = len(picked)
    shares = len(order)
    pieces = max(1, share // PIECE)
    vmem, any_space = pl.BlockSpec(memory_space=pltpu.VMEM), pl.BlockSpec(memory_space=pl.ANY)
    outs = pl.pallas_call(
        functools.partial(product_kernel, count, chunks, len(passed) + len(after), order),
        out_shape=[jax.ShapeDtypeStruct((shares, count * rows // chunks, share), jnp.bfloat16)] * chunks
        + [jax.ShapeDtypeStruct(p.shape, p.dtype) for p in passed],
        in_specs=[pl.BlockSpec(memory_space=pltpu.SMEM)] + [any_space] * (count + 1 + len(passed) + len(after)),
        out_specs=[vmem] * chunks + [any_space] * len(passed),
        input_output_aliases={2 + count + i: chunks + i for i in range(len(passed))},
        scratch_shapes=[
            pltpu.VMEM((shares, wants, share, depth), jnp.bfloat16),
            pltpu.VMEM((wants, count * rows, depth), jnp.bfloat16),
            pltpu.SemaphoreType.DMA((shares, wants, pieces)),
            pltpu.SemaphoreType.DMA((wants, count)),
        ],
        compiler_params=pltpu.CompilerParams(vmem_limit_bytes=limit),
        cost_estimate=pl.CostEstimate(
            flops=2 * 256 * wants * depth * share * shares,
            bytes_accessed=2 * wants * depth * share * shares,
            transcendentals=0,
        ),
        name="product",
    )(shard, *picked, ints, *passed, *after)
    return outs[:chunks], outs[chunks:]


def add(*terms):
    return sum(t.astype(jnp.float32) for t in terms).astype(jnp.bfloat16)


def order_kernel(place, *refs):
    shares, out, held = refs[:-2], refs[-2], refs[-1]
    rows = shares[0].shape[0]
    for j, share in enumerate(shares):
        held[j * rows : (j + 1) * rows, :] = share[...]
    out[...] = jnp.dot(place[...], held[...], preferred_element_type=jnp.float32).astype(jnp.bfloat16)


def order(place, shares):
    size, share = place.shape[0], shares[0].shape[-1]
    vmem = pl.BlockSpec(memory_space=pltpu.VMEM)
    return pl.pallas_call(
        order_kernel,
        out_shape=jax.ShapeDtypeStruct((size, share), jnp.bfloat16),
        in_specs=[vmem] * (1 + len(shares)),
        out_specs=vmem,
        scratch_shapes=[pltpu.VMEM((size, share), jnp.bfloat16)],
        compiler_params=pltpu.CompilerParams(vmem_limit_bytes=LIMIT),
        name="order",
    )(place, *shares)


def on_device(amplitudes, amp_tiles, integrals, cd_tiles, q_owner):
    peers = lax.axis_size("wide")
    devices = lax.axis_size("narrow")
    rows = amplitudes.shape[0]
    at = lax.axis_index("narrow")

    gray = at ^ (at >> 1)
    code = jnp.arange(devices, dtype=jnp.int32) ^ gray
    shard, shift = code, code >> 1
    for _ in range(devices.bit_length() - 2):
        shard, shift = shard ^ shift, shift >> 1
    odd, middle, home = tuple(range(1, devices, 2)), tuple(range(2, devices, 2)), (0,)

    def swap(value, j):
        return lax.ppermute(value, "wide", [(w, w ^ j) for w in range(peers)])

    def swap_line(value, mask):
        return lax.ppermute(value, "narrow", [(n, n ^ mask) for n in range(devices)])

    def first_step(message):
        return dict(zip(odd, swap_line(message, 1)))

    def later_steps(kept, got):
        terms = {0: [got[1]]}
        for r, value in zip(middle, kept):
            terms[r] = [value, got[r ^ 1]]
        messages = []
        step = 1
        while 1 << step < devices:
            names = [r for r in sorted(terms) if r >> step & 1]
            messages.append(jnp.stack([add(*terms.pop(r)) for r in names]))
            for r, value in zip(names, swap_line(messages[-1], (2 << step) - 1)):
                terms[r ^ (1 << step)].append(value)
            step += 1
        return messages[0], terms[0]

    chips = peers // 2
    near = [g for g in range(1, chips) if g & (g - 1) == 0]
    far = [g for g in range(1, chips) if g & (g - 1)]

    def of(groups):
        return [j for g in groups for j in (2 * g, 2 * g + 1)]

    def multiply(names, groups, passed=(), after=(), limit=LIMIT):
        chosen = [lot[j] for j in of(groups)]
        outs, passed = product(shard, names, chosen, integrals, len(groups), list(passed), list(after), limit)
        return dict(zip(groups, outs)), passed

    lot = dict(enumerate(pick(amplitudes, amp_tiles, cd_tiles, q_owner)))
    for j in [1] + of(near):
        lot[j] = swap(lot[j], j)
    wide = jnp.arange(peers * rows, dtype=jnp.int32)
    source = (q_owner ^ lax.axis_index("wide"))[None, :] * rows + jnp.arange(rows, dtype=jnp.int32)[:, None]
    place = (source.reshape(-1, 1) == wide[None, :]).astype(jnp.bfloat16)

    got, ready, sums = {}, {}, {}
    away, _ = multiply(odd, [0])
    got[0] = first_step(away[0])
    outs, passed = multiply(odd, near, [lot[j] for j in of(far)], [away[0]])
    lot.update((j, swap(value, j)) for j, value in zip(of(far), passed))
    away.update(outs)
    first, others = near[0], near[1:]
    got[first] = first_step(away[first])
    kept, passed = multiply(middle, [0] + near, [away[g] for g in others])
    got.update((g, first_step(value)) for g, value in zip(others, passed))
    ready[0], sums[0] = later_steps(kept[0], got[0])
    outs, _ = multiply(odd, far, after=[ready[0]])
    away.update(outs)
    got.update((g, first_step(value)) for g, value in outs.items())
    ready[first], sums[first] = later_steps(kept[first], got[first])
    outs, _ = multiply(middle, far, after=[away[far[0]], ready[first]])
    kept.update(outs)
    for g in others + far:
        ready[g], sums[g] = later_steps(kept[g], got[g])
    own, _ = multiply(home, range(chips), after=[ready[g] for g in others] + [kept[far[0]], place])

    shares = {}
    for g in [0] + near + far:
        total = add(own[g][0], *sums[g]).reshape(2, rows, -1)
        for c in range(2):
            j = 2 * g + c
            shares[j] = swap(total[c], j) if j else total[c]
    return order(place, [shares[j] for j in range(peers)]).reshape(rows, peers, -1)


def solution(mesh):
    placed = (P("wide", None, "narrow"), P(), P("wide", None, None, "narrow"), P(), P())
    return jax.shard_map(
        on_device, mesh=mesh, in_specs=placed, out_specs=P("wide", None, "narrow"), check_vma=False
    )
```

```python
import functools

import jax
import jax.numpy as jnp
from jax import lax
from jax.experimental import pallas as pl
from jax.experimental.pallas import tpu as pltpu
from jax.sharding import PartitionSpec as P

PART = 512
AHEAD = 3
LIMIT = 30 << 20
FIRST = 40 << 20
SECOND = 30 << 20


def pick_kernel(peers, wants, tables_from, amps, *refs):
    outs, (tables, held, slots, sem) = refs[:peers], refs[peers:]
    fetch = pltpu.make_async_copy(tables_from, tables, sem)
    fetch.start()
    width = amps.shape[1]
    for t in range(width):
        held[t] = amps[:, t, :]
    held[width] = jnp.zeros_like(held[width])
    fetch.wait()
    me = lax.axis_index("wide")

    def look(q, carry):
        peer = tables[width + wants, q] ^ me
        for k in range(wants):
            slot = jnp.int32(width)
            for t in range(width):
                slot = jnp.where(tables[t, me] == tables[width + k, q], t, slot)
            slots[peer, k] = slot
        return carry

    lax.fori_loop(0, peers, look, 0)
    for j in range(peers):
        for k in range(wants):
            outs[j][k] = held[slots[j, k]]


def pick(amplitudes, amp_tiles, cd_tiles, q_owner):
    rows, width, depth = amplitudes.shape
    peers, wants = cd_tiles.shape
    tables = jnp.concatenate([amp_tiles.T, cd_tiles.T, q_owner[None]], axis=0)
    vmem = pl.BlockSpec(memory_space=pltpu.VMEM)
    return pl.pallas_call(
        functools.partial(pick_kernel, peers, wants),
        out_shape=[jax.ShapeDtypeStruct((wants, rows, depth), jnp.bfloat16)] * peers,
        in_specs=[pl.BlockSpec(memory_space=pl.ANY), vmem],
        out_specs=[vmem] * peers,
        scratch_shapes=[
            pltpu.SMEM(tables.shape, jnp.int32),
            pltpu.VMEM((width + 1, rows, depth), jnp.bfloat16),
            pltpu.SMEM((peers, wants), jnp.int32),
            pltpu.SemaphoreType.DMA,
        ],
        compiler_params=pltpu.CompilerParams(vmem_limit_bytes=LIMIT),
        name="pick",
    )(tables, amplitudes)


def gray_place(r):
    at = lax.axis_index("narrow")
    code = at ^ (at >> 1) ^ r
    shift = code >> 1
    for _ in range(lax.axis_size("narrow").bit_length() - 2):
        code, shift = code ^ shift, shift >> 1
    return code


def product_kernel(plan, *refs):
    refs = list(refs)
    picked = [refs.pop(0) for _ in range(plan["count"])]
    held = refs.pop(0) if plan["held"] else None
    ints = refs.pop(0) if plan["fetch"] else None
    del refs[: plan["others"]]
    outs = [refs.pop(0) for _ in range(plan["chunks"])]
    brought = refs.pop(0) if plan["fetch"] else None
    left, sems = refs[-2:]
    source = held if plan["held"] else brought
    _, wants, share, depth = source.shape
    part = min(PART, share)
    blocks = [(s, i) for s in range(len(plan["fetch"])) for i in range(share // part)]

    def copies(n):
        s, i = blocks[n]
        start = pl.multiple_of(gray_place(plan["fetch"][s]) * share, share) + i * part
        return [
            pltpu.make_async_copy(
                ints.at[0, k, pl.ds(start, part), :], brought.at[s, k, pl.ds(i * part, part), :], sems.at[n, k]
            )
            for k in range(wants)
        ]

    def start(n):
        if n < len(blocks):
            for copy in copies(n):
                copy.start()

    def wait(n):
        for copy in copies(n):
            copy.wait()

    ahead = len(blocks) if plan["held"] else AHEAD
    for n in range(ahead):
        start(n)
    rows = picked[0].shape[1]
    for i, ref in enumerate(picked):
        for k in range(wants):
            left[k, i * rows : (i + 1) * rows, :] = ref[k]

    each = len(picked) * rows // len(outs)
    for o, s in enumerate(plan["use"]):
        for i in range(share // part):
            at = slice(i * part, (i + 1) * part)
            if not plan["held"]:
                n = blocks.index((s, i))
                wait(n)
                start(n + ahead)
            total = None
            for k in range(wants):
                term = lax.dot_general(
                    left[k], source[s, k, at, :], (((1,), (1,)), ((), ())), preferred_element_type=jnp.float32
                )
                total = term if total is None else total + term
            total = total.astype(jnp.bfloat16)
            for c, out in enumerate(outs):
                out[o, :, at] = total[c * each : (c + 1) * each]
    if plan["held"]:
        for n in range(len(blocks)):
            wait(n)


def product(picked, chunks, use, held, ints, fetch, passed, after, limit):
    _, wants, pairs, depth = ints.shape
    rows = picked[0].shape[1]
    share = pairs // lax.axis_size("narrow")
    count, shares = len(picked), len(use)
    plan = dict(
        count=count, chunks=chunks, use=use, held=held is not None, fetch=fetch, others=len(passed) + len(after)
    )
    vmem, any_space = pl.BlockSpec(memory_space=pltpu.VMEM), pl.BlockSpec(memory_space=pl.ANY)
    resident = ([held] if held is not None else []) + ([ints] if fetch else [])
    first_passed = count + len(resident)
    outs = pl.pallas_call(
        functools.partial(product_kernel, plan),
        out_shape=[jax.ShapeDtypeStruct((shares, count * rows // chunks, share), jnp.bfloat16)] * chunks
        + [jax.ShapeDtypeStruct((len(fetch), wants, share, depth), jnp.bfloat16)] * bool(fetch)
        + [jax.ShapeDtypeStruct(p.shape, p.dtype) for p in passed],
        in_specs=[vmem] * (count + (held is not None)) + [any_space] * (bool(fetch) + len(passed) + len(after)),
        out_specs=[vmem] * (chunks + bool(fetch)) + [any_space] * len(passed),
        input_output_aliases={first_passed + i: chunks + bool(fetch) + i for i in range(len(passed))},
        scratch_shapes=[
            pltpu.VMEM((wants, count * rows, depth), jnp.bfloat16),
            pltpu.SemaphoreType.DMA((max(1, len(fetch) * max(1, share // PART)), wants)),
        ],
        compiler_params=pltpu.CompilerParams(vmem_limit_bytes=limit),
        cost_estimate=pl.CostEstimate(
            flops=2 * 256 * wants * depth * share * shares,
            bytes_accessed=2 * wants * depth * share * shares,
            transcendentals=0,
        ),
        name="product",
    )(*picked, *resident, *passed, *after)
    return outs[:chunks], outs[chunks : chunks + bool(fetch)], outs[chunks + bool(fetch) :]


def add(*terms):
    return sum(t.astype(jnp.float32) for t in terms).astype(jnp.bfloat16)


def place_kernel(peers, q_owner, after, place):
    size = place.shape[0]
    me = lax.axis_index("wide")
    row = lax.broadcasted_iota(jnp.int32, (size, size), 0)
    column = lax.broadcasted_iota(jnp.int32, (size, size), 1)
    source = row // peers
    for q in range(peers):
        source += jnp.where(row % peers == q, (q_owner[q] ^ me) * (size // peers), 0)
    place[...] = (source == column).astype(jnp.bfloat16)


def place_of(q_owner, size, after):
    return pl.pallas_call(
        functools.partial(place_kernel, q_owner.shape[0]),
        out_shape=jax.ShapeDtypeStruct((size, size), jnp.bfloat16),
        in_specs=[pl.BlockSpec(memory_space=pltpu.SMEM), pl.BlockSpec(memory_space=pl.ANY)],
        out_specs=pl.BlockSpec(memory_space=pltpu.VMEM),
        compiler_params=pltpu.CompilerParams(vmem_limit_bytes=LIMIT),
        name="place",
    )(q_owner, after)


def order_kernel(place, *refs):
    shares, out, held = refs[:-2], refs[-2], refs[-1]
    rows = shares[0].shape[0]
    for j, share in enumerate(shares):
        held[j * rows : (j + 1) * rows, :] = share[...]
    out[...] = jnp.dot(place[...], held[...], preferred_element_type=jnp.float32).astype(jnp.bfloat16)


def order(place, shares):
    size, share = place.shape[0], shares[0].shape[-1]
    vmem = pl.BlockSpec(memory_space=pltpu.VMEM)
    return pl.pallas_call(
        order_kernel,
        out_shape=jax.ShapeDtypeStruct((size, share), jnp.bfloat16),
        in_specs=[vmem] * (1 + len(shares)),
        out_specs=vmem,
        scratch_shapes=[pltpu.VMEM((size, share), jnp.bfloat16)],
        compiler_params=pltpu.CompilerParams(vmem_limit_bytes=LIMIT),
        name="order",
    )(place, *shares)


def on_device(amplitudes, amp_tiles, integrals, cd_tiles, q_owner):
    peers = lax.axis_size("wide")
    devices = lax.axis_size("narrow")
    rows = amplitudes.shape[0]

    odd, even = tuple(range(1, devices, 2)), tuple(range(0, devices, 2))
    middle = even[1:]

    def swap(value, j):
        return lax.ppermute(value, "wide", [(w, w ^ j) for w in range(peers)])

    def swap_line(value, mask):
        return lax.ppermute(value, "narrow", [(n, n ^ mask) for n in range(devices)])

    def first_step(message):
        return dict(zip(odd, swap_line(message, 1)))

    def later_steps(kept, got):
        terms = {0: [got[1]]}
        for r, value in zip(middle, kept):
            terms[r] = [value, got[r ^ 1]]
        messages = []
        step = 1
        while 1 << step < devices:
            names = [r for r in sorted(terms) if r >> step & 1]
            messages.append(jnp.stack([add(*terms.pop(r)) for r in names]))
            for r, value in zip(names, swap_line(messages[-1], (2 << step) - 1)):
                terms[r ^ (1 << step)].append(value)
            step += 1
        return messages[0], terms[0]

    chips = peers // 2
    near = [g for g in range(1, chips) if g & (g - 1) == 0]
    far = [g for g in range(1, chips) if g & (g - 1)]

    def of(groups):
        return [j for g in groups for j in (2 * g, 2 * g + 1)]

    def multiply(groups, use, held=None, fetch=(), passed=(), after=(), limit=LIMIT):
        chosen = [lot[j] for j in of(groups)]
        outs, brought, passed = product(
            chosen, len(groups), use, held, integrals, fetch, list(passed), list(after), limit
        )
        return dict(zip(groups, outs)), *brought, passed

    lot = dict(enumerate(pick(amplitudes, amp_tiles, cd_tiles, q_owner)))
    for j in [1] + of(near):
        lot[j] = swap(lot[j], j)

    got, ready, sums = {}, {}, {}
    every, rest = tuple(range(len(odd))), tuple(range(1, len(even)))
    away, odd_ints, _ = multiply([0], every, fetch=odd, limit=FIRST)
    got[0] = first_step(away[0])
    outs, even_ints, passed = multiply(
        near, every, odd_ints, even, [lot[j] for j in of(far)], [away[0]], limit=SECOND
    )
    lot.update((j, swap(value, j)) for j, value in zip(of(far), passed))
    away.update(outs)
    first, others = near[0], near[1:]
    got[first] = first_step(away[first])
    kept, passed = multiply([0] + near, rest, even_ints, passed=[away[g] for g in others])
    got.update((g, first_step(value)) for g, value in zip(others, passed))
    ready[0], sums[0] = later_steps(kept[0], got[0])
    outs, _ = multiply(far, every, odd_ints, after=[ready[0]])
    away.update(outs)
    got.update((g, first_step(value)) for g, value in outs.items())
    ready[first], sums[first] = later_steps(kept[first], got[first])
    outs, _ = multiply(far, rest, even_ints, after=[away[far[0]], ready[first]])
    kept.update(outs)
    for g in others + far:
        ready[g], sums[g] = later_steps(kept[g], got[g])
    own, _ = multiply(range(chips), (0,), even_ints, after=[ready[g] for g in others] + [kept[far[0]]])
    place = place_of(q_owner, peers * rows, kept[far[0]])

    shares = {}
    for g in [0] + near + far:
        total = add(own[g][0], *sums[g]).reshape(2, rows, -1)
        for c in range(2):
            j = 2 * g + c
            shares[j] = swap(total[c], j) if j else total[c]
    return order(place, [shares[j] for j in range(peers)]).reshape(rows, peers, -1)


def solution(mesh):
    placed = (P("wide", None, "narrow"), P(), P("wide", None, None, "narrow"), P(), P())
    return jax.shard_map(
        on_device, mesh=mesh, in_specs=placed, out_specs=P("wide", None, "narrow"), check_vma=False
    )
```

```python
import functools

import jax
import jax.numpy as jnp
from jax import lax
from jax.experimental import pallas as pl
from jax.experimental.pallas import tpu as pltpu
from jax.sharding import PartitionSpec as P

PART = 512
AHEAD = 3
LIMIT = 30 << 20
FIRST = 40 << 20


def pick_kernel(peers, wants, tables_from, amps, *refs):
    outs, (tables, held, slots, sem) = refs[:peers], refs[peers:]
    fetch = pltpu.make_async_copy(tables_from, tables, sem)
    fetch.start()
    width = amps.shape[1]
    for t in range(width):
        held[t] = amps[:, t, :]
    held[width] = jnp.zeros_like(held[width])
    fetch.wait()
    me = lax.axis_index("wide")

    def look(q, carry):
        peer = tables[width + wants, q] ^ me
        for k in range(wants):
            slot = jnp.int32(width)
            for t in range(width):
                slot = jnp.where(tables[t, me] == tables[width + k, q], t, slot)
            slots[peer, k] = slot
        return carry

    lax.fori_loop(0, peers, look, 0)
    for j in range(peers):
        for k in range(wants):
            outs[j][k] = held[slots[j, k]]


def pick(amplitudes, amp_tiles, cd_tiles, q_owner):
    rows, width, depth = amplitudes.shape
    peers, wants = cd_tiles.shape
    tables = jnp.concatenate([amp_tiles.T, cd_tiles.T, q_owner[None]], axis=0)
    vmem = pl.BlockSpec(memory_space=pltpu.VMEM)
    return pl.pallas_call(
        functools.partial(pick_kernel, peers, wants),
        out_shape=[jax.ShapeDtypeStruct((wants, rows, depth), jnp.bfloat16)] * peers,
        in_specs=[pl.BlockSpec(memory_space=pl.ANY), vmem],
        out_specs=[vmem] * peers,
        scratch_shapes=[
            pltpu.SMEM(tables.shape, jnp.int32),
            pltpu.VMEM((width + 1, rows, depth), jnp.bfloat16),
            pltpu.SMEM((peers, wants), jnp.int32),
            pltpu.SemaphoreType.DMA,
        ],
        compiler_params=pltpu.CompilerParams(vmem_limit_bytes=LIMIT),
        name="pick",
    )(tables, amplitudes)


def gray_place(r):
    at = lax.axis_index("narrow")
    code = at ^ (at >> 1) ^ r
    shift = code >> 1
    for _ in range(lax.axis_size("narrow").bit_length() - 2):
        code, shift = code ^ shift, shift >> 1
    return code


def product_kernel(plan, *refs):
    refs = list(refs)
    picked = [refs.pop(0) for _ in range(plan["count"])]
    held = refs.pop(0) if plan["held"] else None
    ints = refs.pop(0) if plan["fetch"] else None
    del refs[: plan["others"]]
    outs = [refs.pop(0) for _ in range(plan["chunks"])]
    brought = refs.pop(0) if plan["fetch"] else None
    left, sems = refs[-2:]
    source = held if plan["held"] else brought
    _, wants, share, depth = source.shape
    part = min(PART, share)
    blocks = [(s, i) for s in range(len(plan["fetch"])) for i in range(share // part)]

    def copies(n):
        s, i = blocks[n]
        start = pl.multiple_of(gray_place(plan["fetch"][s]) * share, share) + i * part
        return [
            pltpu.make_async_copy(
                ints.at[0, k, pl.ds(start, part), :], brought.at[s, k, pl.ds(i * part, part), :], sems.at[n, k]
            )
            for k in range(wants)
        ]

    def start(n):
        if n < len(blocks):
            for copy in copies(n):
                copy.start()

    def wait(n):
        for copy in copies(n):
            copy.wait()

    ahead = len(blocks) if plan["held"] else AHEAD
    for n in range(ahead):
        start(n)
    rows = picked[0].shape[1]
    for i, ref in enumerate(picked):
        for k in range(wants):
            left[k, i * rows : (i + 1) * rows, :] = ref[k]

    each = len(picked) * rows // len(outs)

    def block(o, s, i):
        at = slice(i * part, (i + 1) * part)
        total = None
        for k in range(wants):
            term = lax.dot_general(
                left[k], source[s, k, at, :], (((1,), (1,)), ((), ())), preferred_element_type=jnp.float32
            )
            total = term if total is None else total + term
        total = total.astype(jnp.bfloat16)
        for c, out in enumerate(outs):
            out[o, :, at] = total[c * each : (c + 1) * each]

    if plan["held"]:

        @pl.loop(0, len(plan["use"]))
        def _(o):
            for i in range(share // part):
                block(o, plan["use"][0] + o, i)

        for n in range(len(blocks)):
            wait(n)
    else:
        for n, (s, i) in enumerate(blocks):
            wait(n)
            start(n + ahead)
            block(s, s, i)


def product(picked, chunks, use, held, ints, fetch, passed, after, limit):
    _, wants, pairs, depth = ints.shape
    rows = picked[0].shape[1]
    share = pairs // lax.axis_size("narrow")
    count, shares = len(picked), len(use)
    plan = dict(
        count=count, chunks=chunks, use=use, held=held is not None, fetch=fetch, others=len(passed) + len(after)
    )
    vmem, any_space = pl.BlockSpec(memory_space=pltpu.VMEM), pl.BlockSpec(memory_space=pl.ANY)
    resident = ([held] if held is not None else []) + ([ints] if fetch else [])
    first_passed = count + len(resident)
    outs = pl.pallas_call(
        functools.partial(product_kernel, plan),
        out_shape=[jax.ShapeDtypeStruct((shares, count * rows // chunks, share), jnp.bfloat16)] * chunks
        + [jax.ShapeDtypeStruct((len(fetch), wants, share, depth), jnp.bfloat16)] * bool(fetch)
        + [jax.ShapeDtypeStruct(p.shape, p.dtype) for p in passed],
        in_specs=[vmem] * (count + (held is not None)) + [any_space] * (bool(fetch) + len(passed) + len(after)),
        out_specs=[vmem] * (chunks + bool(fetch)) + [any_space] * len(passed),
        input_output_aliases={first_passed + i: chunks + bool(fetch) + i for i in range(len(passed))},
        scratch_shapes=[
            pltpu.VMEM((wants, count * rows, depth), jnp.bfloat16),
            pltpu.SemaphoreType.DMA((max(1, len(fetch) * max(1, share // PART)), wants)),
        ],
        compiler_params=pltpu.CompilerParams(vmem_limit_bytes=limit),
        cost_estimate=pl.CostEstimate(
            flops=2 * 256 * wants * depth * share * shares,
            bytes_accessed=2 * wants * depth * share * shares,
            transcendentals=0,
        ),
        name="product",
    )(*picked, *resident, *passed, *after)
    return outs[:chunks], outs[chunks : chunks + bool(fetch)], outs[chunks + bool(fetch) :]


def total_kernel(places, halves, *refs):
    outs = refs[len(refs) - (2 if halves else 1) :]
    at = 0
    for o, own_places in enumerate(places):
        total = None
        for place in own_places:
            term = refs[at][place].astype(jnp.float32)
            total = term if total is None else total + term
            at += 1
        total = total.astype(jnp.bfloat16)
        if halves:
            rows = outs[0].shape[0]
            outs[0][...], outs[1][...] = total[:rows], total[rows:]
        else:
            outs[0][o] = total


def totals(lists, after, halves=False):
    terms = [term for terms in lists for term in terms]
    _, rows, share = terms[0][0].shape
    vmem, any_space = pl.BlockSpec(memory_space=pltpu.VMEM), pl.BlockSpec(memory_space=pl.ANY)
    shape = [(rows // 2, share)] * 2 if halves else [(len(lists), rows, share)]
    return pl.pallas_call(
        functools.partial(total_kernel, [[place for _, place in terms] for terms in lists], halves),
        out_shape=[jax.ShapeDtypeStruct(one, jnp.bfloat16) for one in shape],
        in_specs=[vmem] * len(terms) + [any_space] * len(after),
        out_specs=[vmem] * len(shape),
        compiler_params=pltpu.CompilerParams(vmem_limit_bytes=LIMIT),
        name="totals",
    )(*[array for array, _ in terms], *after)


def place_kernel(peers, q_owner, after, place):
    size = place.shape[0]
    me = lax.axis_index("wide")
    row = lax.broadcasted_iota(jnp.int32, (size, size), 0)
    column = lax.broadcasted_iota(jnp.int32, (size, size), 1)
    source = row // peers
    for q in range(peers):
        source += jnp.where(row % peers == q, (q_owner[q] ^ me) * (size // peers), 0)
    place[...] = (source == column).astype(jnp.bfloat16)


def place_of(q_owner, size, after):
    return pl.pallas_call(
        functools.partial(place_kernel, q_owner.shape[0]),
        out_shape=jax.ShapeDtypeStruct((size, size), jnp.bfloat16),
        in_specs=[pl.BlockSpec(memory_space=pltpu.SMEM), pl.BlockSpec(memory_space=pl.ANY)],
        out_specs=pl.BlockSpec(memory_space=pltpu.VMEM),
        compiler_params=pltpu.CompilerParams(vmem_limit_bytes=LIMIT),
        name="place",
    )(q_owner, after)


def order_kernel(place, *refs):
    shares, out, held = refs[:-2], refs[-2], refs[-1]
    rows = shares[0].shape[0]
    for j, share in enumerate(shares):
        held[j * rows : (j + 1) * rows, :] = share[...]
    out[...] = jnp.dot(place[...], held[...], preferred_element_type=jnp.float32).astype(jnp.bfloat16)


def order(place, shares):
    size, share = place.shape[0], shares[0].shape[-1]
    vmem = pl.BlockSpec(memory_space=pltpu.VMEM)
    return pl.pallas_call(
        order_kernel,
        out_shape=jax.ShapeDtypeStruct((size, share), jnp.bfloat16),
        in_specs=[vmem] * (1 + len(shares)),
        out_specs=vmem,
        scratch_shapes=[pltpu.VMEM((size, share), jnp.bfloat16)],
        compiler_params=pltpu.CompilerParams(vmem_limit_bytes=LIMIT),
        name="order",
    )(place, *shares)


def on_device(amplitudes, amp_tiles, integrals, cd_tiles, q_owner):
    peers = lax.axis_size("wide")
    devices = lax.axis_size("narrow")
    rows = amplitudes.shape[0]

    odd, even = tuple(range(1, devices, 2)), tuple(range(0, devices, 2))
    middle = even[1:]

    def swap(value, j):
        return lax.ppermute(value, "wide", [(w, w ^ j) for w in range(peers)])

    def swap_line(value, mask):
        return lax.ppermute(value, "narrow", [(n, n ^ mask) for n in range(devices)])

    def first_step(message):
        return swap_line(message, 1)

    def later_steps(kept, come, after=()):
        terms = {0: [(come, 0)]}
        for i, r in enumerate(middle):
            terms[r] = [(kept, i), (come, odd.index(r ^ 1))]
        messages = []
        step = 1
        while 1 << step < devices:
            names = [r for r in sorted(terms) if r >> step & 1]
            messages += totals([terms.pop(r) for r in names], list(after))
            come = swap_line(messages[-1], (2 << step) - 1)
            for i, r in enumerate(names):
                terms[r ^ (1 << step)].append((come, i))
            step += 1
        return messages[0], terms[0]

    chips = peers // 2
    near = [g for g in range(1, chips) if g & (g - 1) == 0]
    far = [g for g in range(1, chips) if g & (g - 1)]

    def of(groups):
        return [j for g in groups for j in (2 * g, 2 * g + 1)]

    def multiply(groups, use, held=None, fetch=(), passed=(), after=(), limit=LIMIT):
        chosen = [lot[j] for j in of(groups)]
        outs, brought, passed = product(
            chosen, len(groups), use, held, integrals, fetch, list(passed), list(after), limit
        )
        return dict(zip(groups, outs)), *brought, passed

    lot = dict(enumerate(pick(amplitudes, amp_tiles, cd_tiles, q_owner)))
    for j in [1] + of(near):
        lot[j] = swap(lot[j], j)

    come, ready, sums = {}, {}, {}
    first, others = near[0], near[1:]
    all_odd, all_middle = tuple(range(len(odd))), tuple(range(len(middle)))
    away, odd_ints, _ = multiply([0], all_odd, fetch=odd, limit=FIRST)
    come[0] = first_step(away[0])
    outs, middle_ints, passed = multiply(
        near, all_odd, odd_ints, middle, [lot[j] for j in of(far)], [away[0]]
    )
    lot.update((j, swap(value, j)) for j, value in zip(of(far), passed))
    away.update(outs)
    come[first] = first_step(away[first])
    kept, passed = multiply([0] + near, all_middle, middle_ints, passed=[away[g] for g in others], after=[come[0]])
    come.update((g, first_step(value)) for g, value in zip(others, passed))
    ready[0], sums[0] = later_steps(kept[0], come[0])
    ready[first], sums[first] = later_steps(kept[first], come[first], [ready[0]])
    outs, home_ints, _ = multiply(far, all_odd, odd_ints, (0,), after=[ready[first]])
    away.update(outs)
    come.update((g, first_step(away[g])) for g in far)
    outs, _ = multiply(far, all_middle, middle_ints, after=[away[far[0]], sums[0][-1][0], sums[first][-1][0]])
    kept.update(outs)
    last = kept[far[0]]
    for g in others:
        ready[g], sums[g] = later_steps(kept[g], come[g], [last])
        last = ready[g]
    own, _ = multiply(range(chips), (0,), home_ints, after=[last])
    place = place_of(q_owner, peers * rows, own[0])

    shares = {}

    def close(g, after):
        halves = totals([[(own[g], 0)] + sums[g]], after, halves=True)
        for j, value in zip((2 * g, 2 * g + 1), halves):
            shares[j] = swap(value, j) if j else value
        return halves[1]

    last = close(first, [close(0, [place])])
    for g in far:
        ready[g], sums[g] = later_steps(kept[g], come[g], [last])
        last = ready[g]
    for g in others:
        last = close(g, [last])
    for g in far:
        last = close(g, [last] + [shares[j] for j in of([0] + near)])
    return order(place, [shares[j] for j in range(peers)]).reshape(rows, peers, -1)


def solution(mesh):
    placed = (P("wide", None, "narrow"), P(), P("wide", None, None, "narrow"), P(), P())
    return jax.shard_map(
        on_device, mesh=mesh, in_specs=placed, out_specs=P("wide", None, "narrow"), check_vma=False
    )
```

```python
import functools

import jax
import jax.numpy as jnp
from jax import lax
from jax.experimental import pallas as pl
from jax.experimental.pallas import tpu as pltpu
from jax.sharding import PartitionSpec as P

PART = 512
AHEAD = 3
COST = 1
LIMIT = 30 << 20
FIRST = 40 << 20


def pick_kernel(peers, wants, tables_from, amps, *refs):
    outs, (tables, held, slots, sem) = refs[:peers], refs[peers:]
    fetch = pltpu.make_async_copy(tables_from, tables, sem)
    fetch.start()
    width = amps.shape[1]
    for t in range(width):
        held[t] = amps[:, t, :]
    held[width] = jnp.zeros_like(held[width])
    fetch.wait()
    me = lax.axis_index("wide")

    def look(q, carry):
        peer = tables[width + wants, q] ^ me
        for k in range(wants):
            slot = jnp.int32(width)
            for t in range(width):
                slot = jnp.where(tables[t, me] == tables[width + k, q], t, slot)
            slots[peer, k] = slot
        return carry

    lax.fori_loop(0, peers, look, 0)
    for j in range(peers):
        for k in range(wants):
            outs[j][k] = held[slots[j, k]]


def pick(amplitudes, amp_tiles, cd_tiles, q_owner):
    rows, width, depth = amplitudes.shape
    peers, wants = cd_tiles.shape
    tables = jnp.concatenate([amp_tiles.T, cd_tiles.T, q_owner[None]], axis=0)
    vmem = pl.BlockSpec(memory_space=pltpu.VMEM)
    return pl.pallas_call(
        functools.partial(pick_kernel, peers, wants),
        out_shape=[jax.ShapeDtypeStruct((wants, rows, depth), jnp.bfloat16)] * peers,
        in_specs=[pl.BlockSpec(memory_space=pl.ANY), vmem],
        out_specs=[vmem] * peers,
        scratch_shapes=[
            pltpu.SMEM(tables.shape, jnp.int32),
            pltpu.VMEM((width + 1, rows, depth), jnp.bfloat16),
            pltpu.SMEM((peers, wants), jnp.int32),
            pltpu.SemaphoreType.DMA,
        ],
        compiler_params=pltpu.CompilerParams(vmem_limit_bytes=LIMIT),
        name="pick",
    )(tables, amplitudes)


def gray_place(r):
    at = lax.axis_index("narrow")
    code = at ^ (at >> 1) ^ r
    shift = code >> 1
    for _ in range(lax.axis_size("narrow").bit_length() - 2):
        code, shift = code ^ shift, shift >> 1
    return code


def product_kernel(plan, *refs):
    refs = list(refs)
    picked = [refs.pop(0) for _ in range(plan["count"])]
    held = refs.pop(0) if plan["held"] else None
    ints = refs.pop(0) if plan["fetch"] else None
    del refs[: plan["others"]]
    outs = [refs.pop(0) for _ in range(plan["chunks"])]
    brought = refs.pop(0) if plan["fetch"] else None
    left, sems = refs[-2:]
    source = held if plan["held"] else brought
    _, wants, share, depth = source.shape
    part = min(PART, share)
    blocks = [(s, i) for s in range(len(plan["fetch"])) for i in range(share // part)]

    def copies(n):
        s, i = blocks[n]
        start = pl.multiple_of(gray_place(plan["fetch"][s]) * share, share) + i * part
        return [
            pltpu.make_async_copy(
                ints.at[0, k, pl.ds(start, part), :], brought.at[s, k, pl.ds(i * part, part), :], sems.at[n, k]
            )
            for k in range(wants)
        ]

    def start(n):
        if n < len(blocks):
            for copy in copies(n):
                copy.start()

    def wait(n):
        for copy in copies(n):
            copy.wait()

    ahead = len(blocks) if plan["held"] else AHEAD
    for n in range(ahead):
        start(n)
    rows = picked[0].shape[1]
    for i, ref in enumerate(picked):
        for k in range(wants):
            left[k, i * rows : (i + 1) * rows, :] = ref[k]

    each = len(picked) * rows // len(outs)

    def block(o, s, i):
        at = slice(i * part, (i + 1) * part)
        total = None
        for k in range(wants):
            term = lax.dot_general(
                left[k], source[s, k, at, :], (((1,), (1,)), ((), ())), preferred_element_type=jnp.float32
            )
            total = term if total is None else total + term
        total = total.astype(jnp.bfloat16)
        for c, out in enumerate(outs):
            out[o, :, at] = total[c * each : (c + 1) * each]

    if plan["held"]:

        @pl.loop(0, len(plan["use"]))
        def _(o):
            for i in range(share // part):
                block(o, plan["use"][0] + o, i)

        for n in range(len(blocks)):
            wait(n)
    else:
        for n, (s, i) in enumerate(blocks):
            wait(n)
            start(n + ahead)
            block(s, s, i)


def product(picked, chunks, use, held, ints, fetch, passed, after, limit):
    _, wants, pairs, depth = ints.shape
    rows = picked[0].shape[1]
    share = pairs // lax.axis_size("narrow")
    count, shares = len(picked), len(use)
    plan = dict(
        count=count, chunks=chunks, use=use, held=held is not None, fetch=fetch, others=len(passed) + len(after)
    )
    vmem, any_space = pl.BlockSpec(memory_space=pltpu.VMEM), pl.BlockSpec(memory_space=pl.ANY)
    resident = ([held] if held is not None else []) + ([ints] if fetch else [])
    first_passed = count + len(resident)
    outs = pl.pallas_call(
        functools.partial(product_kernel, plan),
        out_shape=[jax.ShapeDtypeStruct((shares, count * rows // chunks, share), jnp.bfloat16)] * chunks
        + [jax.ShapeDtypeStruct((len(fetch), wants, share, depth), jnp.bfloat16)] * bool(fetch)
        + [jax.ShapeDtypeStruct(p.shape, p.dtype) for p in passed],
        in_specs=[vmem] * (count + (held is not None)) + [any_space] * (bool(fetch) + len(passed) + len(after)),
        out_specs=[vmem] * (chunks + bool(fetch)) + [any_space] * len(passed),
        input_output_aliases={first_passed + i: chunks + bool(fetch) + i for i in range(len(passed))},
        scratch_shapes=[
            pltpu.VMEM((wants, count * rows, depth), jnp.bfloat16),
            pltpu.SemaphoreType.DMA((max(1, len(fetch) * max(1, share // PART)), wants)),
        ],
        compiler_params=pltpu.CompilerParams(vmem_limit_bytes=limit),
        cost_estimate=pl.CostEstimate(
            flops=2 * 256 * wants * depth * share * shares // COST,
            bytes_accessed=2 * wants * depth * share * shares // COST,
            transcendentals=0,
        ),
        name="product",
    )(*picked, *resident, *passed, *after)
    return outs[:chunks], outs[chunks : chunks + bool(fetch)], outs[chunks + bool(fetch) :]


def total_kernel(places, halves, *refs):
    outs = refs[len(refs) - (2 if halves else 1) :]
    at = 0
    for o, own_places in enumerate(places):
        total = None
        for place in own_places:
            term = refs[at][place].astype(jnp.float32)
            total = term if total is None else total + term
            at += 1
        total = total.astype(jnp.bfloat16)
        if halves:
            rows = outs[0].shape[0]
            outs[0][...], outs[1][...] = total[:rows], total[rows:]
        else:
            outs[0][o] = total


def totals(lists, after, halves=False):
    terms = [term for terms in lists for term in terms]
    _, rows, share = terms[0][0].shape
    vmem, any_space = pl.BlockSpec(memory_space=pltpu.VMEM), pl.BlockSpec(memory_space=pl.ANY)
    shape = [(rows // 2, share)] * 2 if halves else [(len(lists), rows, share)]
    return pl.pallas_call(
        functools.partial(total_kernel, [[place for _, place in terms] for terms in lists], halves),
        out_shape=[jax.ShapeDtypeStruct(one, jnp.bfloat16) for one in shape],
        in_specs=[vmem] * len(terms) + [any_space] * len(after),
        out_specs=[vmem] * len(shape),
        compiler_params=pltpu.CompilerParams(vmem_limit_bytes=LIMIT),
        name="totals",
    )(*[array for array, _ in terms], *after)


def place_kernel(peers, q_owner, after, place):
    size = place.shape[0]
    me = lax.axis_index("wide")
    row = lax.broadcasted_iota(jnp.int32, (size, size), 0)
    column = lax.broadcasted_iota(jnp.int32, (size, size), 1)
    source = row // peers
    for q in range(peers):
        source += jnp.where(row % peers == q, (q_owner[q] ^ me) * (size // peers), 0)
    place[...] = (source == column).astype(jnp.bfloat16)


def place_of(q_owner, size, after):
    return pl.pallas_call(
        functools.partial(place_kernel, q_owner.shape[0]),
        out_shape=jax.ShapeDtypeStruct((size, size), jnp.bfloat16),
        in_specs=[pl.BlockSpec(memory_space=pltpu.SMEM), pl.BlockSpec(memory_space=pl.ANY)],
        out_specs=pl.BlockSpec(memory_space=pltpu.VMEM),
        compiler_params=pltpu.CompilerParams(vmem_limit_bytes=LIMIT),
        name="place",
    )(q_owner, after)


def order_kernel(peers, halves, *refs):
    shares, (place, out, held) = refs[:-3], refs[-3:]
    rows = held.shape[0] // len(peers)
    for j, half, share in zip(peers, halves, shares):
        held[j * rows : (j + 1) * rows, :] = share[...] if half is None else share[half]
    out[...] = jnp.dot(place[...], held[...], preferred_element_type=jnp.float32).astype(jnp.bfloat16)


def order(place, shares):
    size, share = place.shape[0], shares[0][1].shape[-1]
    peers, shares, halves = zip(*shares)
    vmem = pl.BlockSpec(memory_space=pltpu.VMEM)
    return pl.pallas_call(
        functools.partial(order_kernel, peers, halves),
        out_shape=jax.ShapeDtypeStruct((size, share), jnp.bfloat16),
        in_specs=[vmem] * (1 + len(shares)),
        out_specs=vmem,
        scratch_shapes=[pltpu.VMEM((size, share), jnp.bfloat16)],
        compiler_params=pltpu.CompilerParams(vmem_limit_bytes=LIMIT),
        name="order",
    )(*shares, place)


def on_device(amplitudes, amp_tiles, integrals, cd_tiles, q_owner):
    peers = lax.axis_size("wide")
    devices = lax.axis_size("narrow")
    rows = amplitudes.shape[0]

    odd, even = tuple(range(1, devices, 2)), tuple(range(0, devices, 2))
    middle = even[1:]

    def swap(value, j):
        return lax.ppermute(value, "wide", [(w, w ^ j) for w in range(peers)])

    def swap_line(value, mask):
        return lax.ppermute(value, "narrow", [(n, n ^ mask) for n in range(devices)])

    def first_step(message):
        return swap_line(message, 1)

    def later_steps(kept, come, after=()):
        terms = {0: [(come, 0)]}
        for i, r in enumerate(middle):
            terms[r] = [(kept, i), (come, odd.index(r ^ 1))]
        messages = []
        step = 1
        while 1 << step < devices:
            names = [r for r in sorted(terms) if r >> step & 1]
            messages += totals([terms.pop(r) for r in names], list(after))
            come = swap_line(messages[-1], (2 << step) - 1)
            for i, r in enumerate(names):
                terms[r ^ (1 << step)].append((come, i))
            step += 1
        return messages[0], terms[0]

    chips = peers // 2
    near = [g for g in range(1, chips) if g & (g - 1) == 0]
    far = [g for g in range(1, chips) if g & (g - 1)]

    def of(groups):
        return [j for g in groups for j in (2 * g, 2 * g + 1)]

    def multiply(groups, use, held=None, fetch=(), passed=(), after=(), limit=LIMIT):
        chosen = [lot[j] for j in of(groups)]
        outs, brought, passed = product(
            chosen, len(groups), use, held, integrals, fetch, list(passed), list(after), limit
        )
        return dict(zip(groups, outs)), *brought, passed

    lot = dict(enumerate(pick(amplitudes, amp_tiles, cd_tiles, q_owner)))
    for j in [1] + of(near):
        lot[j] = swap(lot[j], j)

    come, ready, sums = {}, {}, {}
    first, others = near[0], near[1:]
    all_odd, all_middle = tuple(range(len(odd))), tuple(range(len(middle)))
    away, odd_ints, _ = multiply([0], all_odd, fetch=odd, limit=FIRST)
    come[0] = first_step(away[0])
    outs, middle_ints, passed = multiply(
        near, all_odd, odd_ints, middle, [lot[j] for j in of(far)], [away[0]]
    )
    lot.update((j, swap(value, j)) for j, value in zip(of(far), passed))
    away.update(outs)
    come.update((g, first_step(away[g])) for g in near)
    kept, _ = multiply([0] + near, all_middle, middle_ints, after=[come[0]])
    ready[first], sums[first] = later_steps(kept[first], come[first])
    outs, home_ints, _ = multiply(far, all_odd, odd_ints, (0,), after=[ready[first]])
    away.update(outs)
    come.update((g, first_step(away[g])) for g in far)
    last = away[far[0]]
    for g in others:
        ready[g], sums[g] = later_steps(kept[g], come[g], [last])
        last = ready[g]
    outs, _ = multiply(far, all_middle, middle_ints, after=[last, sums[first][-1][0]])
    kept.update(outs)
    own, _ = multiply(range(chips), (0,), home_ints, after=[kept[far[0]]])
    place = place_of(q_owner, peers * rows, own[0])

    shares = {}

    def close(g, after):
        terms = [[(own[g], 0)] + sums[g]]
        if g in far:
            whole, = totals(terms, after)
            got = swap(whole.reshape(2, rows, -1), 2 * g)
            shares[2 * g], shares[2 * g + 1] = (got, 0), (swap(got[1], 1), None)
            return whole
        halves = totals(terms, after, halves=True)
        for j, value in zip((2 * g, 2 * g + 1), halves):
            shares[j] = (swap(value, j) if j else value, None)
        return halves[1]

    last = close(first, [place])
    for g in far + [0]:
        ready[g], sums[g] = later_steps(kept[g], come[g], [last])
        last = ready[g]
    for g in others:
        last = close(g, [last])
    for g in far:
        last = close(g, [last] + [shares[j][0] for j in of(near)])
    close(0, [last])
    return order(place, [(j, *shares[j]) for j in of(far + near + [0])]).reshape(rows, peers, -1)


def solution(mesh):
    placed = (P("wide", None, "narrow"), P(), P("wide", None, None, "narrow"), P(), P())
    return jax.shard_map(
        on_device, mesh=mesh, in_specs=placed, out_specs=P("wide", None, "narrow"), check_vma=False
    )
```

```python
import functools

import jax
import jax.numpy as jnp
from jax import lax
from jax.experimental import pallas as pl
from jax.experimental.pallas import tpu as pltpu
from jax.sharding import PartitionSpec as P

PART = 512
AHEAD = 3
COST = 1
LIMIT = 30 << 20
FIRST = 40 << 20


def pick_kernel(peers, wants, tables_from, amps, *refs):
    outs, (tables, held, slots, sem) = refs[:peers], refs[peers:]
    fetch = pltpu.make_async_copy(tables_from, tables, sem)
    fetch.start()
    width = amps.shape[1]
    for t in range(width):
        held[t] = amps[:, t, :]
    held[width] = jnp.zeros_like(held[width])
    fetch.wait()
    me = lax.axis_index("wide")

    def look(q, carry):
        peer = tables[width + wants, q] ^ me
        for k in range(wants):
            slot = jnp.int32(width)
            for t in range(width):
                slot = jnp.where(tables[t, me] == tables[width + k, q], t, slot)
            slots[peer, k] = slot
        return carry

    lax.fori_loop(0, peers, look, 0)
    for j in range(peers):
        for k in range(wants):
            outs[j][k] = held[slots[j, k]]


def pick(amplitudes, amp_tiles, cd_tiles, q_owner):
    rows, width, depth = amplitudes.shape
    peers, wants = cd_tiles.shape
    tables = jnp.concatenate([amp_tiles.T, cd_tiles.T, q_owner[None]], axis=0)
    vmem = pl.BlockSpec(memory_space=pltpu.VMEM)
    return pl.pallas_call(
        functools.partial(pick_kernel, peers, wants),
        out_shape=[jax.ShapeDtypeStruct((wants, rows, depth), jnp.bfloat16)] * peers,
        in_specs=[pl.BlockSpec(memory_space=pl.ANY), vmem],
        out_specs=[vmem] * peers,
        scratch_shapes=[
            pltpu.SMEM(tables.shape, jnp.int32),
            pltpu.VMEM((width + 1, rows, depth), jnp.bfloat16),
            pltpu.SMEM((peers, wants), jnp.int32),
            pltpu.SemaphoreType.DMA,
        ],
        compiler_params=pltpu.CompilerParams(vmem_limit_bytes=LIMIT),
        name="pick",
    )(tables, amplitudes)


def product_kernel(plan, *refs):
    refs = list(refs[plan["after"] :])
    picked = [refs.pop(0) for _ in range(plan["count"])]
    held = refs.pop(0) if plan["held"] else None
    ints = refs.pop(0) if plan["fetch"] else None
    del refs[: plan["passed"]]
    outs = [refs.pop(0) for _ in range(plan["chunks"])]
    brought = refs.pop(0) if plan["fetch"] else None
    left, sems = refs[-2:]
    source = held if plan["held"] else brought
    _, wants, share, depth = source.shape
    part = min(PART, share)
    blocks = [(s, i) for s in range(len(plan["fetch"])) for i in range(share // part)]

    def copies(n):
        s, i = blocks[n]
        start = pl.multiple_of((lax.axis_index("narrow") ^ plan["fetch"][s]) * share, share) + i * part
        return [
            pltpu.make_async_copy(
                ints.at[0, k, pl.ds(start, part), :], brought.at[s, k, pl.ds(i * part, part), :], sems.at[n, k]
            )
            for k in range(wants)
        ]

    def start(n):
        if n < len(blocks):
            for copy in copies(n):
                copy.start()

    def wait(n):
        for copy in copies(n):
            copy.wait()

    ahead = len(blocks) if plan["held"] else AHEAD
    for n in range(ahead):
        start(n)
    rows = picked[0].shape[1]
    for i, ref in enumerate(picked):
        for k in range(wants):
            left[k, i * rows : (i + 1) * rows, :] = ref[k]

    each = len(picked) * rows // len(outs)

    def block(o, s, i):
        at = slice(i * part, (i + 1) * part)
        total = None
        for k in range(wants):
            term = lax.dot_general(
                left[k], source[s, k, at, :], (((1,), (1,)), ((), ())), preferred_element_type=jnp.float32
            )
            total = term if total is None else total + term
        total = total.astype(jnp.bfloat16)
        for c, out in enumerate(outs):
            out[o, :, at] = total[c * each : (c + 1) * each]

    if plan["held"]:

        @pl.loop(0, len(plan["use"]))
        def _(o):
            for i in range(share // part):
                block(o, plan["use"][0] + o, i)

        for n in range(len(blocks)):
            wait(n)
    else:
        for n, (s, i) in enumerate(blocks):
            wait(n)
            start(n + ahead)
            block(s, s, i)


def product(picked, chunks, use, held, ints, fetch, passed, after, limit):
    _, wants, pairs, depth = ints.shape
    rows = picked[0].shape[1]
    share = pairs // lax.axis_size("narrow")
    count, shares = len(picked), len(use)
    plan = dict(
        count=count,
        chunks=chunks,
        use=use,
        held=held is not None,
        fetch=fetch,
        passed=len(passed),
        after=len(after),
    )
    vmem, any_space = pl.BlockSpec(memory_space=pltpu.VMEM), pl.BlockSpec(memory_space=pl.ANY)
    resident = ([held] if held is not None else []) + ([ints] if fetch else [])
    first_passed = len(after) + count + len(resident)
    outs = pl.pallas_call(
        functools.partial(product_kernel, plan),
        out_shape=[jax.ShapeDtypeStruct((shares, count * rows // chunks, share), jnp.bfloat16)] * chunks
        + [jax.ShapeDtypeStruct((len(fetch), wants, share, depth), jnp.bfloat16)] * bool(fetch)
        + [jax.ShapeDtypeStruct(p.shape, p.dtype) for p in passed],
        in_specs=[any_space] * len(after)
        + [vmem] * (count + (held is not None))
        + [any_space] * (bool(fetch) + len(passed)),
        out_specs=[vmem] * (chunks + bool(fetch)) + [any_space] * len(passed),
        input_output_aliases={first_passed + i: chunks + bool(fetch) + i for i in range(len(passed))},
        scratch_shapes=[
            pltpu.VMEM((wants, count * rows, depth), jnp.bfloat16),
            pltpu.SemaphoreType.DMA((max(1, len(fetch) * max(1, share // PART)), wants)),
        ],
        compiler_params=pltpu.CompilerParams(vmem_limit_bytes=limit),
        cost_estimate=pl.CostEstimate(
            flops=2 * 256 * wants * depth * share * shares // COST,
            bytes_accessed=2 * wants * depth * share * shares // COST,
            transcendentals=0,
        ),
        name="product",
    )(*after, *picked, *resident, *passed)
    return outs[:chunks], outs[chunks : chunks + bool(fetch)], outs[chunks + bool(fetch) :]


def total_kernel(places, halves, *refs):
    outs = refs[len(refs) - (2 if halves else 1) :]
    at = 0
    for o, own_places in enumerate(places):
        total = None
        for place in own_places:
            term = refs[at][place].astype(jnp.float32)
            total = term if total is None else total + term
            at += 1
        total = total.astype(jnp.bfloat16)
        if halves:
            rows = outs[0].shape[0]
            outs[0][...], outs[1][...] = total[:rows], total[rows:]
        else:
            outs[0][o] = total


def totals(lists, after, halves=False):
    terms = [term for terms in lists for term in terms]
    _, rows, share = terms[0][0].shape
    vmem, any_space = pl.BlockSpec(memory_space=pltpu.VMEM), pl.BlockSpec(memory_space=pl.ANY)
    shape = [(rows // 2, share)] * 2 if halves else [(len(lists), rows, share)]
    return pl.pallas_call(
        functools.partial(total_kernel, [[place for _, place in terms] for terms in lists], halves),
        out_shape=[jax.ShapeDtypeStruct(one, jnp.bfloat16) for one in shape],
        in_specs=[vmem] * len(terms) + [any_space] * len(after),
        out_specs=[vmem] * len(shape),
        compiler_params=pltpu.CompilerParams(vmem_limit_bytes=LIMIT),
        name="totals",
    )(*[array for array, _ in terms], *after)


def place_kernel(peers, q_owner, after, place):
    size = place.shape[0]
    me = lax.axis_index("wide")
    row = lax.broadcasted_iota(jnp.int32, (size, size), 0)
    column = lax.broadcasted_iota(jnp.int32, (size, size), 1)
    source = row // peers
    for q in range(peers):
        source += jnp.where(row % peers == q, (q_owner[q] ^ me) * (size // peers), 0)
    place[...] = (source == column).astype(jnp.bfloat16)


def place_of(q_owner, size, after):
    return pl.pallas_call(
        functools.partial(place_kernel, q_owner.shape[0]),
        out_shape=jax.ShapeDtypeStruct((size, size), jnp.bfloat16),
        in_specs=[pl.BlockSpec(memory_space=pltpu.SMEM), pl.BlockSpec(memory_space=pl.ANY)],
        out_specs=pl.BlockSpec(memory_space=pltpu.VMEM),
        compiler_params=pltpu.CompilerParams(vmem_limit_bytes=LIMIT),
        name="place",
    )(q_owner, after)


def order_kernel(peers, halves, *refs):
    shares, (place, out, held) = refs[:-3], refs[-3:]
    rows = held.shape[0] // len(peers)
    for j, half, share in zip(peers, halves, shares):
        held[j * rows : (j + 1) * rows, :] = share[...] if half is None else share[half]
    out[...] = jnp.dot(place[...], held[...], preferred_element_type=jnp.float32).astype(jnp.bfloat16)


def order(place, shares):
    size, share = place.shape[0], shares[0][1].shape[-1]
    peers, shares, halves = zip(*shares)
    vmem = pl.BlockSpec(memory_space=pltpu.VMEM)
    return pl.pallas_call(
        functools.partial(order_kernel, peers, halves),
        out_shape=jax.ShapeDtypeStruct((size, share), jnp.bfloat16),
        in_specs=[vmem] * (1 + len(shares)),
        out_specs=vmem,
        scratch_shapes=[pltpu.VMEM((size, share), jnp.bfloat16)],
        compiler_params=pltpu.CompilerParams(vmem_limit_bytes=LIMIT),
        name="order",
    )(*shares, place)


def on_device(amplitudes, amp_tiles, integrals, cd_tiles, q_owner):
    peers = lax.axis_size("wide")
    devices = lax.axis_size("narrow")
    rows = amplitudes.shape[0]

    odd, even = tuple(range(1, devices, 2)), tuple(range(0, devices, 2))
    middle = even[1:]

    def swap(value, j):
        return lax.ppermute(value, "wide", [(w, w ^ j) for w in range(peers)])

    def swap_line(value, mask):
        return lax.ppermute(value, "narrow", [(n, n ^ mask) for n in range(devices)])

    def first_step(message):
        return swap_line(message, 1)

    def later_steps(kept, come, after=()):
        terms = {0: [(come, 0)]}
        for i, r in enumerate(middle):
            terms[r] = [(kept, i), (come, odd.index(r ^ 1))]
        messages = []
        step = 1
        while 1 << step < devices:
            names = [r for r in sorted(terms) if r >> step & 1]
            messages += totals([terms.pop(r) for r in names], list(after))
            come = swap_line(messages[-1], 1 << step)
            for i, r in enumerate(names):
                terms[r ^ (1 << step)].append((come, i))
            step += 1
        return messages[0], terms[0]

    chips = peers // 2
    near = [g for g in range(1, chips) if g & (g - 1) == 0]
    far = [g for g in range(1, chips) if g & (g - 1)]

    def of(groups):
        return [j for g in groups for j in (2 * g, 2 * g + 1)]

    def multiply(groups, use, held=None, fetch=(), passed=(), after=(), limit=LIMIT):
        chosen = [lot[j] for j in of(groups)]
        outs, brought, passed = product(
            chosen, len(groups), use, held, integrals, fetch, list(passed), list(after), limit
        )
        return dict(zip(groups, outs)), *brought, passed

    lot = dict(enumerate(pick(amplitudes, amp_tiles, cd_tiles, q_owner)))
    for j in [1] + of(near):
        lot[j] = swap(lot[j], j)

    come, ready, sums = {}, {}, {}
    first, others = near[0], near[1:]
    all_odd, all_middle = tuple(range(len(odd))), tuple(range(len(middle)))
    away, odd_ints, _ = multiply([0], all_odd, fetch=odd, limit=FIRST)
    come[0] = first_step(away[0])
    outs, middle_ints, passed = multiply(
        near, all_odd, odd_ints, middle, [lot[j] for j in of(far)], [away[0]]
    )
    lot.update((j, swap(value, j)) for j, value in zip(of(far), passed))
    away.update(outs)
    come.update((g, first_step(away[g])) for g in near)
    kept, _ = multiply([0] + near, all_middle, middle_ints, after=[come[0]])
    ready[first], sums[first] = later_steps(kept[first], come[first])
    outs, home_ints, _ = multiply(far, all_odd, odd_ints, (0,), after=[ready[first]])
    away.update(outs)
    come.update((g, first_step(away[g])) for g in far)
    last = away[far[0]]
    for g in others:
        ready[g], sums[g] = later_steps(kept[g], come[g], [last])
        last = ready[g]
    outs, _ = multiply(far, all_middle, middle_ints, after=[last, sums[first][-1][0]])
    kept.update(outs)
    own, _ = multiply(range(chips), (0,), home_ints, after=[kept[far[0]]])
    place = place_of(q_owner, peers * rows, own[0])

    shares = {}

    def close(g, after):
        terms = [[(own[g], 0)] + sums[g]]
        if g in far:
            whole, = totals(terms, after)
            got = swap(whole.reshape(2, rows, -1), 2 * g)
            shares[2 * g], shares[2 * g + 1] = (got, 0), (swap(got[1], 1), None)
            return whole
        halves = totals(terms, after, halves=True)
        for j, value in zip((2 * g, 2 * g + 1), halves):
            shares[j] = (swap(value, j) if j else value, None)
        return halves[1]

    last = close(first, [place])
    for g in far + [0]:
        ready[g], sums[g] = later_steps(kept[g], come[g], [last])
        last = ready[g]
    for g in others:
        last = close(g, [last])
    for g in far:
        last = close(g, [last] + [shares[j][0] for j in of(near)])
    close(0, [last])
    return order(place, [(j, *shares[j]) for j in of(far + near + [0])]).reshape(rows, peers, -1)


def solution(mesh):
    placed = (P("wide", None, "narrow"), P(), P("wide", None, None, "narrow"), P(), P())
    return jax.shard_map(
        on_device, mesh=mesh, in_specs=placed, out_specs=P("wide", None, "narrow"), check_vma=False
    )
```

```python
import functools

import jax
import jax.numpy as jnp
from jax import lax
from jax.experimental import pallas as pl
from jax.experimental.pallas import tpu as pltpu
from jax.sharding import PartitionSpec as P

PART = 512
AHEAD = 3
COST = 1
LIMIT = 30 << 20
FIRST = 40 << 20


def pick_kernel(peers, wants, tables_from, amps, *refs):
    outs, (tables, held, slots, sem) = refs[:peers], refs[peers:]
    fetch = pltpu.make_async_copy(tables_from, tables, sem)
    fetch.start()
    width = amps.shape[1]
    for t in range(width):
        held[t] = amps[:, t, :]
    held[width] = jnp.zeros_like(held[width])
    fetch.wait()
    me = lax.axis_index("wide")

    def look(q, carry):
        peer = tables[width + wants, q] ^ me
        for k in range(wants):
            slot = jnp.int32(width)
            for t in range(width):
                slot = jnp.where(tables[t, me] == tables[width + k, q], t, slot)
            slots[peer, k] = slot
        return carry

    lax.fori_loop(0, peers, look, 0)
    for j in range(peers):
        for k in range(wants):
            outs[j][k] = held[slots[j, k]]


def pick(amplitudes, amp_tiles, cd_tiles, q_owner):
    rows, width, depth = amplitudes.shape
    peers, wants = cd_tiles.shape
    tables = jnp.concatenate([amp_tiles.T, cd_tiles.T, q_owner[None]], axis=0)
    vmem = pl.BlockSpec(memory_space=pltpu.VMEM)
    return pl.pallas_call(
        functools.partial(pick_kernel, peers, wants),
        out_shape=[jax.ShapeDtypeStruct((wants, rows, depth), jnp.bfloat16)] * peers,
        in_specs=[pl.BlockSpec(memory_space=pl.ANY), vmem],
        out_specs=[vmem] * peers,
        scratch_shapes=[
            pltpu.SMEM(tables.shape, jnp.int32),
            pltpu.VMEM((width + 1, rows, depth), jnp.bfloat16),
            pltpu.SMEM((peers, wants), jnp.int32),
            pltpu.SemaphoreType.DMA,
        ],
        compiler_params=pltpu.CompilerParams(vmem_limit_bytes=LIMIT),
        name="pick",
    )(tables, amplitudes)


def product_kernel(plan, *refs):
    refs = list(refs[plan["after"] :])
    picked = [refs.pop(0) for _ in range(plan["count"])]
    held = refs.pop(0) if plan["held"] else None
    ints = refs.pop(0) if plan["fetch"] else None
    del refs[: plan["passed"]]
    outs = [refs.pop(0) for _ in range(plan["chunks"])]
    brought = refs.pop(0) if plan["fetch"] else None
    left, sems = refs[-2:]
    source = held if plan["held"] else brought
    _, wants, share, depth = source.shape
    part = min(PART, share)
    blocks = [(s, i) for s in range(len(plan["fetch"])) for i in range(share // part)]

    def copies(n):
        s, i = blocks[n]
        start = pl.multiple_of((lax.axis_index("narrow") ^ plan["fetch"][s]) * share, share) + i * part
        return [
            pltpu.make_async_copy(
                ints.at[0, k, pl.ds(start, part), :], brought.at[s, k, pl.ds(i * part, part), :], sems.at[n, k]
            )
            for k in range(wants)
        ]

    def start(n):
        if n < len(blocks):
            for copy in copies(n):
                copy.start()

    def wait(n):
        for copy in copies(n):
            copy.wait()

    ahead = len(blocks) if plan["held"] else AHEAD
    for n in range(ahead):
        start(n)
    rows = picked[0].shape[1]
    for i, ref in enumerate(picked):
        for k in range(wants):
            left[k, i * rows : (i + 1) * rows, :] = ref[k]

    each = len(picked) * rows // len(outs)

    def block(o, s, i):
        at = slice(i * part, (i + 1) * part)
        total = None
        for k in range(wants):
            term = lax.dot_general(
                left[k], source[s, k, at, :], (((1,), (1,)), ((), ())), preferred_element_type=jnp.float32
            )
            total = term if total is None else total + term
        total = total.astype(jnp.bfloat16)
        for c, out in enumerate(outs):
            out[o, :, at] = total[c * each : (c + 1) * each]

    if plan["held"]:

        @pl.loop(0, len(plan["use"]))
        def _(o):
            for i in range(share // part):
                block(o, plan["use"][0] + o, i)

        for n in range(len(blocks)):
            wait(n)
    else:
        for n, (s, i) in enumerate(blocks):
            wait(n)
            start(n + ahead)
            block(s, s, i)


def product(picked, chunks, use, held, ints, fetch, passed, after, limit):
    _, wants, pairs, depth = ints.shape
    rows = picked[0].shape[1]
    share = pairs // lax.axis_size("narrow")
    count, shares = len(picked), len(use)
    plan = dict(
        count=count,
        chunks=chunks,
        use=use,
        held=held is not None,
        fetch=fetch,
        passed=len(passed),
        after=len(after),
    )
    vmem, any_space = pl.BlockSpec(memory_space=pltpu.VMEM), pl.BlockSpec(memory_space=pl.ANY)
    resident = ([held] if held is not None else []) + ([ints] if fetch else [])
    first_passed = len(after) + count + len(resident)
    outs = pl.pallas_call(
        functools.partial(product_kernel, plan),
        out_shape=[jax.ShapeDtypeStruct((shares, count * rows // chunks, share), jnp.bfloat16)] * chunks
        + [jax.ShapeDtypeStruct((len(fetch), wants, share, depth), jnp.bfloat16)] * bool(fetch)
        + [jax.ShapeDtypeStruct(p.shape, p.dtype) for p in passed],
        in_specs=[any_space] * len(after)
        + [vmem] * (count + (held is not None))
        + [any_space] * (bool(fetch) + len(passed)),
        out_specs=[vmem] * (chunks + bool(fetch)) + [any_space] * len(passed),
        input_output_aliases={first_passed + i: chunks + bool(fetch) + i for i in range(len(passed))},
        scratch_shapes=[
            pltpu.VMEM((wants, count * rows, depth), jnp.bfloat16),
            pltpu.SemaphoreType.DMA((max(1, len(fetch) * max(1, share // PART)), wants)),
        ],
        compiler_params=pltpu.CompilerParams(vmem_limit_bytes=limit),
        cost_estimate=pl.CostEstimate(
            flops=2 * 256 * wants * depth * share * shares // COST,
            bytes_accessed=2 * wants * depth * share * shares // COST,
            transcendentals=0,
        ),
        name="product",
    )(*after, *picked, *resident, *passed)
    return outs[:chunks], outs[chunks : chunks + bool(fetch)], outs[chunks + bool(fetch) :]


def total_kernel(places, halves, *refs):
    outs = refs[len(refs) - (2 if halves else 1) :]
    at = 0
    for o, own_places in enumerate(places):
        total = None
        for place in own_places:
            term = refs[at][place].astype(jnp.float32)
            total = term if total is None else total + term
            at += 1
        total = total.astype(jnp.bfloat16)
        if halves:
            rows = outs[0].shape[0]
            outs[0][...], outs[1][...] = total[:rows], total[rows:]
        else:
            outs[0][o] = total


def totals(lists, after, halves=False):
    terms = [term for terms in lists for term in terms]
    _, rows, share = terms[0][0].shape
    vmem, any_space = pl.BlockSpec(memory_space=pltpu.VMEM), pl.BlockSpec(memory_space=pl.ANY)
    shape = [(rows // 2, share)] * 2 if halves else [(len(lists), rows, share)]
    return pl.pallas_call(
        functools.partial(total_kernel, [[place for _, place in terms] for terms in lists], halves),
        out_shape=[jax.ShapeDtypeStruct(one, jnp.bfloat16) for one in shape],
        in_specs=[vmem] * len(terms) + [any_space] * len(after),
        out_specs=[vmem] * len(shape),
        compiler_params=pltpu.CompilerParams(vmem_limit_bytes=LIMIT),
        name="totals",
    )(*[array for array, _ in terms], *after)


def place_kernel(peers, q_owner, after, place):
    size = place.shape[0]
    me = lax.axis_index("wide")
    row = lax.broadcasted_iota(jnp.int32, (size, size), 0)
    column = lax.broadcasted_iota(jnp.int32, (size, size), 1)
    source = row // peers
    for q in range(peers):
        source += jnp.where(row % peers == q, (q_owner[q] ^ me) * (size // peers), 0)
    place[...] = (source == column).astype(jnp.bfloat16)


def place_of(q_owner, size, after):
    return pl.pallas_call(
        functools.partial(place_kernel, q_owner.shape[0]),
        out_shape=jax.ShapeDtypeStruct((size, size), jnp.bfloat16),
        in_specs=[pl.BlockSpec(memory_space=pltpu.SMEM), pl.BlockSpec(memory_space=pl.ANY)],
        out_specs=pl.BlockSpec(memory_space=pltpu.VMEM),
        compiler_params=pltpu.CompilerParams(vmem_limit_bytes=LIMIT),
        name="place",
    )(q_owner, after)


def order_kernel(peers, halves, *refs):
    shares, (place, out, held) = refs[:-3], refs[-3:]
    rows = held.shape[0] // len(peers)
    for j, half, share in zip(peers, halves, shares):
        held[j * rows : (j + 1) * rows, :] = share[...] if half is None else share[half]
    out[...] = jnp.dot(place[...], held[...], preferred_element_type=jnp.float32).astype(jnp.bfloat16)


def order(place, shares):
    size, share = place.shape[0], shares[0][1].shape[-1]
    peers, shares, halves = zip(*shares)
    vmem = pl.BlockSpec(memory_space=pltpu.VMEM)
    return pl.pallas_call(
        functools.partial(order_kernel, peers, halves),
        out_shape=jax.ShapeDtypeStruct((size, share), jnp.bfloat16),
        in_specs=[vmem] * (1 + len(shares)),
        out_specs=vmem,
        scratch_shapes=[pltpu.VMEM((size, share), jnp.bfloat16)],
        compiler_params=pltpu.CompilerParams(vmem_limit_bytes=LIMIT),
        name="order",
    )(*shares, place)


def on_device(amplitudes, amp_tiles, integrals, cd_tiles, q_owner):
    peers = lax.axis_size("wide")
    devices = lax.axis_size("narrow")
    rows = amplitudes.shape[0]

    odd, even = tuple(range(1, devices, 2)), tuple(range(0, devices, 2))
    middle = even[1:]

    def swap(value, j):
        return lax.ppermute(value, "wide", [(w, w ^ j) for w in range(peers)])

    def swap_line(value, mask):
        return lax.ppermute(value, "narrow", [(n, n ^ mask) for n in range(devices)])

    def first_step(message):
        return swap_line(message, 1)

    def later_steps(kept, come, after=()):
        terms = {0: [(come, 0)]}
        for i, r in enumerate(middle):
            terms[r] = [(kept, i), (come, odd.index(r ^ 1))]
        messages = []
        step = 1
        while 1 << step < devices:
            names = [r for r in sorted(terms) if r >> step & 1]
            messages += totals([terms.pop(r) for r in names], list(after))
            come = swap_line(messages[-1], 1 << step)
            for i, r in enumerate(names):
                terms[r ^ (1 << step)].append((come, i))
            step += 1
        return messages[0], terms[0]

    chips = peers // 2
    near = [g for g in range(1, chips) if g & (g - 1) == 0]
    far = [g for g in range(1, chips) if g & (g - 1)]

    def of(groups):
        return [j for g in groups for j in (2 * g, 2 * g + 1)]

    def multiply(groups, use, held=None, fetch=(), passed=(), after=(), limit=LIMIT):
        chosen = [lot[j] for j in of(groups)]
        outs, brought, passed = product(
            chosen, len(groups), use, held, integrals, fetch, list(passed), list(after), limit
        )
        return dict(zip(groups, outs)), *brought, passed

    lot = dict(enumerate(pick(amplitudes, amp_tiles, cd_tiles, q_owner)))
    for j in [1] + of(near):
        lot[j] = swap(lot[j], j)

    come, ready, sums = {}, {}, {}
    first, others = near[0], near[1:]
    all_odd, all_middle = tuple(range(len(odd))), tuple(range(len(middle)))
    away, odd_ints, _ = multiply([0], all_odd, fetch=odd, limit=FIRST)
    come[0] = first_step(away[0])
    outs, middle_ints, passed = multiply(
        near, all_odd, odd_ints, middle, [lot[j] for j in of(far)], [away[0]]
    )
    lot.update((j, swap(value, j)) for j, value in zip(of(far), passed))
    away.update(outs)
    come.update((g, first_step(away[g])) for g in near)
    kept, _ = multiply([0] + near, all_middle, middle_ints, after=[come[0]])
    ready[first], sums[first] = later_steps(kept[first], come[first])
    outs, home_ints, _ = multiply(far, all_odd, odd_ints, (0,), after=[ready[first]])
    away.update(outs)
    last = away[far[0]]
    for g in others:
        ready[g], sums[g] = later_steps(kept[g], come[g], [last])
        last = ready[g]
    outs, _ = multiply(far, all_middle, middle_ints, after=[last, sums[first][-1][0]])
    kept.update(outs)
    for g in far:
        sums[g] = [(swap_line(away[g][i : i + 1], r), 0) for i, r in enumerate(odd)]
        sums[g] += [(swap_line(kept[g][i : i + 1], r), 0) for i, r in enumerate(middle)]
    own, _ = multiply(range(chips), (0,), home_ints, after=[kept[far[0]]])
    place = place_of(q_owner, peers * rows, own[0])

    shares = {}

    def close(g, after):
        terms = [[(own[g], 0)] + sums[g]]
        if g in far:
            whole, = totals(terms, after)
            got = swap(whole.reshape(2, rows, -1), 2 * g)
            shares[2 * g], shares[2 * g + 1] = (got, 0), (swap(got[1], 1), None)
            return whole
        halves = totals(terms, after, halves=True)
        for j, value in zip((2 * g, 2 * g + 1), halves):
            shares[j] = (swap(value, j) if j else value, None)
        return halves[1]

    last = close(first, [place])
    ready[0], sums[0] = later_steps(kept[0], come[0], [last])
    last = ready[0]
    for g in others:
        last = close(g, [last])
    for g in far:
        last = close(g, [last] + [shares[j][0] for j in of(near)])
    close(0, [last])
    return order(place, [(j, *shares[j]) for j in of(far + near + [0])]).reshape(rows, peers, -1)


def solution(mesh):
    placed = (P("wide", None, "narrow"), P(), P("wide", None, None, "narrow"), P(), P())
    return jax.shard_map(
        on_device, mesh=mesh, in_specs=placed, out_specs=P("wide", None, "narrow"), check_vma=False
    )
```

```python
import functools

import jax
import jax.numpy as jnp
from jax import lax
from jax.experimental import pallas as pl
from jax.experimental.pallas import tpu as pltpu
from jax.sharding import PartitionSpec as P

PART = 512
AHEAD = 3
COST = 1
LIMIT = 30 << 20
FIRST = 40 << 20


def pick_kernel(peers, wants, tables_from, amps, *refs):
    outs, (tables, held, slots, sem) = refs[:peers], refs[peers:]
    fetch = pltpu.make_async_copy(tables_from, tables, sem)
    fetch.start()
    width = amps.shape[1]
    for t in range(width):
        held[t] = amps[:, t, :]
    held[width] = jnp.zeros_like(held[width])
    fetch.wait()
    me = lax.axis_index("wide")

    def look(q, carry):
        peer = tables[width + wants, q] ^ me
        for k in range(wants):
            slot = jnp.int32(width)
            for t in range(width):
                slot = jnp.where(tables[t, me] == tables[width + k, q], t, slot)
            slots[peer, k] = slot
        return carry

    lax.fori_loop(0, peers, look, 0)
    for j in range(peers):
        for k in range(wants):
            outs[j][k] = held[slots[j, k]]


def pick(amplitudes, amp_tiles, cd_tiles, q_owner):
    rows, width, depth = amplitudes.shape
    peers, wants = cd_tiles.shape
    tables = jnp.concatenate([amp_tiles.T, cd_tiles.T, q_owner[None]], axis=0)
    vmem = pl.BlockSpec(memory_space=pltpu.VMEM)
    return pl.pallas_call(
        functools.partial(pick_kernel, peers, wants),
        out_shape=[jax.ShapeDtypeStruct((wants, rows, depth), jnp.bfloat16)] * peers,
        in_specs=[pl.BlockSpec(memory_space=pl.ANY), vmem],
        out_specs=[vmem] * peers,
        scratch_shapes=[
            pltpu.SMEM(tables.shape, jnp.int32),
            pltpu.VMEM((width + 1, rows, depth), jnp.bfloat16),
            pltpu.SMEM((peers, wants), jnp.int32),
            pltpu.SemaphoreType.DMA,
        ],
        compiler_params=pltpu.CompilerParams(vmem_limit_bytes=LIMIT),
        name="pick",
    )(tables, amplitudes)


def product_kernel(plan, *refs):
    refs = list(refs[plan["after"] :])
    picked = [refs.pop(0) for _ in range(plan["count"])]
    held = refs.pop(0) if plan["held"] else None
    ints = refs.pop(0) if plan["fetch"] else None
    del refs[: plan["passed"]]
    outs = [refs.pop(0) for _ in range(plan["chunks"])]
    brought = refs.pop(0) if plan["fetch"] else None
    left, sems = refs[-2:]
    source = held if plan["held"] else brought
    _, wants, share, depth = source.shape
    part = min(PART, share)
    blocks = [(s, i) for s in range(len(plan["fetch"])) for i in range(share // part)]

    def copies(n):
        s, i = blocks[n]
        start = pl.multiple_of((lax.axis_index("narrow") ^ plan["fetch"][s]) * share, share) + i * part
        return [
            pltpu.make_async_copy(
                ints.at[0, k, pl.ds(start, part), :], brought.at[s, k, pl.ds(i * part, part), :], sems.at[n, k]
            )
            for k in range(wants)
        ]

    def start(n):
        if n < len(blocks):
            for copy in copies(n):
                copy.start()

    def wait(n):
        for copy in copies(n):
            copy.wait()

    ahead = len(blocks) if plan["held"] else AHEAD
    for n in range(ahead):
        start(n)
    rows = picked[0].shape[1]
    for i, ref in enumerate(picked):
        for k in range(wants):
            left[k, i * rows : (i + 1) * rows, :] = ref[k]

    each = len(picked) * rows // len(outs)

    def block(o, s, i):
        at = slice(i * part, (i + 1) * part)
        total = None
        for k in range(wants):
            term = lax.dot_general(
                left[k], source[s, k, at, :], (((1,), (1,)), ((), ())), preferred_element_type=jnp.float32
            )
            total = term if total is None else total + term
        total = total.astype(jnp.bfloat16)
        for c, out in enumerate(outs):
            out[o, :, at] = total[c * each : (c + 1) * each]

    if plan["held"]:

        @pl.loop(0, len(plan["use"]))
        def _(o):
            for i in range(share // part):
                block(o, plan["use"][0] + o, i)

        for n in range(len(blocks)):
            wait(n)
    else:
        for n, (s, i) in enumerate(blocks):
            wait(n)
            start(n + ahead)
            block(s, s, i)


def product(picked, chunks, use, held, ints, fetch, passed, after, limit):
    _, wants, pairs, depth = ints.shape
    rows = picked[0].shape[1]
    share = pairs // lax.axis_size("narrow")
    count, shares = len(picked), len(use)
    plan = dict(
        count=count,
        chunks=chunks,
        use=use,
        held=held is not None,
        fetch=fetch,
        passed=len(passed),
        after=len(after),
    )
    vmem, any_space = pl.BlockSpec(memory_space=pltpu.VMEM), pl.BlockSpec(memory_space=pl.ANY)
    resident = ([held] if held is not None else []) + ([ints] if fetch else [])
    first_passed = len(after) + count + len(resident)
    outs = pl.pallas_call(
        functools.partial(product_kernel, plan),
        out_shape=[jax.ShapeDtypeStruct((shares, count * rows // chunks, share), jnp.bfloat16)] * chunks
        + [jax.ShapeDtypeStruct((len(fetch), wants, share, depth), jnp.bfloat16)] * bool(fetch)
        + [jax.ShapeDtypeStruct(p.shape, p.dtype) for p in passed],
        in_specs=[any_space] * len(after)
        + [vmem] * (count + (held is not None))
        + [any_space] * (bool(fetch) + len(passed)),
        out_specs=[vmem] * (chunks + bool(fetch)) + [any_space] * len(passed),
        input_output_aliases={first_passed + i: chunks + bool(fetch) + i for i in range(len(passed))},
        scratch_shapes=[
            pltpu.VMEM((wants, count * rows, depth), jnp.bfloat16),
            pltpu.SemaphoreType.DMA((max(1, len(fetch) * max(1, share // PART)), wants)),
        ],
        compiler_params=pltpu.CompilerParams(vmem_limit_bytes=limit),
        cost_estimate=pl.CostEstimate(
            flops=2 * 256 * wants * depth * share * shares // COST,
            bytes_accessed=2 * wants * depth * share * shares // COST,
            transcendentals=0,
        ),
        name="product",
    )(*after, *picked, *resident, *passed)
    return outs[:chunks], outs[chunks : chunks + bool(fetch)], outs[chunks + bool(fetch) :]


def total_kernel(places, halves, *refs):
    outs = refs[len(refs) - (2 if halves else 1) :]
    at = 0
    for o, own_places in enumerate(places):
        total = None
        for place in own_places:
            term = refs[at][place].astype(jnp.float32)
            total = term if total is None else total + term
            at += 1
        total = total.astype(jnp.bfloat16)
        if halves:
            rows = outs[0].shape[0]
            outs[0][...], outs[1][...] = total[:rows], total[rows:]
        else:
            outs[0][o] = total


def totals(lists, after, halves=False):
    terms = [term for terms in lists for term in terms]
    _, rows, share = terms[0][0].shape
    vmem, any_space = pl.BlockSpec(memory_space=pltpu.VMEM), pl.BlockSpec(memory_space=pl.ANY)
    shape = [(rows // 2, share)] * 2 if halves else [(len(lists), rows, share)]
    return pl.pallas_call(
        functools.partial(total_kernel, [[place for _, place in terms] for terms in lists], halves),
        out_shape=[jax.ShapeDtypeStruct(one, jnp.bfloat16) for one in shape],
        in_specs=[vmem] * len(terms) + [any_space] * len(after),
        out_specs=[vmem] * len(shape),
        compiler_params=pltpu.CompilerParams(vmem_limit_bytes=LIMIT),
        name="totals",
    )(*[array for array, _ in terms], *after)


def place_kernel(peers, q_owner, after, place):
    size = place.shape[0]
    me = lax.axis_index("wide")
    row = lax.broadcasted_iota(jnp.int32, (size, size), 0)
    column = lax.broadcasted_iota(jnp.int32, (size, size), 1)
    source = row // peers
    for q in range(peers):
        source += jnp.where(row % peers == q, (q_owner[q] ^ me) * (size // peers), 0)
    place[...] = (source == column).astype(jnp.bfloat16)


def place_of(q_owner, size, after):
    return pl.pallas_call(
        functools.partial(place_kernel, q_owner.shape[0]),
        out_shape=jax.ShapeDtypeStruct((size, size), jnp.bfloat16),
        in_specs=[pl.BlockSpec(memory_space=pltpu.SMEM), pl.BlockSpec(memory_space=pl.ANY)],
        out_specs=pl.BlockSpec(memory_space=pltpu.VMEM),
        compiler_params=pltpu.CompilerParams(vmem_limit_bytes=LIMIT),
        name="place",
    )(q_owner, after)


def order_kernel(peers, halves, *refs):
    shares, (place, out, held) = refs[:-3], refs[-3:]
    rows = held.shape[0] // len(peers)
    for j, half, share in zip(peers, halves, shares):
        held[j * rows : (j + 1) * rows, :] = share[...] if half is None else share[half]
    out[...] = jnp.dot(place[...], held[...], preferred_element_type=jnp.float32).astype(jnp.bfloat16)


def order(place, shares):
    size, share = place.shape[0], shares[0][1].shape[-1]
    peers, shares, halves = zip(*shares)
    vmem = pl.BlockSpec(memory_space=pltpu.VMEM)
    return pl.pallas_call(
        functools.partial(order_kernel, peers, halves),
        out_shape=jax.ShapeDtypeStruct((size, share), jnp.bfloat16),
        in_specs=[vmem] * (1 + len(shares)),
        out_specs=vmem,
        scratch_shapes=[pltpu.VMEM((size, share), jnp.bfloat16)],
        compiler_params=pltpu.CompilerParams(vmem_limit_bytes=LIMIT),
        name="order",
    )(*shares, place)


def on_device(amplitudes, amp_tiles, integrals, cd_tiles, q_owner):
    peers = lax.axis_size("wide")
    devices = lax.axis_size("narrow")
    rows = amplitudes.shape[0]

    odd, even = tuple(range(1, devices, 2)), tuple(range(0, devices, 2))
    middle = even[1:]

    def swap(value, j):
        return lax.ppermute(value, "wide", [(w, w ^ j) for w in range(peers)])

    def swap_line(value, mask):
        return lax.ppermute(value, "narrow", [(n, n ^ mask) for n in range(devices)])

    def first_step(message):
        return swap_line(message, 1)

    def later_steps(kept, come, after=()):
        terms = {0: [(come, 0)]}
        for i, r in enumerate(middle):
            terms[r] = [(kept, i), (come, odd.index(r ^ 1))]
        messages = []
        step = 1
        while 1 << step < devices:
            names = [r for r in sorted(terms) if r >> step & 1]
            messages += totals([terms.pop(r) for r in names], list(after))
            come = swap_line(messages[-1], 1 << step)
            for i, r in enumerate(names):
                terms[r ^ (1 << step)].append((come, i))
            step += 1
        return messages[0], terms[0]

    chips = peers // 2
    near = [g for g in range(1, chips) if g & (g - 1) == 0]
    far = [g for g in range(1, chips) if g & (g - 1)]

    def of(groups):
        return [j for g in groups for j in (2 * g, 2 * g + 1)]

    def multiply(groups, use, held=None, fetch=(), passed=(), after=(), limit=LIMIT):
        chosen = [lot[j] for j in of(groups)]
        outs, brought, passed = product(
            chosen, len(groups), use, held, integrals, fetch, list(passed), list(after), limit
        )
        return dict(zip(groups, outs)), *brought, passed

    lot = dict(enumerate(pick(amplitudes, amp_tiles, cd_tiles, q_owner)))
    for j in [1] + of(near):
        lot[j] = swap(lot[j], j)

    come, ready, sums = {}, {}, {}
    first, others = near[0], near[1:]
    all_odd, all_middle = tuple(range(len(odd))), tuple(range(len(middle)))
    away, odd_ints, _ = multiply([0], all_odd, fetch=odd, limit=FIRST)
    come[0] = first_step(away[0])
    outs, middle_ints, passed = multiply(
        near, all_odd, odd_ints, middle, [lot[j] for j in of(far)], [away[0]]
    )
    lot.update((j, swap(value, j)) for j, value in zip(of(far), passed))
    away.update(outs)
    come.update((g, first_step(away[g])) for g in near)
    kept, _ = multiply([0] + near, all_middle, middle_ints, after=[come[0]])
    ready[first], sums[first] = later_steps(kept[first], come[first])
    last = ready[first]
    for g in others:
        ready[g], sums[g] = later_steps(kept[g], come[g], [last])
        last = ready[g]
    outs, home_ints, _ = multiply(far, all_odd, odd_ints, (0,), after=[last])
    away.update(outs)
    outs, _ = multiply(far, all_middle, middle_ints, after=[away[far[0]], sums[first][-1][0]])
    kept.update(outs)
    for g in far:
        sums[g] = [(swap_line(away[g][i : i + 1], r), 0) for i, r in enumerate(odd)]
        sums[g] += [(swap_line(kept[g][i : i + 1], r), 0) for i, r in enumerate(middle)]
    own, _ = multiply(range(chips), (0,), home_ints, after=[kept[far[0]]])
    place = place_of(q_owner, peers * rows, own[0])

    shares = {}

    def close(g, after):
        terms = [[(own[g], 0)] + sums[g]]
        if g in far:
            whole, = totals(terms, after)
            got = swap(whole.reshape(2, rows, -1), 2 * g)
            shares[2 * g], shares[2 * g + 1] = (got, 0), (swap(got[1], 1), None)
            return whole
        halves = totals(terms, after, halves=True)
        for j, value in zip((2 * g, 2 * g + 1), halves):
            shares[j] = (swap(value, j) if j else value, None)
        return halves[1]

    last = close(first, [place])
    ready[0], sums[0] = later_steps(kept[0], come[0], [last])
    last = ready[0]
    for g in others:
        last = close(g, [last])
    for g in far:
        last = close(g, [last] + [shares[j][0] for j in of(near)])
    close(0, [last])
    return order(place, [(j, *shares[j]) for j in of(far + near + [0])]).reshape(rows, peers, -1)


def solution(mesh):
    placed = (P("wide", None, "narrow"), P(), P("wide", None, None, "narrow"), P(), P())
    return jax.shard_map(
        on_device, mesh=mesh, in_specs=placed, out_specs=P("wide", None, "narrow"), check_vma=False
    )
```

```python
import functools

import jax
import jax.numpy as jnp
from jax import lax
from jax.experimental import pallas as pl
from jax.experimental.pallas import tpu as pltpu
from jax.sharding import PartitionSpec as P

PART = 512
AHEAD = 3
COST = 1
LIMIT = 30 << 20
FIRST = 40 << 20


def pick_kernel(peers, wants, tables_from, amps, *refs):
    outs, (tables, held, slots, sem) = refs[:peers], refs[peers:]
    fetch = pltpu.make_async_copy(tables_from, tables, sem)
    fetch.start()
    width = amps.shape[1]
    for t in range(width):
        held[t] = amps[:, t, :]
    held[width] = jnp.zeros_like(held[width])
    fetch.wait()
    me = lax.axis_index("wide")

    def look(q, carry):
        peer = tables[width + wants, q] ^ me
        for k in range(wants):
            slot = jnp.int32(width)
            for t in range(width):
                slot = jnp.where(tables[t, me] == tables[width + k, q], t, slot)
            slots[peer, k] = slot
        return carry

    lax.fori_loop(0, peers, look, 0)
    for j in range(peers):
        for k in range(wants):
            outs[j][k] = held[slots[j, k]]


def pick(amplitudes, amp_tiles, cd_tiles, q_owner):
    rows, width, depth = amplitudes.shape
    peers, wants = cd_tiles.shape
    tables = jnp.concatenate([amp_tiles.T, cd_tiles.T, q_owner[None]], axis=0)
    vmem = pl.BlockSpec(memory_space=pltpu.VMEM)
    return pl.pallas_call(
        functools.partial(pick_kernel, peers, wants),
        out_shape=[jax.ShapeDtypeStruct((wants, rows, depth), jnp.bfloat16)] * peers,
        in_specs=[pl.BlockSpec(memory_space=pl.ANY), vmem],
        out_specs=[vmem] * peers,
        scratch_shapes=[
            pltpu.SMEM(tables.shape, jnp.int32),
            pltpu.VMEM((width + 1, rows, depth), jnp.bfloat16),
            pltpu.SMEM((peers, wants), jnp.int32),
            pltpu.SemaphoreType.DMA,
        ],
        compiler_params=pltpu.CompilerParams(vmem_limit_bytes=LIMIT),
        name="pick",
    )(tables, amplitudes)


def product_kernel(plan, *refs):
    refs = list(refs[plan["after"] :])
    picked = [refs.pop(0) for _ in range(plan["count"])]
    held = refs.pop(0) if plan["held"] else None
    ints = refs.pop(0) if plan["fetch"] else None
    del refs[: plan["passed"]]
    outs = [refs.pop(0) for _ in range(plan["chunks"])]
    brought = refs.pop(0) if plan["fetch"] else None
    left, sems = refs[-2:]
    source = held if plan["held"] else brought
    _, wants, share, depth = source.shape
    part = min(PART, share)
    blocks = [(s, i) for s in range(len(plan["fetch"])) for i in range(share // part)]

    def copies(n):
        s, i = blocks[n]
        start = pl.multiple_of((lax.axis_index("narrow") ^ plan["fetch"][s]) * share, share) + i * part
        return [
            pltpu.make_async_copy(
                ints.at[0, k, pl.ds(start, part), :], brought.at[s, k, pl.ds(i * part, part), :], sems.at[n, k]
            )
            for k in range(wants)
        ]

    def start(n):
        if n < len(blocks):
            for copy in copies(n):
                copy.start()

    def wait(n):
        for copy in copies(n):
            copy.wait()

    ahead = len(blocks) if plan["held"] else AHEAD
    for n in range(ahead):
        start(n)
    rows = picked[0].shape[1]
    for i, ref in enumerate(picked):
        for k in range(wants):
            left[k, i * rows : (i + 1) * rows, :] = ref[k]

    each = len(picked) * rows // len(outs)

    def block(o, s, i):
        at = slice(i * part, (i + 1) * part)
        total = None
        for k in range(wants):
            term = lax.dot_general(
                left[k], source[s, k, at, :], (((1,), (1,)), ((), ())), preferred_element_type=jnp.float32
            )
            total = term if total is None else total + term
        total = total.astype(jnp.bfloat16)
        for c, out in enumerate(outs):
            out[o, :, at] = total[c * each : (c + 1) * each]

    if plan["held"]:

        @pl.loop(0, len(plan["use"]))
        def _(o):
            for i in range(share // part):
                block(o, plan["use"][0] + o, i)

        for n in range(len(blocks)):
            wait(n)
    else:
        for n, (s, i) in enumerate(blocks):
            wait(n)
            start(n + ahead)
            block(s, s, i)


def product(picked, chunks, use, held, ints, fetch, passed, after, limit):
    _, wants, pairs, depth = ints.shape
    rows = picked[0].shape[1]
    share = pairs // lax.axis_size("narrow")
    count, shares = len(picked), len(use)
    plan = dict(
        count=count,
        chunks=chunks,
        use=use,
        held=held is not None,
        fetch=fetch,
        passed=len(passed),
        after=len(after),
    )
    vmem, any_space = pl.BlockSpec(memory_space=pltpu.VMEM), pl.BlockSpec(memory_space=pl.ANY)
    resident = ([held] if held is not None else []) + ([ints] if fetch else [])
    first_passed = len(after) + count + len(resident)
    outs = pl.pallas_call(
        functools.partial(product_kernel, plan),
        out_shape=[jax.ShapeDtypeStruct((shares, count * rows // chunks, share), jnp.bfloat16)] * chunks
        + [jax.ShapeDtypeStruct((len(fetch), wants, share, depth), jnp.bfloat16)] * bool(fetch)
        + [jax.ShapeDtypeStruct(p.shape, p.dtype) for p in passed],
        in_specs=[any_space] * len(after)
        + [vmem] * (count + (held is not None))
        + [any_space] * (bool(fetch) + len(passed)),
        out_specs=[vmem] * (chunks + bool(fetch)) + [any_space] * len(passed),
        input_output_aliases={first_passed + i: chunks + bool(fetch) + i for i in range(len(passed))},
        scratch_shapes=[
            pltpu.VMEM((wants, count * rows, depth), jnp.bfloat16),
            pltpu.SemaphoreType.DMA((max(1, len(fetch) * max(1, share // PART)), wants)),
        ],
        compiler_params=pltpu.CompilerParams(vmem_limit_bytes=limit),
        cost_estimate=pl.CostEstimate(
            flops=2 * 256 * wants * depth * share * shares // COST,
            bytes_accessed=2 * wants * depth * share * shares // COST,
            transcendentals=0,
        ),
        name="product",
    )(*after, *picked, *resident, *passed)
    return outs[:chunks], outs[chunks : chunks + bool(fetch)], outs[chunks + bool(fetch) :]


def total_kernel(places, halves, *refs):
    outs = refs[len(refs) - (2 if halves else 1) :]
    at = 0
    for o, own_places in enumerate(places):
        total = None
        for place in own_places:
            term = refs[at][place].astype(jnp.float32)
            total = term if total is None else total + term
            at += 1
        total = total.astype(jnp.bfloat16)
        if halves:
            rows = outs[0].shape[0]
            outs[0][...], outs[1][...] = total[:rows], total[rows:]
        else:
            outs[0][o] = total


def totals(lists, after, halves=False):
    terms = [term for terms in lists for term in terms]
    _, rows, share = terms[0][0].shape
    vmem, any_space = pl.BlockSpec(memory_space=pltpu.VMEM), pl.BlockSpec(memory_space=pl.ANY)
    shape = [(rows // 2, share)] * 2 if halves else [(len(lists), rows, share)]
    return pl.pallas_call(
        functools.partial(total_kernel, [[place for _, place in terms] for terms in lists], halves),
        out_shape=[jax.ShapeDtypeStruct(one, jnp.bfloat16) for one in shape],
        in_specs=[vmem] * len(terms) + [any_space] * len(after),
        out_specs=[vmem] * len(shape),
        compiler_params=pltpu.CompilerParams(vmem_limit_bytes=LIMIT),
        name="totals",
    )(*[array for array, _ in terms], *after)


def place_kernel(peers, q_owner, after, place):
    size = place.shape[0]
    me = lax.axis_index("wide")
    row = lax.broadcasted_iota(jnp.int32, (size, size), 0)
    column = lax.broadcasted_iota(jnp.int32, (size, size), 1)
    source = row // peers
    for q in range(peers):
        source += jnp.where(row % peers == q, (q_owner[q] ^ me) * (size // peers), 0)
    place[...] = (source == column).astype(jnp.bfloat16)


def place_of(q_owner, size, after):
    return pl.pallas_call(
        functools.partial(place_kernel, q_owner.shape[0]),
        out_shape=jax.ShapeDtypeStruct((size, size), jnp.bfloat16),
        in_specs=[pl.BlockSpec(memory_space=pltpu.SMEM), pl.BlockSpec(memory_space=pl.ANY)],
        out_specs=pl.BlockSpec(memory_space=pltpu.VMEM),
        compiler_params=pltpu.CompilerParams(vmem_limit_bytes=LIMIT),
        name="place",
    )(q_owner, after)


def order_kernel(peers, halves, *refs):
    shares, (place, out, held) = refs[:-3], refs[-3:]
    rows = held.shape[0] // len(peers)
    for j, half, share in zip(peers, halves, shares):
        held[j * rows : (j + 1) * rows, :] = share[...] if half is None else share[half]
    out[...] = jnp.dot(place[...], held[...], preferred_element_type=jnp.float32).astype(jnp.bfloat16)


def order(place, shares):
    size, share = place.shape[0], shares[0][1].shape[-1]
    peers, shares, halves = zip(*shares)
    vmem = pl.BlockSpec(memory_space=pltpu.VMEM)
    return pl.pallas_call(
        functools.partial(order_kernel, peers, halves),
        out_shape=jax.ShapeDtypeStruct((size, share), jnp.bfloat16),
        in_specs=[vmem] * (1 + len(shares)),
        out_specs=vmem,
        scratch_shapes=[pltpu.VMEM((size, share), jnp.bfloat16)],
        compiler_params=pltpu.CompilerParams(vmem_limit_bytes=LIMIT),
        name="order",
    )(*shares, place)


def on_device(amplitudes, amp_tiles, integrals, cd_tiles, q_owner):
    peers = lax.axis_size("wide")
    devices = lax.axis_size("narrow")
    rows = amplitudes.shape[0]

    odd, even = tuple(range(1, devices, 2)), tuple(range(0, devices, 2))
    middle = even[1:]

    def swap(value, j):
        return lax.ppermute(value, "wide", [(w, w ^ j) for w in range(peers)])

    def swap_line(value, mask):
        return lax.ppermute(value, "narrow", [(n, n ^ mask) for n in range(devices)])

    def first_step(message):
        return swap_line(message, 1)

    def later_steps(kept, come, after=()):
        terms = {0: [(come, 0)]}
        for i, r in enumerate(middle):
            terms[r] = [(kept, i), (come, odd.index(r ^ 1))]
        messages = []
        step = 1
        while 1 << step < devices:
            names = [r for r in sorted(terms) if r >> step & 1]
            messages += totals([terms.pop(r) for r in names], list(after))
            come = swap_line(messages[-1], 1 << step)
            for i, r in enumerate(names):
                terms[r ^ (1 << step)].append((come, i))
            step += 1
        return messages[0], terms[0]

    chips = peers // 2
    near = [g for g in range(1, chips) if g & (g - 1) == 0]
    far = [g for g in range(1, chips) if g & (g - 1)]

    def of(groups):
        return [j for g in groups for j in (2 * g, 2 * g + 1)]

    def multiply(groups, use, held=None, fetch=(), passed=(), after=(), limit=LIMIT):
        chosen = [lot[j] for j in of(groups)]
        outs, brought, passed = product(
            chosen, len(groups), use, held, integrals, fetch, list(passed), list(after), limit
        )
        return dict(zip(groups, outs)), *brought, passed

    lot = dict(enumerate(pick(amplitudes, amp_tiles, cd_tiles, q_owner)))
    for j in [1] + of(near):
        lot[j] = swap(lot[j], j)

    come, ready, sums = {}, {}, {}
    first, others = near[0], near[1:]
    all_odd, all_middle = tuple(range(len(odd))), tuple(range(len(middle)))
    away, odd_ints, _ = multiply([0], all_odd, fetch=odd, limit=FIRST)
    come[0] = first_step(away[0])
    outs, middle_ints, passed = multiply(
        near, all_odd, odd_ints, middle, [lot[j] for j in of(far)], [away[0]]
    )
    lot.update((j, swap(value, j)) for j, value in zip(of(far), passed))
    away.update(outs)
    come.update((g, first_step(away[g])) for g in near)
    kept, _ = multiply([0] + near, all_middle, middle_ints, after=[come[0]])
    ready[first], sums[first] = later_steps(kept[first], come[first])
    outs, home_ints, _ = multiply(far, all_odd, odd_ints, (0,), after=[ready[first]])
    away.update(outs)
    come.update((g, first_step(away[g])) for g in far)
    last = away[far[0]]
    for g in others:
        ready[g], sums[g] = later_steps(kept[g], come[g], [last])
        last = ready[g]
    outs, _ = multiply(far, all_middle, middle_ints, after=[last, sums[first][-1][0]])
    kept.update(outs)
    own, _ = multiply(range(chips), (0,), home_ints, after=[kept[far[0]]])
    place = place_of(q_owner, peers * rows, own[0])

    shares = {}

    def close(g, after):
        terms = [[(own[g], 0)] + sums[g]]
        if g:
            whole, = totals(terms, after)
            got = swap(whole.reshape(2, rows, -1), 2 * g)
            shares[2 * g], shares[2 * g + 1] = (got, 0), (swap(got[1], 1), None)
            return whole
        halves = totals(terms, after, halves=True)
        shares[0], shares[1] = (halves[0], None), (swap(halves[1], 1), None)
        return halves[1]

    last = close(first, [place])
    for g in far + [0]:
        ready[g], sums[g] = later_steps(kept[g], come[g], [last])
        last = ready[g]
    for g in others:
        last = close(g, [last])
    for g in far:
        last = close(g, [last])
    close(0, [last])
    return order(place, [(j, *shares[j]) for j in of(far + near + [0])]).reshape(rows, peers, -1)


def solution(mesh):
    placed = (P("wide", None, "narrow"), P(), P("wide", None, None, "narrow"), P(), P())
    return jax.shard_map(
        on_device, mesh=mesh, in_specs=placed, out_specs=P("wide", None, "narrow"), check_vma=False
    )
```

```python
import functools

import jax
import jax.numpy as jnp
from jax import lax
from jax.experimental import pallas as pl
from jax.experimental.pallas import tpu as pltpu
from jax.sharding import PartitionSpec as P

PART = 512
AHEAD = 3
COST = 1
LIMIT = 30 << 20
FIRST = 40 << 20


def pick_kernel(peers, wants, tables_from, amps, *refs):
    outs, (tables, held, slots, sem) = refs[:peers], refs[peers:]
    fetch = pltpu.make_async_copy(tables_from, tables, sem)
    fetch.start()
    width = amps.shape[1]
    for t in range(width):
        held[t] = amps[:, t, :]
    held[width] = jnp.zeros_like(held[width])
    fetch.wait()
    me = lax.axis_index("wide")

    def look(q, carry):
        peer = tables[width + wants, q] ^ me
        for k in range(wants):
            slot = jnp.int32(width)
            for t in range(width):
                slot = jnp.where(tables[t, me] == tables[width + k, q], t, slot)
            slots[peer, k] = slot
        return carry

    lax.fori_loop(0, peers, look, 0)
    for j in range(peers):
        for k in range(wants):
            outs[j][k] = held[slots[j, k]]


def pick(amplitudes, amp_tiles, cd_tiles, q_owner):
    rows, width, depth = amplitudes.shape
    peers, wants = cd_tiles.shape
    tables = jnp.concatenate([amp_tiles.T, cd_tiles.T, q_owner[None]], axis=0)
    vmem = pl.BlockSpec(memory_space=pltpu.VMEM)
    return pl.pallas_call(
        functools.partial(pick_kernel, peers, wants),
        out_shape=[jax.ShapeDtypeStruct((wants, rows, depth), jnp.bfloat16)] * peers,
        in_specs=[pl.BlockSpec(memory_space=pl.ANY), vmem],
        out_specs=[vmem] * peers,
        scratch_shapes=[
            pltpu.SMEM(tables.shape, jnp.int32),
            pltpu.VMEM((width + 1, rows, depth), jnp.bfloat16),
            pltpu.SMEM((peers, wants), jnp.int32),
            pltpu.SemaphoreType.DMA,
        ],
        compiler_params=pltpu.CompilerParams(vmem_limit_bytes=LIMIT),
        name="pick",
    )(tables, amplitudes)


def product_kernel(plan, *refs):
    refs = list(refs[plan["after"] :])
    picked = [refs.pop(0) for _ in range(plan["count"])]
    held = refs.pop(0) if plan["held"] else None
    ints = refs.pop(0) if plan["fetch"] else None
    del refs[: plan["passed"]]
    outs = [refs.pop(0) for _ in range(plan["chunks"])]
    brought = refs.pop(0) if plan["fetch"] else None
    left, sems = refs[-2:]
    source = held if plan["held"] else brought
    _, wants, share, depth = source.shape
    part = min(PART, share)
    blocks = [(s, i) for s in range(len(plan["fetch"])) for i in range(share // part)]

    def copies(n):
        s, i = blocks[n]
        start = pl.multiple_of((lax.axis_index("narrow") ^ plan["fetch"][s]) * share, share) + i * part
        return [
            pltpu.make_async_copy(
                ints.at[0, k, pl.ds(start, part), :], brought.at[s, k, pl.ds(i * part, part), :], sems.at[n, k]
            )
            for k in range(wants)
        ]

    def start(n):
        if n < len(blocks):
            for copy in copies(n):
                copy.start()

    def wait(n):
        for copy in copies(n):
            copy.wait()

    ahead = len(blocks) if plan["held"] else AHEAD
    for n in range(ahead):
        start(n)
    rows = picked[0].shape[1]
    for i, ref in enumerate(picked):
        for k in range(wants):
            left[k, i * rows : (i + 1) * rows, :] = ref[k]

    each = len(picked) * rows // len(outs)

    def block(o, s, i):
        at = slice(i * part, (i + 1) * part)
        total = None
        for k in range(wants):
            term = lax.dot_general(
                left[k], source[s, k, at, :], (((1,), (1,)), ((), ())), preferred_element_type=jnp.float32
            )
            total = term if total is None else total + term
        total = total.astype(jnp.bfloat16)
        for c, out in enumerate(outs):
            out[o, :, at] = total[c * each : (c + 1) * each]

    if plan["held"]:

        @pl.loop(0, len(plan["use"]))
        def _(o):
            for i in range(share // part):
                block(o, plan["use"][0] + o, i)

        for n in range(len(blocks)):
            wait(n)
    else:
        for n, (s, i) in enumerate(blocks):
            wait(n)
            start(n + ahead)
            block(s, s, i)


def product(picked, chunks, use, held, ints, fetch, passed, after, limit):
    _, wants, pairs, depth = ints.shape
    rows = picked[0].shape[1]
    share = pairs // lax.axis_size("narrow")
    count, shares = len(picked), len(use)
    plan = dict(
        count=count,
        chunks=chunks,
        use=use,
        held=held is not None,
        fetch=fetch,
        passed=len(passed),
        after=len(after),
    )
    vmem, any_space = pl.BlockSpec(memory_space=pltpu.VMEM), pl.BlockSpec(memory_space=pl.ANY)
    resident = ([held] if held is not None else []) + ([ints] if fetch else [])
    first_passed = len(after) + count + len(resident)
    outs = pl.pallas_call(
        functools.partial(product_kernel, plan),
        out_shape=[jax.ShapeDtypeStruct((shares, count * rows // chunks, share), jnp.bfloat16)] * chunks
        + [jax.ShapeDtypeStruct((len(fetch), wants, share, depth), jnp.bfloat16)] * bool(fetch)
        + [jax.ShapeDtypeStruct(p.shape, p.dtype) for p in passed],
        in_specs=[any_space] * len(after)
        + [vmem] * (count + (held is not None))
        + [any_space] * (bool(fetch) + len(passed)),
        out_specs=[vmem] * (chunks + bool(fetch)) + [any_space] * len(passed),
        input_output_aliases={first_passed + i: chunks + bool(fetch) + i for i in range(len(passed))},
        scratch_shapes=[
            pltpu.VMEM((wants, count * rows, depth), jnp.bfloat16),
            pltpu.SemaphoreType.DMA((max(1, len(fetch) * max(1, share // PART)), wants)),
        ],
        compiler_params=pltpu.CompilerParams(vmem_limit_bytes=limit),
        cost_estimate=pl.CostEstimate(
            flops=2 * 256 * wants * depth * share * shares // COST,
            bytes_accessed=2 * wants * depth * share * shares // COST,
            transcendentals=0,
        ),
        name="product",
    )(*after, *picked, *resident, *passed)
    return outs[:chunks], outs[chunks : chunks + bool(fetch)], outs[chunks + bool(fetch) :]


def total_kernel(places, halves, *refs):
    outs = refs[len(refs) - (2 if halves else 1) :]
    at = 0
    for o, own_places in enumerate(places):
        total = None
        for place in own_places:
            term = refs[at][place].astype(jnp.float32)
            total = term if total is None else total + term
            at += 1
        total = total.astype(jnp.bfloat16)
        if halves:
            rows = outs[0].shape[0]
            outs[0][...], outs[1][...] = total[:rows], total[rows:]
        else:
            outs[0][o] = total


def totals(lists, after, halves=False):
    terms = [term for terms in lists for term in terms]
    _, rows, share = terms[0][0].shape
    vmem, any_space = pl.BlockSpec(memory_space=pltpu.VMEM), pl.BlockSpec(memory_space=pl.ANY)
    shape = [(rows // 2, share)] * 2 if halves else [(len(lists), rows, share)]
    return pl.pallas_call(
        functools.partial(total_kernel, [[place for _, place in terms] for terms in lists], halves),
        out_shape=[jax.ShapeDtypeStruct(one, jnp.bfloat16) for one in shape],
        in_specs=[vmem] * len(terms) + [any_space] * len(after),
        out_specs=[vmem] * len(shape),
        compiler_params=pltpu.CompilerParams(vmem_limit_bytes=LIMIT),
        name="totals",
    )(*[array for array, _ in terms], *after)


def place_kernel(peers, q_owner, after, place):
    size = place.shape[0]
    me = lax.axis_index("wide")
    row = lax.broadcasted_iota(jnp.int32, (size, size), 0)
    column = lax.broadcasted_iota(jnp.int32, (size, size), 1)
    source = row // peers
    for q in range(peers):
        source += jnp.where(row % peers == q, (q_owner[q] ^ me) * (size // peers), 0)
    place[...] = (source == column).astype(jnp.bfloat16)


def place_of(q_owner, size, after):
    return pl.pallas_call(
        functools.partial(place_kernel, q_owner.shape[0]),
        out_shape=jax.ShapeDtypeStruct((size, size), jnp.bfloat16),
        in_specs=[pl.BlockSpec(memory_space=pltpu.SMEM), pl.BlockSpec(memory_space=pl.ANY)],
        out_specs=pl.BlockSpec(memory_space=pltpu.VMEM),
        compiler_params=pltpu.CompilerParams(vmem_limit_bytes=LIMIT),
        name="place",
    )(q_owner, after)


def order_kernel(peers, halves, *refs):
    shares, (place, out, held) = refs[:-3], refs[-3:]
    rows = held.shape[0] // len(peers)
    for j, half, share in zip(peers, halves, shares):
        held[j * rows : (j + 1) * rows, :] = share[...] if half is None else share[half]
    out[...] = jnp.dot(place[...], held[...], preferred_element_type=jnp.float32).astype(jnp.bfloat16)


def order(place, shares):
    size, share = place.shape[0], shares[0][1].shape[-1]
    peers, shares, halves = zip(*shares)
    vmem = pl.BlockSpec(memory_space=pltpu.VMEM)
    return pl.pallas_call(
        functools.partial(order_kernel, peers, halves),
        out_shape=jax.ShapeDtypeStruct((size, share), jnp.bfloat16),
        in_specs=[vmem] * (1 + len(shares)),
        out_specs=vmem,
        scratch_shapes=[pltpu.VMEM((size, share), jnp.bfloat16)],
        compiler_params=pltpu.CompilerParams(vmem_limit_bytes=LIMIT),
        name="order",
    )(*shares, place)


def on_device(amplitudes, amp_tiles, integrals, cd_tiles, q_owner):
    peers = lax.axis_size("wide")
    devices = lax.axis_size("narrow")
    rows = amplitudes.shape[0]

    odd, even = tuple(range(1, devices, 2)), tuple(range(0, devices, 2))
    middle = even[1:]

    def swap(value, j):
        return lax.ppermute(value, "wide", [(w, w ^ j) for w in range(peers)])

    def swap_line(value, mask):
        return lax.ppermute(value, "narrow", [(n, n ^ mask) for n in range(devices)])

    def first_step(message):
        return swap_line(message, 1)

    def later_steps(kept, come, after=()):
        terms = {0: [(come, 0)]}
        for i, r in enumerate(middle):
            terms[r] = [(kept, i), (come, odd.index(r ^ 1))]
        messages = []
        step = 1
        while 1 << step < devices:
            names = [r for r in sorted(terms) if r >> step & 1]
            messages += totals([terms.pop(r) for r in names], list(after))
            come = swap_line(messages[-1], 1 << step)
            for i, r in enumerate(names):
                terms[r ^ (1 << step)].append((come, i))
            step += 1
        return messages[0], terms[0]

    chips = peers // 2
    mine = (0, 1)
    near = [(2 * g, 2 * g + 1) for g in range(1, chips) if g & (g - 1) == 0]
    far = [(j,) for g in range(1, chips) if g & (g - 1) for j in (2 * g, 2 * g + 1)]

    def multiply(units, use, held=None, fetch=(), passed=(), after=(), limit=LIMIT):
        chosen = [lot[j] for unit in units for j in unit]
        outs, brought, passed = product(
            chosen, len(units), use, held, integrals, fetch, list(passed), list(after), limit
        )
        return dict(zip(units, outs)), *brought, passed

    lot = dict(enumerate(pick(amplitudes, amp_tiles, cd_tiles, q_owner)))
    for j in [1] + [j for unit in near for j in unit]:
        lot[j] = swap(lot[j], j)

    come, ready, sums = {}, {}, {}
    first, others = near[0], near[1:]
    all_odd, all_middle = tuple(range(len(odd))), tuple(range(len(middle)))
    away, odd_ints, _ = multiply([mine], all_odd, fetch=odd, limit=FIRST)
    come[mine] = first_step(away[mine])
    outs, middle_ints, passed = multiply(
        near, all_odd, odd_ints, middle, [lot[j] for j, in far], [away[mine]]
    )
    lot.update((j, swap(value, j)) for (j,), value in zip(far, passed))
    away.update(outs)
    come.update((u, first_step(away[u])) for u in near)
    kept, _ = multiply([mine] + near, all_middle, middle_ints, after=[come[mine]])
    ready[first], sums[first] = later_steps(kept[first], come[first])
    outs, home_ints, _ = multiply(far, all_odd, odd_ints, (0,), after=[ready[first]])
    away.update(outs)
    come.update((u, first_step(away[u])) for u in far)
    last = away[far[0]]
    for u in others:
        ready[u], sums[u] = later_steps(kept[u], come[u], [last])
        last = ready[u]
    outs, _ = multiply(far, all_middle, middle_ints, after=[last, sums[first][-1][0]])
    kept.update(outs)
    own, _ = multiply([mine] + near, (0,), home_ints, after=[kept[far[0]]])
    outs, _ = multiply(far, (0,), home_ints, after=[own[mine]])
    own.update(outs)
    place = place_of(q_owner, peers * rows, own[far[0]])

    shares = {}

    def close(u, after):
        terms = [[(own[u], 0)] + sums[u]]
        if u == mine:
            halves = totals(terms, after, halves=True)
            shares[0], shares[1] = (halves[0], None), (swap(halves[1], 1), None)
            return halves[1]
        whole, = totals(terms, after)
        j = u[0]
        got = swap(whole.reshape(len(u), rows, -1), j)
        shares[j] = got, 0
        if len(u) == 2:
            shares[j + 1] = swap(got[1], 1), None
        return whole

    last = close(first, [place])
    for u in far + [mine]:
        ready[u], sums[u] = later_steps(kept[u], come[u], [last])
        last = ready[u]
    for u in others + far + [mine]:
        last = close(u, [last])
    return order(place, [(j, *shares[j]) for u in far + near + [mine] for j in u]).reshape(rows, peers, -1)


def solution(mesh):
    placed = (P("wide", None, "narrow"), P(), P("wide", None, None, "narrow"), P(), P())
    return jax.shard_map(
        on_device, mesh=mesh, in_specs=placed, out_specs=P("wide", None, "narrow"), check_vma=False
    )
```

```python
import functools

import jax
import jax.numpy as jnp
from jax import lax
from jax.experimental import pallas as pl
from jax.experimental.pallas import tpu as pltpu
from jax.sharding import PartitionSpec as P

PART = 512
AHEAD = 3
COST = 1
LIMIT = 30 << 20
FIRST = 40 << 20


def pick_kernel(peers, wants, tables_from, amps, *refs):
    outs, (tables, held, slots, sem) = refs[:peers], refs[peers:]
    fetch = pltpu.make_async_copy(tables_from, tables, sem)
    fetch.start()
    width = amps.shape[1]
    for t in range(width):
        held[t] = amps[:, t, :]
    held[width] = jnp.zeros_like(held[width])
    fetch.wait()
    me = lax.axis_index("wide")

    def look(q, carry):
        peer = tables[width + wants, q] ^ me
        for k in range(wants):
            slot = jnp.int32(width)
            for t in range(width):
                slot = jnp.where(tables[t, me] == tables[width + k, q], t, slot)
            slots[peer, k] = slot
        return carry

    lax.fori_loop(0, peers, look, 0)
    for j in range(peers):
        for k in range(wants):
            outs[j][k] = held[slots[j, k]]


def pick(amplitudes, amp_tiles, cd_tiles, q_owner):
    rows, width, depth = amplitudes.shape
    peers, wants = cd_tiles.shape
    tables = jnp.concatenate([amp_tiles.T, cd_tiles.T, q_owner[None]], axis=0)
    vmem = pl.BlockSpec(memory_space=pltpu.VMEM)
    return pl.pallas_call(
        functools.partial(pick_kernel, peers, wants),
        out_shape=[jax.ShapeDtypeStruct((wants, rows, depth), jnp.bfloat16)] * peers,
        in_specs=[pl.BlockSpec(memory_space=pl.ANY), vmem],
        out_specs=[vmem] * peers,
        scratch_shapes=[
            pltpu.SMEM(tables.shape, jnp.int32),
            pltpu.VMEM((width + 1, rows, depth), jnp.bfloat16),
            pltpu.SMEM((peers, wants), jnp.int32),
            pltpu.SemaphoreType.DMA,
        ],
        compiler_params=pltpu.CompilerParams(vmem_limit_bytes=LIMIT),
        name="pick",
    )(tables, amplitudes)


def product_kernel(plan, *refs):
    refs = list(refs[plan["after"] :])
    picked = [refs.pop(0) for _ in range(plan["count"])]
    held = refs.pop(0) if plan["held"] else None
    ints = refs.pop(0) if plan["fetch"] else None
    del refs[: plan["passed"]]
    outs = [refs.pop(0) for _ in range(plan["chunks"])]
    brought = refs.pop(0) if plan["fetch"] else None
    left, sems = refs[-2:]
    source = held if plan["held"] else brought
    _, wants, share, depth = source.shape
    part = min(PART, share)
    blocks = [(s, i) for s in range(len(plan["fetch"])) for i in range(share // part)]

    def copies(n):
        s, i = blocks[n]
        start = pl.multiple_of((lax.axis_index("narrow") ^ plan["fetch"][s]) * share, share) + i * part
        return [
            pltpu.make_async_copy(
                ints.at[0, k, pl.ds(start, part), :], brought.at[s, k, pl.ds(i * part, part), :], sems.at[n, k]
            )
            for k in range(wants)
        ]

    def start(n):
        if n < len(blocks):
            for copy in copies(n):
                copy.start()

    def wait(n):
        for copy in copies(n):
            copy.wait()

    ahead = len(blocks) if plan["held"] else AHEAD
    for n in range(ahead):
        start(n)
    rows = picked[0].shape[1]
    for i, ref in enumerate(picked):
        for k in range(wants):
            left[k, i * rows : (i + 1) * rows, :] = ref[k]

    each = len(picked) * rows // len(outs)

    def block(o, s, i):
        at = slice(i * part, (i + 1) * part)
        total = None
        for k in range(wants):
            term = lax.dot_general(
                left[k], source[s, k, at, :], (((1,), (1,)), ((), ())), preferred_element_type=jnp.float32
            )
            total = term if total is None else total + term
        total = total.astype(jnp.bfloat16)
        for c, out in enumerate(outs):
            out[o, :, at] = total[c * each : (c + 1) * each]

    if plan["held"]:

        @pl.loop(0, len(plan["use"]))
        def _(o):
            for i in range(share // part):
                block(o, plan["use"][0] + o, i)

        for n in range(len(blocks)):
            wait(n)
    else:
        for n, (s, i) in enumerate(blocks):
            wait(n)
            start(n + ahead)
            block(s, s, i)


def product(picked, chunks, use, held, ints, fetch, passed, after, limit):
    _, wants, pairs, depth = ints.shape
    rows = picked[0].shape[1]
    share = pairs // lax.axis_size("narrow")
    count, shares = len(picked), len(use)
    plan = dict(
        count=count,
        chunks=chunks,
        use=use,
        held=held is not None,
        fetch=fetch,
        passed=len(passed),
        after=len(after),
    )
    vmem, any_space = pl.BlockSpec(memory_space=pltpu.VMEM), pl.BlockSpec(memory_space=pl.ANY)
    resident = ([held] if held is not None else []) + ([ints] if fetch else [])
    first_passed = len(after) + count + len(resident)
    outs = pl.pallas_call(
        functools.partial(product_kernel, plan),
        out_shape=[jax.ShapeDtypeStruct((shares, count * rows // chunks, share), jnp.bfloat16)] * chunks
        + [jax.ShapeDtypeStruct((len(fetch), wants, share, depth), jnp.bfloat16)] * bool(fetch)
        + [jax.ShapeDtypeStruct(p.shape, p.dtype) for p in passed],
        in_specs=[any_space] * len(after)
        + [vmem] * (count + (held is not None))
        + [any_space] * (bool(fetch) + len(passed)),
        out_specs=[vmem] * (chunks + bool(fetch)) + [any_space] * len(passed),
        input_output_aliases={first_passed + i: chunks + bool(fetch) + i for i in range(len(passed))},
        scratch_shapes=[
            pltpu.VMEM((wants, count * rows, depth), jnp.bfloat16),
            pltpu.SemaphoreType.DMA((max(1, len(fetch) * max(1, share // PART)), wants)),
        ],
        compiler_params=pltpu.CompilerParams(vmem_limit_bytes=limit),
        cost_estimate=pl.CostEstimate(
            flops=2 * 256 * wants * depth * share * shares // COST,
            bytes_accessed=2 * wants * depth * share * shares // COST,
            transcendentals=0,
        ),
        name="product",
    )(*after, *picked, *resident, *passed)
    return outs[:chunks], outs[chunks : chunks + bool(fetch)], outs[chunks + bool(fetch) :]


def total_kernel(places, halves, *refs):
    outs = refs[len(refs) - (2 if halves else 1) :]
    at = 0
    for o, own_places in enumerate(places):
        total = None
        for place in own_places:
            term = refs[at][place].astype(jnp.float32)
            total = term if total is None else total + term
            at += 1
        total = total.astype(jnp.bfloat16)
        if halves:
            rows = outs[0].shape[0]
            outs[0][...], outs[1][...] = total[:rows], total[rows:]
        else:
            outs[0][o] = total


def totals(lists, after, halves=False):
    terms = [term for terms in lists for term in terms]
    _, rows, share = terms[0][0].shape
    vmem, any_space = pl.BlockSpec(memory_space=pltpu.VMEM), pl.BlockSpec(memory_space=pl.ANY)
    shape = [(rows // 2, share)] * 2 if halves else [(len(lists), rows, share)]
    return pl.pallas_call(
        functools.partial(total_kernel, [[place for _, place in terms] for terms in lists], halves),
        out_shape=[jax.ShapeDtypeStruct(one, jnp.bfloat16) for one in shape],
        in_specs=[vmem] * len(terms) + [any_space] * len(after),
        out_specs=[vmem] * len(shape),
        compiler_params=pltpu.CompilerParams(vmem_limit_bytes=LIMIT),
        name="totals",
    )(*[array for array, _ in terms], *after)


def place_kernel(peers, q_owner, after, place):
    size = place.shape[0]
    me = lax.axis_index("wide")
    row = lax.broadcasted_iota(jnp.int32, (size, size), 0)
    column = lax.broadcasted_iota(jnp.int32, (size, size), 1)
    source = row // peers
    for q in range(peers):
        source += jnp.where(row % peers == q, (q_owner[q] ^ me) * (size // peers), 0)
    place[...] = (source == column).astype(jnp.bfloat16)


def place_of(q_owner, size, after):
    return pl.pallas_call(
        functools.partial(place_kernel, q_owner.shape[0]),
        out_shape=jax.ShapeDtypeStruct((size, size), jnp.bfloat16),
        in_specs=[pl.BlockSpec(memory_space=pltpu.SMEM), pl.BlockSpec(memory_space=pl.ANY)],
        out_specs=pl.BlockSpec(memory_space=pltpu.VMEM),
        compiler_params=pltpu.CompilerParams(vmem_limit_bytes=LIMIT),
        name="place",
    )(q_owner, after)


def order_kernel(peers, halves, *refs):
    shares, (place, out, held) = refs[:-3], refs[-3:]
    rows = held.shape[0] // len(peers)
    for j, half, share in zip(peers, halves, shares):
        held[j * rows : (j + 1) * rows, :] = share[...] if half is None else share[half]
    out[...] = jnp.dot(place[...], held[...], preferred_element_type=jnp.float32).astype(jnp.bfloat16)


def order(place, shares):
    size, share = place.shape[0], shares[0][1].shape[-1]
    peers, shares, halves = zip(*shares)
    vmem = pl.BlockSpec(memory_space=pltpu.VMEM)
    return pl.pallas_call(
        functools.partial(order_kernel, peers, halves),
        out_shape=jax.ShapeDtypeStruct((size, share), jnp.bfloat16),
        in_specs=[vmem] * (1 + len(shares)),
        out_specs=vmem,
        scratch_shapes=[pltpu.VMEM((size, share), jnp.bfloat16)],
        compiler_params=pltpu.CompilerParams(vmem_limit_bytes=LIMIT),
        name="order",
    )(*shares, place)


def on_device(amplitudes, amp_tiles, integrals, cd_tiles, q_owner):
    peers = lax.axis_size("wide")
    devices = lax.axis_size("narrow")
    rows = amplitudes.shape[0]

    odd, even = tuple(range(1, devices, 2)), tuple(range(0, devices, 2))
    middle = even[1:]

    def swap(value, j):
        return lax.ppermute(value, "wide", [(w, w ^ j) for w in range(peers)])

    def swap_line(value, mask):
        return lax.ppermute(value, "narrow", [(n, n ^ mask) for n in range(devices)])

    def first_step(message):
        return swap_line(message, 1)

    def later_steps(kept, come, after=()):
        terms = {0: [(come, 0)]}
        for i, r in enumerate(middle):
            terms[r] = [(kept, i + 1), (come, odd.index(r ^ 1))]
        messages = []
        step = 1
        while 1 << step < devices:
            names = [r for r in sorted(terms) if r >> step & 1]
            messages += totals([terms.pop(r) for r in names], list(after))
            come = swap_line(messages[-1], 1 << step)
            for i, r in enumerate(names):
                terms[r ^ (1 << step)].append((come, i))
            step += 1
        return messages[0], terms[0]

    chips = peers // 2
    mine = (0, 1)
    near = [(2 * g, 2 * g + 1) for g in range(1, chips) if g & (g - 1) == 0]
    far = [(j,) for g in range(1, chips) if g & (g - 1) for j in (2 * g, 2 * g + 1)]

    def multiply(units, use, held=None, fetch=(), passed=(), after=(), limit=LIMIT):
        chosen = [lot[j] for unit in units for j in unit]
        outs, brought, passed = product(
            chosen, len(units), use, held, integrals, fetch, list(passed), list(after), limit
        )
        return dict(zip(units, outs)), *brought, passed

    lot = dict(enumerate(pick(amplitudes, amp_tiles, cd_tiles, q_owner)))
    for j in [1] + [j for unit in near for j in unit]:
        lot[j] = swap(lot[j], j)

    come, ready, sums = {}, {}, {}
    first, others = near[0], near[1:]
    all_odd, all_even = tuple(range(len(odd))), tuple(range(len(even)))
    away, odd_ints, _ = multiply([mine], all_odd, fetch=odd, limit=FIRST)
    come[mine] = first_step(away[mine])
    outs, even_ints, passed = multiply(near, all_odd, odd_ints, even, [lot[j] for j, in far], [away[mine]])
    lot.update((j, swap(value, j)) for (j,), value in zip(far, passed))
    away.update(outs)
    come.update((u, first_step(away[u])) for u in near)
    kept, _ = multiply([mine] + near, all_even, even_ints, after=[come[mine]])
    place = place_of(q_owner, peers * rows, kept[mine])
    ready[first], sums[first] = later_steps(kept[first], come[first], [place])
    outs, _ = multiply(far, all_odd, odd_ints, after=[ready[first]])
    away.update(outs)
    come.update((u, first_step(away[u])) for u in far)
    last = away[far[0]]
    for u in others:
        ready[u], sums[u] = later_steps(kept[u], come[u], [last])
        last = ready[u]
    outs, _ = multiply(far, all_even, even_ints, after=[last, sums[first][-1][0]])
    kept.update(outs)

    shares = {}

    def close(u, after):
        terms = [[(kept[u], 0)] + sums[u]]
        if u == mine:
            halves = totals(terms, after, halves=True)
            shares[0], shares[1] = (halves[0], None), (swap(halves[1], 1), None)
            return halves[1]
        whole, = totals(terms, after)
        j = u[0]
        got = swap(whole.reshape(len(u), rows, -1), j)
        shares[j] = got, 0
        if len(u) == 2:
            shares[j + 1] = swap(got[1], 1), None
        return whole

    last = close(first, [kept[far[0]]])
    for u in far + [mine]:
        ready[u], sums[u] = later_steps(kept[u], come[u], [last])
        last = ready[u]
    for u in others + far:
        last = close(u, [last])
    close(mine, [last] + [shares[j][0] for j in first])
    return order(place, [(j, *shares[j]) for u in far + near + [mine] for j in u]).reshape(rows, peers, -1)


def solution(mesh):
    placed = (P("wide", None, "narrow"), P(), P("wide", None, None, "narrow"), P(), P())
    return jax.shard_map(
        on_device, mesh=mesh, in_specs=placed, out_specs=P("wide", None, "narrow"), check_vma=False
    )
```

```python
import functools

import jax
import jax.numpy as jnp
from jax import lax
from jax.experimental import pallas as pl
from jax.experimental.pallas import tpu as pltpu
from jax.sharding import PartitionSpec as P

PART = 512
AHEAD = 3
COST = 1
LIMIT = 30 << 20
FIRST = 40 << 20


def pick_kernel(peers, wants, tables_from, amps, *refs):
    outs, (tables, held, slots, sem) = refs[:peers], refs[peers:]
    fetch = pltpu.make_async_copy(tables_from, tables, sem)
    fetch.start()
    width = amps.shape[1]
    for t in range(width):
        held[t] = amps[:, t, :]
    held[width] = jnp.zeros_like(held[width])
    fetch.wait()
    me = lax.axis_index("wide")

    def look(q, carry):
        peer = tables[width + wants, q] ^ me
        for k in range(wants):
            slot = jnp.int32(width)
            for t in range(width):
                slot = jnp.where(tables[t, me] == tables[width + k, q], t, slot)
            slots[peer, k] = slot
        return carry

    lax.fori_loop(0, peers, look, 0)
    for j in range(peers):
        for k in range(wants):
            outs[j][k] = held[slots[j, k]]


def pick(amplitudes, amp_tiles, cd_tiles, q_owner):
    rows, width, depth = amplitudes.shape
    peers, wants = cd_tiles.shape
    tables = jnp.concatenate([amp_tiles.T, cd_tiles.T, q_owner[None]], axis=0)
    vmem = pl.BlockSpec(memory_space=pltpu.VMEM)
    return pl.pallas_call(
        functools.partial(pick_kernel, peers, wants),
        out_shape=[jax.ShapeDtypeStruct((wants, rows, depth), jnp.bfloat16)] * peers,
        in_specs=[pl.BlockSpec(memory_space=pl.ANY), vmem],
        out_specs=[vmem] * peers,
        scratch_shapes=[
            pltpu.SMEM(tables.shape, jnp.int32),
            pltpu.VMEM((width + 1, rows, depth), jnp.bfloat16),
            pltpu.SMEM((peers, wants), jnp.int32),
            pltpu.SemaphoreType.DMA,
        ],
        compiler_params=pltpu.CompilerParams(vmem_limit_bytes=LIMIT),
        name="pick",
    )(tables, amplitudes)


def product_kernel(plan, *refs):
    refs = list(refs[plan["after"] :])
    picked = [refs.pop(0) for _ in range(plan["count"])]
    held = refs.pop(0) if plan["held"] else None
    ints = refs.pop(0) if plan["fetch"] else None
    del refs[: plan["passed"]]
    outs = [refs.pop(0) for _ in range(plan["chunks"])]
    brought = refs.pop(0) if plan["fetch"] else None
    left, sems = refs[-2:]
    source = held if plan["held"] else brought
    _, wants, share, depth = source.shape
    part = min(PART, share)
    blocks = [(s, at, part) for s in range(len(plan["fetch"])) for at in range(0, share, part)]
    if not plan["held"]:
        s, at, _ = blocks.pop()
        blocks += [(s, at, part // 2), (s, at + part // 2, part // 2)]

    def copies(n):
        s, at, size = blocks[n]
        start = pl.multiple_of((lax.axis_index("narrow") ^ plan["fetch"][s]) * share, share) + at
        return [
            pltpu.make_async_copy(
                ints.at[0, k, pl.ds(start, size), :], brought.at[s, k, pl.ds(at, size), :], sems.at[n, k]
            )
            for k in range(wants)
        ]

    def start(n):
        if n < len(blocks):
            for copy in copies(n):
                copy.start()

    def wait(n):
        for copy in copies(n):
            copy.wait()

    ahead = len(blocks) if plan["held"] else AHEAD
    for n in range(ahead):
        start(n)
    rows = picked[0].shape[1]
    for i, ref in enumerate(picked):
        for k in range(wants):
            left[k, i * rows : (i + 1) * rows, :] = ref[k]

    each = len(picked) * rows // len(outs)

    def block(o, s, start, size):
        at = slice(start, start + size)
        total = None
        for k in range(wants):
            term = lax.dot_general(
                left[k], source[s, k, at, :], (((1,), (1,)), ((), ())), preferred_element_type=jnp.float32
            )
            total = term if total is None else total + term
        total = total.astype(jnp.bfloat16)
        for c, out in enumerate(outs):
            out[o, :, at] = total[c * each : (c + 1) * each]

    if plan["held"]:

        @pl.loop(0, len(plan["use"]))
        def _(o):
            for at in range(0, share, part):
                block(o, plan["use"][0] + o, at, part)

        for n in range(len(blocks)):
            wait(n)
    else:
        for n, (s, at, size) in enumerate(blocks):
            wait(n)
            start(n + ahead)
            block(s, s, at, size)


def product(picked, chunks, use, held, ints, fetch, passed, after, limit):
    _, wants, pairs, depth = ints.shape
    rows = picked[0].shape[1]
    share = pairs // lax.axis_size("narrow")
    count, shares = len(picked), len(use)
    plan = dict(
        count=count,
        chunks=chunks,
        use=use,
        held=held is not None,
        fetch=fetch,
        passed=len(passed),
        after=len(after),
    )
    vmem, any_space = pl.BlockSpec(memory_space=pltpu.VMEM), pl.BlockSpec(memory_space=pl.ANY)
    resident = ([held] if held is not None else []) + ([ints] if fetch else [])
    first_passed = len(after) + count + len(resident)
    outs = pl.pallas_call(
        functools.partial(product_kernel, plan),
        out_shape=[jax.ShapeDtypeStruct((shares, count * rows // chunks, share), jnp.bfloat16)] * chunks
        + [jax.ShapeDtypeStruct((len(fetch), wants, share, depth), jnp.bfloat16)] * bool(fetch)
        + [jax.ShapeDtypeStruct(p.shape, p.dtype) for p in passed],
        in_specs=[any_space] * len(after)
        + [vmem] * (count + (held is not None))
        + [any_space] * (bool(fetch) + len(passed)),
        out_specs=[vmem] * (chunks + bool(fetch)) + [any_space] * len(passed),
        input_output_aliases={first_passed + i: chunks + bool(fetch) + i for i in range(len(passed))},
        scratch_shapes=[
            pltpu.VMEM((wants, count * rows, depth), jnp.bfloat16),
            pltpu.SemaphoreType.DMA((1 + len(fetch) * max(1, share // PART), wants)),
        ],
        compiler_params=pltpu.CompilerParams(vmem_limit_bytes=limit),
        cost_estimate=pl.CostEstimate(
            flops=2 * 256 * wants * depth * share * shares // COST,
            bytes_accessed=2 * wants * depth * share * shares // COST,
            transcendentals=0,
        ),
        name="product",
    )(*after, *picked, *resident, *passed)
    return outs[:chunks], outs[chunks : chunks + bool(fetch)], outs[chunks + bool(fetch) :]


def total_kernel(places, halves, *refs):
    outs = refs[len(refs) - (2 if halves else 1) :]
    at = 0
    for o, own_places in enumerate(places):
        total = None
        for place in own_places:
            term = refs[at][place].astype(jnp.float32)
            total = term if total is None else total + term
            at += 1
        total = total.astype(jnp.bfloat16)
        if halves:
            rows = outs[0].shape[0]
            outs[0][...], outs[1][...] = total[:rows], total[rows:]
        else:
            outs[0][o] = total


def totals(lists, after, halves=False):
    terms = [term for terms in lists for term in terms]
    _, rows, share = terms[0][0].shape
    vmem, any_space = pl.BlockSpec(memory_space=pltpu.VMEM), pl.BlockSpec(memory_space=pl.ANY)
    shape = [(rows // 2, share)] * 2 if halves else [(len(lists), rows, share)]
    return pl.pallas_call(
        functools.partial(total_kernel, [[place for _, place in terms] for terms in lists], halves),
        out_shape=[jax.ShapeDtypeStruct(one, jnp.bfloat16) for one in shape],
        in_specs=[vmem] * len(terms) + [any_space] * len(after),
        out_specs=[vmem] * len(shape),
        compiler_params=pltpu.CompilerParams(vmem_limit_bytes=LIMIT),
        name="totals",
    )(*[array for array, _ in terms], *after)


def place_kernel(peers, q_owner, after, place):
    size = place.shape[0]
    me = lax.axis_index("wide")
    row = lax.broadcasted_iota(jnp.int32, (size, size), 0)
    column = lax.broadcasted_iota(jnp.int32, (size, size), 1)
    source = row // peers
    for q in range(peers):
        source += jnp.where(row % peers == q, (q_owner[q] ^ me) * (size // peers), 0)
    place[...] = (source == column).astype(jnp.bfloat16)


def place_of(q_owner, size, after):
    return pl.pallas_call(
        functools.partial(place_kernel, q_owner.shape[0]),
        out_shape=jax.ShapeDtypeStruct((size, size), jnp.bfloat16),
        in_specs=[pl.BlockSpec(memory_space=pltpu.SMEM), pl.BlockSpec(memory_space=pl.ANY)],
        out_specs=pl.BlockSpec(memory_space=pltpu.VMEM),
        compiler_params=pltpu.CompilerParams(vmem_limit_bytes=LIMIT),
        name="place",
    )(q_owner, after)


def order_kernel(peers, halves, *refs):
    shares, (place, out, held, ready, sems) = refs[:-5], refs[-5:]
    rows = held.shape[0] // len(peers)
    for j, half, share in zip(peers, halves, shares):
        held[j * rows : (j + 1) * rows, :] = share[...] if half is None else share[half]
    half = held.shape[1] // 2
    copies = []
    for c in range(2):
        at = slice(c * half, (c + 1) * half)
        ready[:, at] = jnp.dot(place[...], held[:, at], preferred_element_type=jnp.float32).astype(jnp.bfloat16)
        copies.append(pltpu.make_async_copy(ready.at[:, at], out.at[:, at], sems.at[c]))
        copies[c].start()
    for copy in copies:
        copy.wait()


def order(place, shares):
    size, share = place.shape[0], shares[0][1].shape[-1]
    peers, shares, halves = zip(*shares)
    vmem = pl.BlockSpec(memory_space=pltpu.VMEM)
    return pl.pallas_call(
        functools.partial(order_kernel, peers, halves),
        out_shape=jax.ShapeDtypeStruct((size, share), jnp.bfloat16),
        in_specs=[vmem] * (1 + len(shares)),
        out_specs=pl.BlockSpec(memory_space=pl.ANY),
        scratch_shapes=[
            pltpu.VMEM((size, share), jnp.bfloat16),
            pltpu.VMEM((size, share), jnp.bfloat16),
            pltpu.SemaphoreType.DMA((2,)),
        ],
        compiler_params=pltpu.CompilerParams(vmem_limit_bytes=LIMIT),
        name="order",
    )(*shares, place)


def on_device(amplitudes, amp_tiles, integrals, cd_tiles, q_owner):
    peers = lax.axis_size("wide")
    devices = lax.axis_size("narrow")
    rows = amplitudes.shape[0]

    odd, even = tuple(range(1, devices, 2)), tuple(range(0, devices, 2))
    middle = even[1:]

    def swap(value, j):
        return lax.ppermute(value, "wide", [(w, w ^ j) for w in range(peers)])

    def swap_line(value, mask):
        return lax.ppermute(value, "narrow", [(n, n ^ mask) for n in range(devices)])

    def first_step(message):
        return swap_line(message, 1)

    def later_steps(kept, come, after=()):
        terms = {0: [(come, 0)]}
        for i, r in enumerate(middle):
            terms[r] = [(kept, i + 1), (come, odd.index(r ^ 1))]
        messages = []
        step = 1
        while 1 << step < devices:
            names = [r for r in sorted(terms) if r >> step & 1]
            messages += totals([terms.pop(r) for r in names], list(after))
            come = swap_line(messages[-1], 1 << step)
            for i, r in enumerate(names):
                terms[r ^ (1 << step)].append((come, i))
            step += 1
        return messages[0], terms[0]

    chips = peers // 2
    mine = (0, 1)
    near = [(2 * g, 2 * g + 1) for g in range(1, chips) if g & (g - 1) == 0]
    far = [(j,) for g in range(1, chips) if g & (g - 1) for j in (2 * g, 2 * g + 1)]

    def multiply(units, use, held=None, fetch=(), passed=(), after=(), limit=LIMIT):
        chosen = [lot[j] for unit in units for j in unit]
        outs, brought, passed = product(
            chosen, len(units), use, held, integrals, fetch, list(passed), list(after), limit
        )
        return dict(zip(units, outs)), *brought, passed

    lot = dict(enumerate(pick(amplitudes, amp_tiles, cd_tiles, q_owner)))
    for j in [1] + [j for unit in near for j in unit]:
        lot[j] = swap(lot[j], j)

    come, ready, sums = {}, {}, {}
    first, others = near[0], near[1:]
    all_odd, all_even = tuple(range(len(odd))), tuple(range(len(even)))
    away, odd_ints, _ = multiply([mine], all_odd, fetch=odd, limit=FIRST)
    come[mine] = first_step(away[mine])
    outs, even_ints, passed = multiply(near, all_odd, odd_ints, even, [lot[j] for j, in far], [away[mine]])
    lot.update((j, swap(value, j)) for (j,), value in zip(far, passed))
    away.update(outs)
    come.update((u, first_step(away[u])) for u in near)
    kept, _ = multiply([mine] + near, all_even, even_ints, after=[come[mine]])
    place = place_of(q_owner, peers * rows, kept[mine])
    ready[first], sums[first] = later_steps(kept[first], come[first], [place])
    outs, _ = multiply(far, all_odd, odd_ints, after=[ready[first]])
    away.update(outs)
    come.update((u, first_step(away[u])) for u in far)
    last = away[far[0]]
    for u in others:
        ready[u], sums[u] = later_steps(kept[u], come[u], [last])
        last = ready[u]
    outs, _ = multiply(far, all_even, even_ints, after=[last, sums[first][-1][0]])
    kept.update(outs)

    shares = {}

    def close(u, after):
        terms = [[(kept[u], 0)] + sums[u]]
        if u == mine:
            halves = totals(terms, after, halves=True)
            shares[0], shares[1] = (halves[0], None), (swap(halves[1], 1), None)
            return halves[1]
        whole, = totals(terms, after)
        j = u[0]
        got = swap(whole.reshape(len(u), rows, -1), j)
        shares[j] = got, 0
        if len(u) == 2:
            shares[j + 1] = swap(got[1], 1), None
        return whole

    last = close(first, [kept[far[0]]])
    for u in far + [mine]:
        ready[u], sums[u] = later_steps(kept[u], come[u], [last])
        last = ready[u]
    for u in others:
        last = close(u, [last, shares[first[0]][0]])
    for u in far + [mine]:
        last = close(u, [last])
    return order(place, [(j, *shares[j]) for u in far + near + [mine] for j in u]).reshape(rows, peers, -1)


def solution(mesh):
    placed = (P("wide", None, "narrow"), P(), P("wide", None, None, "narrow"), P(), P())
    return jax.shard_map(
        on_device, mesh=mesh, in_specs=placed, out_specs=P("wide", None, "narrow"), check_vma=False
    )
```

```python
import functools

import jax
import jax.numpy as jnp
from jax import lax
from jax.experimental import pallas as pl
from jax.experimental.pallas import tpu as pltpu
from jax.sharding import PartitionSpec as P

PART = 512
AHEAD = 3
COST = 1
LIMIT = 30 << 20
FIRST = 40 << 20


def pick_kernel(peers, wants, tables_from, amps, *refs):
    outs, (tables, held, slots, sem) = refs[:peers], refs[peers:]
    fetch = pltpu.make_async_copy(tables_from, tables, sem)
    fetch.start()
    width = amps.shape[1]
    for t in range(width):
        held[t] = amps[:, t, :]
    held[width] = jnp.zeros_like(held[width])
    fetch.wait()
    me = lax.axis_index("wide")

    def look(q, carry):
        peer = tables[width + wants, q] ^ me
        for k in range(wants):
            slot = jnp.int32(width)
            for t in range(width):
                slot = jnp.where(tables[t, me] == tables[width + k, q], t, slot)
            slots[peer, k] = slot
        return carry

    lax.fori_loop(0, peers, look, 0)
    for j in range(peers):
        for k in range(wants):
            outs[j][k] = held[slots[j, k]]


def pick(amplitudes, amp_tiles, cd_tiles, q_owner):
    rows, width, depth = amplitudes.shape
    peers, wants = cd_tiles.shape
    tables = jnp.concatenate([amp_tiles.T, cd_tiles.T, q_owner[None]], axis=0)
    vmem = pl.BlockSpec(memory_space=pltpu.VMEM)
    return pl.pallas_call(
        functools.partial(pick_kernel, peers, wants),
        out_shape=[jax.ShapeDtypeStruct((wants, rows, depth), jnp.bfloat16)] * peers,
        in_specs=[pl.BlockSpec(memory_space=pl.ANY), vmem],
        out_specs=[vmem] * peers,
        scratch_shapes=[
            pltpu.SMEM(tables.shape, jnp.int32),
            pltpu.VMEM((width + 1, rows, depth), jnp.bfloat16),
            pltpu.SMEM((peers, wants), jnp.int32),
            pltpu.SemaphoreType.DMA,
        ],
        compiler_params=pltpu.CompilerParams(vmem_limit_bytes=LIMIT),
        name="pick",
    )(tables, amplitudes)


def product_kernel(plan, *refs):
    refs = list(refs[plan["after"] :])
    picked = [refs.pop(0) for _ in range(plan["count"])]
    held = refs.pop(0) if plan["held"] else None
    ints = refs.pop(0) if plan["fetch"] else None
    del refs[: plan["passed"]]
    outs = [refs.pop(0) for _ in range(plan["chunks"])]
    brought = refs.pop(0) if plan["fetch"] else None
    left, sems = refs[-2:]
    source = held if plan["held"] else brought
    _, wants, share, depth = source.shape
    part = min(PART, share)
    blocks = [(s, at, part) for s in range(len(plan["fetch"])) for at in range(0, share, part)]
    def copies(n):
        s, at, size = blocks[n]
        start = pl.multiple_of((lax.axis_index("narrow") ^ plan["fetch"][s]) * share, share) + at
        return [
            pltpu.make_async_copy(
                ints.at[0, k, pl.ds(start, size), :], brought.at[s, k, pl.ds(at, size), :], sems.at[n, k]
            )
            for k in range(wants)
        ]

    def start(n):
        if n < len(blocks):
            for copy in copies(n):
                copy.start()

    def wait(n):
        for copy in copies(n):
            copy.wait()

    ahead = len(blocks) if plan["held"] else AHEAD
    for n in range(ahead):
        start(n)
    rows = picked[0].shape[1]
    for i, ref in enumerate(picked):
        for k in range(wants):
            left[k, i * rows : (i + 1) * rows, :] = ref[k]

    each = len(picked) * rows // len(outs)

    def block(o, s, start, size):
        at = slice(start, start + size)
        total = None
        for k in range(wants):
            term = lax.dot_general(
                left[k], source[s, k, at, :], (((1,), (1,)), ((), ())), preferred_element_type=jnp.float32
            )
            total = term if total is None else total + term
        total = total.astype(jnp.bfloat16)
        for c, out in enumerate(outs):
            out[o, :, at] = total[c * each : (c + 1) * each]

    if plan["held"]:

        @pl.loop(0, len(plan["use"]))
        def _(o):
            for at in range(0, share, part):
                block(o, plan["use"][0] + o, at, part)

        for n in range(len(blocks)):
            wait(n)
    else:
        for n, (s, at, size) in enumerate(blocks):
            wait(n)
            start(n + ahead)
            block(s, s, at, size)


def product(picked, chunks, use, held, ints, fetch, passed, after, limit):
    _, wants, pairs, depth = ints.shape
    rows = picked[0].shape[1]
    share = pairs // lax.axis_size("narrow")
    count, shares = len(picked), len(use)
    plan = dict(
        count=count,
        chunks=chunks,
        use=use,
        held=held is not None,
        fetch=fetch,
        passed=len(passed),
        after=len(after),
    )
    vmem, any_space = pl.BlockSpec(memory_space=pltpu.VMEM), pl.BlockSpec(memory_space=pl.ANY)
    resident = ([held] if held is not None else []) + ([ints] if fetch else [])
    first_passed = len(after) + count + len(resident)
    outs = pl.pallas_call(
        functools.partial(product_kernel, plan),
        out_shape=[jax.ShapeDtypeStruct((shares, count * rows // chunks, share), jnp.bfloat16)] * chunks
        + [jax.ShapeDtypeStruct((len(fetch), wants, share, depth), jnp.bfloat16)] * bool(fetch)
        + [jax.ShapeDtypeStruct(p.shape, p.dtype) for p in passed],
        in_specs=[any_space] * len(after)
        + [vmem] * (count + (held is not None))
        + [any_space] * (bool(fetch) + len(passed)),
        out_specs=[vmem] * (chunks + bool(fetch)) + [any_space] * len(passed),
        input_output_aliases={first_passed + i: chunks + bool(fetch) + i for i in range(len(passed))},
        scratch_shapes=[
            pltpu.VMEM((wants, count * rows, depth), jnp.bfloat16),
            pltpu.SemaphoreType.DMA((1 + len(fetch) * max(1, share // PART), wants)),
        ],
        compiler_params=pltpu.CompilerParams(vmem_limit_bytes=limit),
        cost_estimate=pl.CostEstimate(
            flops=2 * 256 * wants * depth * share * shares // COST,
            bytes_accessed=2 * wants * depth * share * shares // COST,
            transcendentals=0,
        ),
        name="product",
    )(*after, *picked, *resident, *passed)
    return outs[:chunks], outs[chunks : chunks + bool(fetch)], outs[chunks + bool(fetch) :]


def total_kernel(places, halves, *refs):
    outs = refs[len(refs) - (2 if halves else 1) :]
    at = 0
    for o, own_places in enumerate(places):
        total = None
        for place in own_places:
            term = refs[at][place].astype(jnp.float32)
            total = term if total is None else total + term
            at += 1
        total = total.astype(jnp.bfloat16)
        if halves:
            rows = outs[0].shape[0]
            outs[0][...], outs[1][...] = total[:rows], total[rows:]
        else:
            outs[0][o] = total


def totals(lists, after, halves=False):
    terms = [term for terms in lists for term in terms]
    _, rows, share = terms[0][0].shape
    vmem, any_space = pl.BlockSpec(memory_space=pltpu.VMEM), pl.BlockSpec(memory_space=pl.ANY)
    shape = [(rows // 2, share)] * 2 if halves else [(len(lists), rows, share)]
    return pl.pallas_call(
        functools.partial(total_kernel, [[place for _, place in terms] for terms in lists], halves),
        out_shape=[jax.ShapeDtypeStruct(one, jnp.bfloat16) for one in shape],
        in_specs=[vmem] * len(terms) + [any_space] * len(after),
        out_specs=[vmem] * len(shape),
        compiler_params=pltpu.CompilerParams(vmem_limit_bytes=LIMIT),
        name="totals",
    )(*[array for array, _ in terms], *after)


def place_kernel(peers, q_owner, after, place):
    size = place.shape[0]
    me = lax.axis_index("wide")
    row = lax.broadcasted_iota(jnp.int32, (size, size), 0)
    column = lax.broadcasted_iota(jnp.int32, (size, size), 1)
    source = row // peers
    for q in range(peers):
        source += jnp.where(row % peers == q, (q_owner[q] ^ me) * (size // peers), 0)
    place[...] = (source == column).astype(jnp.bfloat16)


def place_of(q_owner, size, after):
    return pl.pallas_call(
        functools.partial(place_kernel, q_owner.shape[0]),
        out_shape=jax.ShapeDtypeStruct((size, size), jnp.bfloat16),
        in_specs=[pl.BlockSpec(memory_space=pltpu.SMEM), pl.BlockSpec(memory_space=pl.ANY)],
        out_specs=pl.BlockSpec(memory_space=pltpu.VMEM),
        compiler_params=pltpu.CompilerParams(vmem_limit_bytes=LIMIT),
        name="place",
    )(q_owner, after)


def order_kernel(peers, halves, *refs):
    shares, (place, out, held, ready, sems) = refs[:-5], refs[-5:]
    rows = held.shape[0] // len(peers)
    for j, half, share in zip(peers, halves, shares):
        held[j * rows : (j + 1) * rows, :] = share[...] if half is None else share[half]
    half = held.shape[1] // 2
    copies = []
    for c in range(2):
        at = slice(c * half, (c + 1) * half)
        ready[:, at] = jnp.dot(place[...], held[:, at], preferred_element_type=jnp.float32).astype(jnp.bfloat16)
        copies.append(pltpu.make_async_copy(ready.at[:, at], out.at[:, at], sems.at[c]))
        copies[c].start()
    for copy in copies:
        copy.wait()


def order(place, shares):
    size, share = place.shape[0], shares[0][1].shape[-1]
    peers, shares, halves = zip(*shares)
    vmem = pl.BlockSpec(memory_space=pltpu.VMEM)
    return pl.pallas_call(
        functools.partial(order_kernel, peers, halves),
        out_shape=jax.ShapeDtypeStruct((size, share), jnp.bfloat16),
        in_specs=[vmem] * (1 + len(shares)),
        out_specs=pl.BlockSpec(memory_space=pl.ANY),
        scratch_shapes=[
            pltpu.VMEM((size, share), jnp.bfloat16),
            pltpu.VMEM((size, share), jnp.bfloat16),
            pltpu.SemaphoreType.DMA((2,)),
        ],
        compiler_params=pltpu.CompilerParams(vmem_limit_bytes=LIMIT),
        name="order",
    )(*shares, place)


def on_device(amplitudes, amp_tiles, integrals, cd_tiles, q_owner):
    peers = lax.axis_size("wide")
    devices = lax.axis_size("narrow")
    rows = amplitudes.shape[0]

    odd, even = tuple(range(1, devices, 2)), tuple(range(0, devices, 2))
    middle = even[1:]

    def swap(value, j):
        return lax.ppermute(value, "wide", [(w, w ^ j) for w in range(peers)])

    def swap_line(value, mask):
        return lax.ppermute(value, "narrow", [(n, n ^ mask) for n in range(devices)])

    def first_step(message):
        return swap_line(message, 1)

    def later_steps(kept, come, after=()):
        terms = {0: [(come, 0)]}
        for i, r in enumerate(middle):
            terms[r] = [(kept, i + 1), (come, odd.index(r ^ 1))]
        messages = []
        step = 1
        while 1 << step < devices:
            names = [r for r in sorted(terms) if r >> step & 1]
            messages += totals([terms.pop(r) for r in names], list(after))
            come = swap_line(messages[-1], 1 << step)
            for i, r in enumerate(names):
                terms[r ^ (1 << step)].append((come, i))
            step += 1
        return messages[0], terms[0]

    chips = peers // 2
    mine = (0, 1)
    near = [(2 * g, 2 * g + 1) for g in range(1, chips) if g & (g - 1) == 0]
    far = [(j,) for g in range(1, chips) if g & (g - 1) for j in (2 * g, 2 * g + 1)]

    def multiply(units, use, held=None, fetch=(), passed=(), after=(), limit=LIMIT):
        chosen = [lot[j] for unit in units for j in unit]
        outs, brought, passed = product(
            chosen, len(units), use, held, integrals, fetch, list(passed), list(after), limit
        )
        return dict(zip(units, outs)), *brought, passed

    lot = dict(enumerate(pick(amplitudes, amp_tiles, cd_tiles, q_owner)))
    for j in [1] + [j for unit in near for j in unit]:
        lot[j] = swap(lot[j], j)

    come, ready, sums = {}, {}, {}
    first, others = near[0], near[1:]
    all_odd, all_even = tuple(range(len(odd))), tuple(range(len(even)))
    away, odd_ints, _ = multiply([mine], all_odd, fetch=odd, limit=FIRST)
    come[mine] = first_step(away[mine])
    outs, even_ints, passed = multiply(near, all_odd, odd_ints, even, [lot[j] for j, in far], [away[mine]])
    lot.update((j, swap(value, j)) for (j,), value in zip(far, passed))
    away.update(outs)
    come.update((u, first_step(away[u])) for u in near)
    kept, _ = multiply([mine] + near, all_even, even_ints, after=[come[mine]])
    place = place_of(q_owner, peers * rows, kept[mine])
    ready[first], sums[first] = later_steps(kept[first], come[first], [place])
    outs, _ = multiply(far, all_odd, odd_ints, after=[ready[first]])
    away.update(outs)
    come.update((u, first_step(away[u])) for u in far)
    last = away[far[0]]
    for u in others:
        ready[u], sums[u] = later_steps(kept[u], come[u], [last])
        last = ready[u]
    outs, _ = multiply(far, all_even, even_ints, after=[last, sums[first][-1][0]])
    kept.update(outs)

    shares = {}

    def close(u, after):
        terms = [[(kept[u], 0)] + sums[u]]
        if u == mine:
            halves = totals(terms, after, halves=True)
            shares[0], shares[1] = (halves[0], None), (swap(halves[1], 1), None)
            return halves[1]
        whole, = totals(terms, after)
        j = u[0]
        got = swap(whole.reshape(len(u), rows, -1), j)
        shares[j] = got, 0
        if len(u) == 2:
            shares[j + 1] = swap(got[1], 1), None
        return whole

    last = close(first, [kept[far[0]]])
    for u in far:
        ready[u], sums[u] = later_steps(kept[u], come[u], [last])
        last = ready[u]
    for u in others:
        last = close(u, [last, shares[first[0]][0]])
    last = close(far[0], [last])
    ready[mine], sums[mine] = later_steps(kept[mine], come[mine], [last])
    last = ready[mine]
    for u in far[1:] + [mine]:
        last = close(u, [last])
    return order(place, [(j, *shares[j]) for u in far + near + [mine] for j in u]).reshape(rows, peers, -1)


def solution(mesh):
    placed = (P("wide", None, "narrow"), P(), P("wide", None, None, "narrow"), P(), P())
    return jax.shard_map(
        on_device, mesh=mesh, in_specs=placed, out_specs=P("wide", None, "narrow"), check_vma=False
    )
```

```python
import functools

import jax
import jax.numpy as jnp
from jax import lax
from jax.experimental import pallas as pl
from jax.experimental.pallas import tpu as pltpu
from jax.sharding import PartitionSpec as P

PART = 512
AHEAD = 3
COST = 1
LIMIT = 30 << 20
FIRST = 40 << 20


def pick_kernel(peers, wants, tables_from, amps, *refs):
    outs, (tables, held, slots, sem) = refs[:peers], refs[peers:]
    fetch = pltpu.make_async_copy(tables_from, tables, sem)
    fetch.start()
    width = amps.shape[1]
    for t in range(width):
        held[t] = amps[:, t, :]
    held[width] = jnp.zeros_like(held[width])
    fetch.wait()
    me = lax.axis_index("wide")

    def look(q, carry):
        peer = tables[width + wants, q] ^ me
        for k in range(wants):
            slot = jnp.int32(width)
            for t in range(width):
                slot = jnp.where(tables[t, me] == tables[width + k, q], t, slot)
            slots[peer, k] = slot
        return carry

    lax.fori_loop(0, peers, look, 0)
    for j in range(peers):
        for k in range(wants):
            outs[j][k] = held[slots[j, k]]


def pick(amplitudes, amp_tiles, cd_tiles, q_owner):
    rows, width, depth = amplitudes.shape
    peers, wants = cd_tiles.shape
    tables = jnp.concatenate([amp_tiles.T, cd_tiles.T, q_owner[None]], axis=0)
    vmem = pl.BlockSpec(memory_space=pltpu.VMEM)
    return pl.pallas_call(
        functools.partial(pick_kernel, peers, wants),
        out_shape=[jax.ShapeDtypeStruct((wants, rows, depth), jnp.bfloat16)] * peers,
        in_specs=[pl.BlockSpec(memory_space=pl.ANY), vmem],
        out_specs=[vmem] * peers,
        scratch_shapes=[
            pltpu.SMEM(tables.shape, jnp.int32),
            pltpu.VMEM((width + 1, rows, depth), jnp.bfloat16),
            pltpu.SMEM((peers, wants), jnp.int32),
            pltpu.SemaphoreType.DMA,
        ],
        compiler_params=pltpu.CompilerParams(vmem_limit_bytes=LIMIT),
        name="pick",
    )(tables, amplitudes)


def product_kernel(plan, *refs):
    refs = list(refs[plan["after"] :])
    picked = [refs.pop(0) for _ in range(plan["count"])]
    held = refs.pop(0) if plan["held"] else None
    ints = refs.pop(0) if plan["fetch"] else None
    del refs[: plan["passed"]]
    outs = [refs.pop(0) for _ in range(plan["chunks"])]
    brought = refs.pop(0) if plan["fetch"] else None
    left, sems = refs[-2:]
    source = held if plan["held"] else brought
    _, wants, share, depth = source.shape
    part = min(PART, share)
    blocks = [(s, at, part) for s in range(len(plan["fetch"])) for at in range(0, share, part)]
    def copies(n):
        s, at, size = blocks[n]
        start = pl.multiple_of((lax.axis_index("narrow") ^ plan["fetch"][s]) * share, share) + at
        return [
            pltpu.make_async_copy(
                ints.at[0, k, pl.ds(start, size), :], brought.at[s, k, pl.ds(at, size), :], sems.at[n, k]
            )
            for k in range(wants)
        ]

    def start(n):
        if n < len(blocks):
            for copy in copies(n):
                copy.start()

    def wait(n):
        for copy in copies(n):
            copy.wait()

    ahead = len(blocks) if plan["held"] else AHEAD
    for n in range(ahead):
        start(n)
    rows = picked[0].shape[1]
    for i, ref in enumerate(picked):
        for k in range(wants):
            left[k, i * rows : (i + 1) * rows, :] = ref[k]

    each = len(picked) * rows // len(outs)

    def block(o, s, start, size):
        at = slice(start, start + size)
        total = None
        for k in range(wants):
            term = lax.dot_general(
                left[k], source[s, k, at, :], (((1,), (1,)), ((), ())), preferred_element_type=jnp.float32
            )
            total = term if total is None else total + term
        total = total.astype(jnp.bfloat16)
        for c, out in enumerate(outs):
            out[o, :, at] = total[c * each : (c + 1) * each]

    if plan["held"]:

        @pl.loop(0, len(plan["use"]))
        def _(o):
            for at in range(0, share, part):
                block(o, plan["use"][0] + o, at, part)

        for n in range(len(blocks)):
            wait(n)
    else:
        for n, (s, at, size) in enumerate(blocks):
            wait(n)
            start(n + ahead)
            block(s, s, at, size)


def product(picked, chunks, use, held, ints, fetch, passed, after, limit):
    _, wants, pairs, depth = ints.shape
    rows = picked[0].shape[1]
    share = pairs // lax.axis_size("narrow")
    count, shares = len(picked), len(use)
    plan = dict(
        count=count,
        chunks=chunks,
        use=use,
        held=held is not None,
        fetch=fetch,
        passed=len(passed),
        after=len(after),
    )
    vmem, any_space = pl.BlockSpec(memory_space=pltpu.VMEM), pl.BlockSpec(memory_space=pl.ANY)
    resident = ([held] if held is not None else []) + ([ints] if fetch else [])
    first_passed = len(after) + count + len(resident)
    outs = pl.pallas_call(
        functools.partial(product_kernel, plan),
        out_shape=[jax.ShapeDtypeStruct((shares, count * rows // chunks, share), jnp.bfloat16)] * chunks
        + [jax.ShapeDtypeStruct((len(fetch), wants, share, depth), jnp.bfloat16)] * bool(fetch)
        + [jax.ShapeDtypeStruct(p.shape, p.dtype) for p in passed],
        in_specs=[any_space] * len(after)
        + [vmem] * (count + (held is not None))
        + [any_space] * (bool(fetch) + len(passed)),
        out_specs=[vmem] * (chunks + bool(fetch)) + [any_space] * len(passed),
        input_output_aliases={first_passed + i: chunks + bool(fetch) + i for i in range(len(passed))},
        scratch_shapes=[
            pltpu.VMEM((wants, count * rows, depth), jnp.bfloat16),
            pltpu.SemaphoreType.DMA((1 + len(fetch) * max(1, share // PART), wants)),
        ],
        compiler_params=pltpu.CompilerParams(vmem_limit_bytes=limit),
        cost_estimate=pl.CostEstimate(
            flops=2 * 256 * wants * depth * share * shares // COST,
            bytes_accessed=2 * wants * depth * share * shares // COST,
            transcendentals=0,
        ),
        name="product",
    )(*after, *picked, *resident, *passed)
    return outs[:chunks], outs[chunks : chunks + bool(fetch)], outs[chunks + bool(fetch) :]


def total_kernel(places, halves, *refs):
    outs = refs[len(refs) - (2 if halves else 1) :]
    at = 0
    for o, own_places in enumerate(places):
        total = None
        for place in own_places:
            term = refs[at][place].astype(jnp.float32)
            total = term if total is None else total + term
            at += 1
        total = total.astype(jnp.bfloat16)
        if halves:
            rows = outs[0].shape[0]
            outs[0][...], outs[1][...] = total[:rows], total[rows:]
        else:
            outs[0][o] = total


def totals(lists, after, halves=False):
    terms = [term for terms in lists for term in terms]
    _, rows, share = terms[0][0].shape
    vmem, any_space = pl.BlockSpec(memory_space=pltpu.VMEM), pl.BlockSpec(memory_space=pl.ANY)
    shape = [(rows // 2, share)] * 2 if halves else [(len(lists), rows, share)]
    return pl.pallas_call(
        functools.partial(total_kernel, [[place for _, place in terms] for terms in lists], halves),
        out_shape=[jax.ShapeDtypeStruct(one, jnp.bfloat16) for one in shape],
        in_specs=[vmem] * len(terms) + [any_space] * len(after),
        out_specs=[vmem] * len(shape),
        compiler_params=pltpu.CompilerParams(vmem_limit_bytes=LIMIT),
        name="totals",
    )(*[array for array, _ in terms], *after)


def place_kernel(peers, q_owner, after, place):
    size = place.shape[0]
    me = lax.axis_index("wide")
    row = lax.broadcasted_iota(jnp.int32, (size, size), 0)
    column = lax.broadcasted_iota(jnp.int32, (size, size), 1)
    source = row // peers
    for q in range(peers):
        source += jnp.where(row % peers == q, (q_owner[q] ^ me) * (size // peers), 0)
    place[...] = (source == column).astype(jnp.bfloat16)


def place_of(q_owner, size, after):
    return pl.pallas_call(
        functools.partial(place_kernel, q_owner.shape[0]),
        out_shape=jax.ShapeDtypeStruct((size, size), jnp.bfloat16),
        in_specs=[pl.BlockSpec(memory_space=pltpu.SMEM), pl.BlockSpec(memory_space=pl.ANY)],
        out_specs=pl.BlockSpec(memory_space=pltpu.VMEM),
        compiler_params=pltpu.CompilerParams(vmem_limit_bytes=LIMIT),
        name="place",
    )(q_owner, after)


def order_kernel(peers, halves, *refs):
    shares, (place, out, held, ready, sems) = refs[:-5], refs[-5:]
    rows = held.shape[0] // len(peers)
    for j, half, share in zip(peers, halves, shares):
        held[j * rows : (j + 1) * rows, :] = share[...] if half is None else share[half]
    half = held.shape[1] // 2
    copies = []
    for c in range(2):
        at = slice(c * half, (c + 1) * half)
        ready[:, at] = jnp.dot(place[...], held[:, at], preferred_element_type=jnp.float32).astype(jnp.bfloat16)
        copies.append(pltpu.make_async_copy(ready.at[:, at], out.at[:, at], sems.at[c]))
        copies[c].start()
    for copy in copies:
        copy.wait()


def order(place, shares):
    size, share = place.shape[0], shares[0][1].shape[-1]
    peers, shares, halves = zip(*shares)
    vmem = pl.BlockSpec(memory_space=pltpu.VMEM)
    return pl.pallas_call(
        functools.partial(order_kernel, peers, halves),
        out_shape=jax.ShapeDtypeStruct((size, share), jnp.bfloat16),
        in_specs=[vmem] * (1 + len(shares)),
        out_specs=pl.BlockSpec(memory_space=pl.ANY),
        scratch_shapes=[
            pltpu.VMEM((size, share), jnp.bfloat16),
            pltpu.VMEM((size, share), jnp.bfloat16),
            pltpu.SemaphoreType.DMA((2,)),
        ],
        compiler_params=pltpu.CompilerParams(vmem_limit_bytes=LIMIT),
        name="order",
    )(*shares, place)


def on_device(amplitudes, amp_tiles, integrals, cd_tiles, q_owner):
    peers = lax.axis_size("wide")
    devices = lax.axis_size("narrow")
    rows = amplitudes.shape[0]

    odd, even = tuple(range(1, devices, 2)), tuple(range(0, devices, 2))
    middle = even[1:]

    def swap(value, j):
        return lax.ppermute(value, "wide", [(w, w ^ j) for w in range(peers)])

    def swap_line(value, mask):
        return lax.ppermute(value, "narrow", [(n, n ^ mask) for n in range(devices)])

    def first_step(message):
        return swap_line(message, 1)

    def later_steps(kept, come, after=()):
        terms = {0: [(come, 0)]}
        for i, r in enumerate(middle):
            terms[r] = [(kept, i + 1), (come, odd.index(r ^ 1))]
        messages = []
        step = 1
        while 1 << step < devices:
            names = [r for r in sorted(terms) if r >> step & 1]
            messages += totals([terms.pop(r) for r in names], list(after))
            come = swap_line(messages[-1], 1 << step)
            for i, r in enumerate(names):
                terms[r ^ (1 << step)].append((come, i))
            step += 1
        return messages[0], terms[0]

    chips = peers // 2
    mine = (0, 1)
    near = [(2 * g, 2 * g + 1) for g in range(1, chips) if g & (g - 1) == 0]
    far = [(j,) for g in range(1, chips) if g & (g - 1) for j in (2 * g, 2 * g + 1)]

    def multiply(units, use, held=None, fetch=(), passed=(), after=(), limit=LIMIT):
        chosen = [lot[j] for unit in units for j in unit]
        outs, brought, passed = product(
            chosen, len(units), use, held, integrals, fetch, list(passed), list(after), limit
        )
        return dict(zip(units, outs)), *brought, passed

    lot = dict(enumerate(pick(amplitudes, amp_tiles, cd_tiles, q_owner)))
    for j in [1] + [j for unit in near for j in unit]:
        lot[j] = swap(lot[j], j)

    come, ready, sums = {}, {}, {}
    first, others = near[0], near[1:]
    all_odd, all_even = tuple(range(len(odd))), tuple(range(len(even)))
    away, odd_ints, _ = multiply([mine], all_odd, fetch=odd, limit=FIRST)
    come[mine] = first_step(away[mine])
    outs, even_ints, passed = multiply(near, all_odd, odd_ints, even, [lot[j] for j, in far], [away[mine]])
    lot.update((j, swap(value, j)) for (j,), value in zip(far, passed))
    away.update(outs)
    come.update((u, first_step(away[u])) for u in near)
    kept, _ = multiply([mine] + near, all_even, even_ints, after=[come[mine]])
    place = place_of(q_owner, peers * rows, kept[mine])
    ready[first], sums[first] = later_steps(kept[first], come[first], [place])
    outs, _ = multiply(far, all_odd, odd_ints, after=[ready[first]])
    away.update(outs)
    come.update((u, first_step(away[u])) for u in far)
    outs, _ = multiply(far, all_even, even_ints, after=[away[far[0]]])
    kept.update(outs)
    last = kept[far[0]]
    for u in others:
        ready[u], sums[u] = later_steps(kept[u], come[u], [last, sums[first][-1][0]])
        last = ready[u]

    shares = {}

    def close(u, after):
        terms = [[(kept[u], 0)] + sums[u]]
        if u == mine:
            halves = totals(terms, after, halves=True)
            shares[0], shares[1] = (halves[0], None), (swap(halves[1], 1), None)
            return halves[1]
        whole, = totals(terms, after)
        j = u[0]
        got = swap(whole.reshape(len(u), rows, -1), j)
        shares[j] = got, 0
        if len(u) == 2:
            shares[j + 1] = swap(got[1], 1), None
        return whole

    last = close(first, [last])
    for u in far[::-1]:
        ready[u], sums[u] = later_steps(kept[u], come[u], [last])
        last = ready[u]
    for u in others:
        last = close(u, [last, shares[first[0]][0]])
    last = close(far[-1], [last])
    ready[mine], sums[mine] = later_steps(kept[mine], come[mine], [last])
    last = ready[mine]
    for u in far[:-1] + [mine]:
        last = close(u, [last])
    return order(place, [(j, *shares[j]) for u in far + near + [mine] for j in u]).reshape(rows, peers, -1)


def solution(mesh):
    placed = (P("wide", None, "narrow"), P(), P("wide", None, None, "narrow"), P(), P())
    return jax.shard_map(
        on_device, mesh=mesh, in_specs=placed, out_specs=P("wide", None, "narrow"), check_vma=False
    )
```

```python
import functools

import jax
import jax.numpy as jnp
from jax import lax
from jax.experimental import pallas as pl
from jax.experimental.pallas import tpu as pltpu
from jax.sharding import PartitionSpec as P

PART = 512
AHEAD = 3
COST = 1
LIMIT = 30 << 20
FIRST = 40 << 20


def pick_kernel(peers, wants, tables_from, amps, *refs):
    outs, (tables, held, slots, sem) = refs[:peers], refs[peers:]
    fetch = pltpu.make_async_copy(tables_from, tables, sem)
    fetch.start()
    width = amps.shape[1]
    for t in range(width):
        held[t] = amps[:, t, :]
    held[width] = jnp.zeros_like(held[width])
    fetch.wait()
    me = lax.axis_index("wide")

    def look(q, carry):
        peer = tables[width + wants, q] ^ me
        for k in range(wants):
            slot = jnp.int32(width)
            for t in range(width):
                slot = jnp.where(tables[t, me] == tables[width + k, q], t, slot)
            slots[peer, k] = slot
        return carry

    lax.fori_loop(0, peers, look, 0)
    for j in range(peers):
        for k in range(wants):
            outs[j][k] = held[slots[j, k]]


def pick(amplitudes, amp_tiles, cd_tiles, q_owner):
    rows, width, depth = amplitudes.shape
    peers, wants = cd_tiles.shape
    tables = jnp.concatenate([amp_tiles.T, cd_tiles.T, q_owner[None]], axis=0)
    vmem = pl.BlockSpec(memory_space=pltpu.VMEM)
    return pl.pallas_call(
        functools.partial(pick_kernel, peers, wants),
        out_shape=[jax.ShapeDtypeStruct((wants, rows, depth), jnp.bfloat16)] * peers,
        in_specs=[pl.BlockSpec(memory_space=pl.ANY), vmem],
        out_specs=[vmem] * peers,
        scratch_shapes=[
            pltpu.SMEM(tables.shape, jnp.int32),
            pltpu.VMEM((width + 1, rows, depth), jnp.bfloat16),
            pltpu.SMEM((peers, wants), jnp.int32),
            pltpu.SemaphoreType.DMA,
        ],
        compiler_params=pltpu.CompilerParams(vmem_limit_bytes=LIMIT),
        name="pick",
    )(tables, amplitudes)


def product_kernel(plan, *refs):
    refs = list(refs[plan["after"] :])
    picked = [refs.pop(0) for _ in range(plan["count"])]
    held = refs.pop(0) if plan["held"] else None
    ints = refs.pop(0) if plan["fetch"] else None
    del refs[: plan["passed"]]
    outs = [refs.pop(0) for _ in range(plan["chunks"])]
    brought = refs.pop(0) if plan["fetch"] else None
    left, sems = refs[-2:]
    source = held if plan["held"] else brought
    _, wants, share, depth = source.shape
    part = min(PART, share)
    blocks = [(s, at, part) for s in range(len(plan["fetch"])) for at in range(0, share, part)]
    def copies(n):
        s, at, size = blocks[n]
        start = pl.multiple_of((lax.axis_index("narrow") ^ plan["fetch"][s]) * share, share) + at
        return [
            pltpu.make_async_copy(
                ints.at[0, k, pl.ds(start, size), :], brought.at[s, k, pl.ds(at, size), :], sems.at[n, k]
            )
            for k in range(wants)
        ]

    def start(n):
        if n < len(blocks):
            for copy in copies(n):
                copy.start()

    def wait(n):
        for copy in copies(n):
            copy.wait()

    ahead = len(blocks) if plan["held"] else AHEAD
    for n in range(ahead):
        start(n)
    rows = picked[0].shape[1]
    for i, ref in enumerate(picked):
        for k in range(wants):
            left[k, i * rows : (i + 1) * rows, :] = ref[k]

    each = len(picked) * rows // len(outs)

    def block(o, s, start, size):
        at = slice(start, start + size)
        total = None
        for k in range(wants):
            term = lax.dot_general(
                left[k], source[s, k, at, :], (((1,), (1,)), ((), ())), preferred_element_type=jnp.float32
            )
            total = term if total is None else total + term
        total = total.astype(jnp.bfloat16)
        for c, out in enumerate(outs):
            out[o, :, at] = total[c * each : (c + 1) * each]

    if plan["held"]:

        @pl.loop(0, len(plan["use"]))
        def _(o):
            for at in range(0, share, part):
                block(o, plan["use"][0] + o, at, part)

        for n in range(len(blocks)):
            wait(n)
    else:
        for n, (s, at, size) in enumerate(blocks):
            wait(n)
            start(n + ahead)
            block(s, s, at, size)


def product(picked, chunks, use, held, ints, fetch, passed, after, limit):
    _, wants, pairs, depth = ints.shape
    rows = picked[0].shape[1]
    share = pairs // lax.axis_size("narrow")
    count, shares = len(picked), len(use)
    plan = dict(
        count=count,
        chunks=chunks,
        use=use,
        held=held is not None,
        fetch=fetch,
        passed=len(passed),
        after=len(after),
    )
    vmem, any_space = pl.BlockSpec(memory_space=pltpu.VMEM), pl.BlockSpec(memory_space=pl.ANY)
    resident = ([held] if held is not None else []) + ([ints] if fetch else [])
    first_passed = len(after) + count + len(resident)
    outs = pl.pallas_call(
        functools.partial(product_kernel, plan),
        out_shape=[jax.ShapeDtypeStruct((shares, count * rows // chunks, share), jnp.bfloat16)] * chunks
        + [jax.ShapeDtypeStruct((len(fetch), wants, share, depth), jnp.bfloat16)] * bool(fetch)
        + [jax.ShapeDtypeStruct(p.shape, p.dtype) for p in passed],
        in_specs=[any_space] * len(after)
        + [vmem] * (count + (held is not None))
        + [any_space] * (bool(fetch) + len(passed)),
        out_specs=[vmem] * (chunks + bool(fetch)) + [any_space] * len(passed),
        input_output_aliases={first_passed + i: chunks + bool(fetch) + i for i in range(len(passed))},
        scratch_shapes=[
            pltpu.VMEM((wants, count * rows, depth), jnp.bfloat16),
            pltpu.SemaphoreType.DMA((1 + len(fetch) * max(1, share // PART), wants)),
        ],
        compiler_params=pltpu.CompilerParams(vmem_limit_bytes=limit),
        cost_estimate=pl.CostEstimate(
            flops=2 * 256 * wants * depth * share * shares // COST,
            bytes_accessed=2 * wants * depth * share * shares // COST,
            transcendentals=0,
        ),
        name="product",
    )(*after, *picked, *resident, *passed)
    return outs[:chunks], outs[chunks : chunks + bool(fetch)], outs[chunks + bool(fetch) :]


def total_kernel(places, halves, *refs):
    outs = refs[len(refs) - (2 if halves else 1) :]
    at = 0
    for o, own_places in enumerate(places):
        total = None
        for place in own_places:
            term = refs[at][place].astype(jnp.float32)
            total = term if total is None else total + term
            at += 1
        total = total.astype(jnp.bfloat16)
        if halves:
            rows = outs[0].shape[0]
            outs[0][...], outs[1][...] = total[:rows], total[rows:]
        else:
            outs[0][o] = total


def totals(lists, after, halves=False):
    terms = [term for terms in lists for term in terms]
    _, rows, share = terms[0][0].shape
    vmem, any_space = pl.BlockSpec(memory_space=pltpu.VMEM), pl.BlockSpec(memory_space=pl.ANY)
    shape = [(rows // 2, share)] * 2 if halves else [(len(lists), rows, share)]
    return pl.pallas_call(
        functools.partial(total_kernel, [[place for _, place in terms] for terms in lists], halves),
        out_shape=[jax.ShapeDtypeStruct(one, jnp.bfloat16) for one in shape],
        in_specs=[vmem] * len(terms) + [any_space] * len(after),
        out_specs=[vmem] * len(shape),
        compiler_params=pltpu.CompilerParams(vmem_limit_bytes=LIMIT),
        name="totals",
    )(*[array for array, _ in terms], *after)


def place_kernel(peers, q_owner, after, place):
    size = place.shape[0]
    me = lax.axis_index("wide")
    row = lax.broadcasted_iota(jnp.int32, (size, size), 0)
    column = lax.broadcasted_iota(jnp.int32, (size, size), 1)
    source = row // peers
    for q in range(peers):
        source += jnp.where(row % peers == q, (q_owner[q] ^ me) * (size // peers), 0)
    place[...] = (source == column).astype(jnp.bfloat16)


def place_of(q_owner, size, after):
    return pl.pallas_call(
        functools.partial(place_kernel, q_owner.shape[0]),
        out_shape=jax.ShapeDtypeStruct((size, size), jnp.bfloat16),
        in_specs=[pl.BlockSpec(memory_space=pltpu.SMEM), pl.BlockSpec(memory_space=pl.ANY)],
        out_specs=pl.BlockSpec(memory_space=pltpu.VMEM),
        compiler_params=pltpu.CompilerParams(vmem_limit_bytes=LIMIT),
        name="place",
    )(q_owner, after)


def order_kernel(peers, halves, *refs):
    shares, (place, out, held, ready, sems) = refs[:-5], refs[-5:]
    rows = held.shape[0] // len(peers)
    for j, half, share in zip(peers, halves, shares):
        held[j * rows : (j + 1) * rows, :] = share[...] if half is None else share[half]
    half = held.shape[1] // 2
    copies = []
    for c in range(2):
        at = slice(c * half, (c + 1) * half)
        ready[:, at] = jnp.dot(place[...], held[:, at], preferred_element_type=jnp.float32).astype(jnp.bfloat16)
        copies.append(pltpu.make_async_copy(ready.at[:, at], out.at[:, at], sems.at[c]))
        copies[c].start()
    for copy in copies:
        copy.wait()


def order(place, shares):
    size, share = place.shape[0], shares[0][1].shape[-1]
    peers, shares, halves = zip(*shares)
    vmem = pl.BlockSpec(memory_space=pltpu.VMEM)
    return pl.pallas_call(
        functools.partial(order_kernel, peers, halves),
        out_shape=jax.ShapeDtypeStruct((size, share), jnp.bfloat16),
        in_specs=[vmem] * (1 + len(shares)),
        out_specs=pl.BlockSpec(memory_space=pl.ANY),
        scratch_shapes=[
            pltpu.VMEM((size, share), jnp.bfloat16),
            pltpu.VMEM((size, share), jnp.bfloat16),
            pltpu.SemaphoreType.DMA((2,)),
        ],
        compiler_params=pltpu.CompilerParams(vmem_limit_bytes=LIMIT),
        name="order",
    )(*shares, place)


def on_device(amplitudes, amp_tiles, integrals, cd_tiles, q_owner):
    peers = lax.axis_size("wide")
    devices = lax.axis_size("narrow")
    rows = amplitudes.shape[0]

    odd, even = tuple(range(1, devices, 2)), tuple(range(0, devices, 2))
    middle = even[1:]

    def swap(value, j):
        return lax.ppermute(value, "wide", [(w, w ^ j) for w in range(peers)])

    def swap_line(value, mask):
        return lax.ppermute(value, "narrow", [(n, n ^ mask) for n in range(devices)])

    def first_step(message):
        return swap_line(message, 1)

    def later_steps(kept, come, after=()):
        terms = {0: [(come, 0)]}
        for i, r in enumerate(middle):
            terms[r] = [(kept, i + 1), (come, odd.index(r ^ 1))]
        messages = []
        step = 1
        while 1 << step < devices:
            names = [r for r in sorted(terms) if r >> step & 1]
            messages += totals([terms.pop(r) for r in names], list(after))
            come = swap_line(messages[-1], 1 << step)
            for i, r in enumerate(names):
                terms[r ^ (1 << step)].append((come, i))
            step += 1
        return messages[0], terms[0]

    chips = peers // 2
    mine = (0, 1)
    near = [(2 * g, 2 * g + 1) for g in range(1, chips) if g & (g - 1) == 0]
    far = [(j,) for g in range(1, chips) if g & (g - 1) for j in (2 * g, 2 * g + 1)]

    def multiply(units, use, held=None, fetch=(), passed=(), after=(), limit=LIMIT):
        chosen = [lot[j] for unit in units for j in unit]
        outs, brought, passed = product(
            chosen, len(units), use, held, integrals, fetch, list(passed), list(after), limit
        )
        return dict(zip(units, outs)), *brought, passed

    lot = dict(enumerate(pick(amplitudes, amp_tiles, cd_tiles, q_owner)))
    for j in [1] + [j for unit in near for j in unit]:
        lot[j] = swap(lot[j], j)

    come, ready, sums = {}, {}, {}
    first, others = near[0], near[1:]
    all_odd, all_even = tuple(range(len(odd))), tuple(range(len(even)))
    away, odd_ints, _ = multiply([mine], all_odd, fetch=odd, limit=FIRST)
    come[mine] = first_step(away[mine])
    outs, even_ints, passed = multiply(near, all_odd, odd_ints, even, [lot[j] for j, in far], [away[mine]])
    lot.update((j, swap(value, j)) for (j,), value in zip(far, passed))
    away.update(outs)
    come.update((u, first_step(away[u])) for u in near)
    kept, _ = multiply([mine] + near, all_even, even_ints, after=[come[mine]])
    ready[mine], sums[mine] = later_steps(kept[mine], come[mine])
    place = place_of(q_owner, peers * rows, ready[mine])
    ready[first], sums[first] = later_steps(kept[first], come[first], [place])
    outs, _ = multiply(far, all_odd, odd_ints, after=[ready[first]])
    away.update(outs)
    come.update((u, first_step(away[u])) for u in far)
    last = away[far[0]]
    for u in others:
        ready[u], sums[u] = later_steps(kept[u], come[u], [last])
        last = ready[u]
    outs, _ = multiply(far, all_even, even_ints, after=[last, sums[first][-1][0], sums[mine][-1][0]])
    kept.update(outs)

    shares = {}

    def close(u, after):
        terms = [[(kept[u], 0)] + sums[u]]
        if u == mine:
            halves = totals(terms, after, halves=True)
            shares[0], shares[1] = (halves[0], None), (swap(halves[1], 1), None)
            return halves[1]
        whole, = totals(terms, after)
        j = u[0]
        got = swap(whole.reshape(len(u), rows, -1), j)
        shares[j] = got, 0
        if len(u) == 2:
            shares[j + 1] = swap(got[1], 1), None
        return whole

    last = close(first, [kept[far[0]]])
    for u in far:
        ready[u], sums[u] = later_steps(kept[u], come[u], [last])
        last = ready[u]
    last = close(mine, [last])
    for u in others:
        last = close(u, [last, shares[first[0]][0]])
    for u in far:
        last = close(u, [last])
    return order(place, [(j, *shares[j]) for u in far + near + [mine] for j in u]).reshape(rows, peers, -1)


def solution(mesh):
    placed = (P("wide", None, "narrow"), P(), P("wide", None, None, "narrow"), P(), P())
    return jax.shard_map(
        on_device, mesh=mesh, in_specs=placed, out_specs=P("wide", None, "narrow"), check_vma=False
    )
```

```python
import functools

import jax
import jax.numpy as jnp
from jax import lax
from jax.experimental import pallas as pl
from jax.experimental.pallas import tpu as pltpu
from jax.sharding import PartitionSpec as P

PART = 512
AHEAD = 3
COST = 1
LIMIT = 30 << 20
FIRST = 40 << 20


def pick_kernel(peers, wants, tables_from, amps, *refs):
    outs, (tables, held, slots, sem) = refs[:peers], refs[peers:]
    fetch = pltpu.make_async_copy(tables_from, tables, sem)
    fetch.start()
    width = amps.shape[1]
    for t in range(width):
        held[t] = amps[:, t, :]
    held[width] = jnp.zeros_like(held[width])
    fetch.wait()
    me = lax.axis_index("wide")

    def look(q, carry):
        peer = tables[width + wants, q] ^ me
        for k in range(wants):
            slot = jnp.int32(width)
            for t in range(width):
                slot = jnp.where(tables[t, me] == tables[width + k, q], t, slot)
            slots[peer, k] = slot
        return carry

    lax.fori_loop(0, peers, look, 0)
    for j in range(peers):
        for k in range(wants):
            outs[j][k] = held[slots[j, k]]


def pick(amplitudes, amp_tiles, cd_tiles, q_owner):
    rows, width, depth = amplitudes.shape
    peers, wants = cd_tiles.shape
    tables = jnp.concatenate([amp_tiles.T, cd_tiles.T, q_owner[None]], axis=0)
    vmem = pl.BlockSpec(memory_space=pltpu.VMEM)
    return pl.pallas_call(
        functools.partial(pick_kernel, peers, wants),
        out_shape=[jax.ShapeDtypeStruct((wants, rows, depth), jnp.bfloat16)] * peers,
        in_specs=[pl.BlockSpec(memory_space=pl.ANY), vmem],
        out_specs=[vmem] * peers,
        scratch_shapes=[
            pltpu.SMEM(tables.shape, jnp.int32),
            pltpu.VMEM((width + 1, rows, depth), jnp.bfloat16),
            pltpu.SMEM((peers, wants), jnp.int32),
            pltpu.SemaphoreType.DMA,
        ],
        compiler_params=pltpu.CompilerParams(vmem_limit_bytes=LIMIT),
        name="pick",
    )(tables, amplitudes)


def product_kernel(plan, *refs):
    refs = list(refs[plan["after"] :])
    picked = [refs.pop(0) for _ in range(plan["count"])]
    held = refs.pop(0) if plan["held"] else None
    ints = refs.pop(0) if plan["fetch"] else None
    del refs[: plan["passed"]]
    outs = [refs.pop(0) for _ in range(plan["chunks"])]
    brought = refs.pop(0) if plan["fetch"] else None
    left, sems = refs[-2:]
    source = held if plan["held"] else brought
    _, wants, share, depth = source.shape
    part = min(PART, share)
    blocks = [(s, at, part) for s in range(len(plan["fetch"])) for at in range(0, share, part)]
    def copies(n):
        s, at, size = blocks[n]
        start = pl.multiple_of((lax.axis_index("narrow") ^ plan["fetch"][s]) * share, share) + at
        return [
            pltpu.make_async_copy(
                ints.at[0, k, pl.ds(start, size), :], brought.at[s, k, pl.ds(at, size), :], sems.at[n, k]
            )
            for k in range(wants)
        ]

    def start(n):
        if n < len(blocks):
            for copy in copies(n):
                copy.start()

    def wait(n):
        for copy in copies(n):
            copy.wait()

    ahead = len(blocks) if plan["held"] else AHEAD
    for n in range(ahead):
        start(n)
    rows = picked[0].shape[1]
    for i, ref in enumerate(picked):
        for k in range(wants):
            left[k, i * rows : (i + 1) * rows, :] = ref[k]

    each = len(picked) * rows // len(outs)

    def block(o, s, start, size):
        at = slice(start, start + size)
        total = None
        for k in range(wants):
            term = lax.dot_general(
                left[k], source[s, k, at, :], (((1,), (1,)), ((), ())), preferred_element_type=jnp.float32
            )
            total = term if total is None else total + term
        total = total.astype(jnp.bfloat16)
        for c, out in enumerate(outs):
            out[o, :, at] = total[c * each : (c + 1) * each]

    if plan["held"]:

        @pl.loop(0, len(plan["use"]))
        def _(o):
            for at in range(0, share, part):
                block(o, plan["use"][0] + o, at, part)

        for n in range(len(blocks)):
            wait(n)
    else:
        for n, (s, at, size) in enumerate(blocks):
            wait(n)
            start(n + ahead)
            block(s, s, at, size)


def product(picked, chunks, use, held, ints, fetch, passed, after, limit):
    _, wants, pairs, depth = ints.shape
    rows = picked[0].shape[1]
    share = pairs // lax.axis_size("narrow")
    count, shares = len(picked), len(use)
    plan = dict(
        count=count,
        chunks=chunks,
        use=use,
        held=held is not None,
        fetch=fetch,
        passed=len(passed),
        after=len(after),
    )
    vmem, any_space = pl.BlockSpec(memory_space=pltpu.VMEM), pl.BlockSpec(memory_space=pl.ANY)
    resident = ([held] if held is not None else []) + ([ints] if fetch else [])
    first_passed = len(after) + count + len(resident)
    outs = pl.pallas_call(
        functools.partial(product_kernel, plan),
        out_shape=[jax.ShapeDtypeStruct((shares, count * rows // chunks, share), jnp.bfloat16)] * chunks
        + [jax.ShapeDtypeStruct((len(fetch), wants, share, depth), jnp.bfloat16)] * bool(fetch)
        + [jax.ShapeDtypeStruct(p.shape, p.dtype) for p in passed],
        in_specs=[any_space] * len(after)
        + [vmem] * (count + (held is not None))
        + [any_space] * (bool(fetch) + len(passed)),
        out_specs=[vmem] * (chunks + bool(fetch)) + [any_space] * len(passed),
        input_output_aliases={first_passed + i: chunks + bool(fetch) + i for i in range(len(passed))},
        scratch_shapes=[
            pltpu.VMEM((wants, count * rows, depth), jnp.bfloat16),
            pltpu.SemaphoreType.DMA((1 + len(fetch) * max(1, share // PART), wants)),
        ],
        compiler_params=pltpu.CompilerParams(vmem_limit_bytes=limit),
        cost_estimate=pl.CostEstimate(
            flops=2 * 256 * wants * depth * share * shares // COST,
            bytes_accessed=2 * wants * depth * share * shares // COST,
            transcendentals=0,
        ),
        name="product",
    )(*after, *picked, *resident, *passed)
    return outs[:chunks], outs[chunks : chunks + bool(fetch)], outs[chunks + bool(fetch) :]


def total_kernel(places, halves, *refs):
    outs = refs[len(refs) - (2 if halves else 1) :]
    at = 0
    for o, own_places in enumerate(places):
        total = None
        for place in own_places:
            term = refs[at][place].astype(jnp.float32)
            total = term if total is None else total + term
            at += 1
        total = total.astype(jnp.bfloat16)
        if halves:
            rows = outs[0].shape[0]
            outs[0][...], outs[1][...] = total[:rows], total[rows:]
        else:
            outs[0][o] = total


def totals(lists, after, halves=False):
    terms = [term for terms in lists for term in terms]
    _, rows, share = terms[0][0].shape
    vmem, any_space = pl.BlockSpec(memory_space=pltpu.VMEM), pl.BlockSpec(memory_space=pl.ANY)
    shape = [(rows // 2, share)] * 2 if halves else [(len(lists), rows, share)]
    return pl.pallas_call(
        functools.partial(total_kernel, [[place for _, place in terms] for terms in lists], halves),
        out_shape=[jax.ShapeDtypeStruct(one, jnp.bfloat16) for one in shape],
        in_specs=[vmem] * len(terms) + [any_space] * len(after),
        out_specs=[vmem] * len(shape),
        compiler_params=pltpu.CompilerParams(vmem_limit_bytes=LIMIT),
        name="totals",
    )(*[array for array, _ in terms], *after)


def place_kernel(peers, q_owner, after, place):
    size = place.shape[0]
    me = lax.axis_index("wide")
    row = lax.broadcasted_iota(jnp.int32, (size, size), 0)
    column = lax.broadcasted_iota(jnp.int32, (size, size), 1)
    source = row // peers
    for q in range(peers):
        source += jnp.where(row % peers == q, (q_owner[q] ^ me) * (size // peers), 0)
    place[...] = (source == column).astype(jnp.bfloat16)


def place_of(q_owner, size, after):
    return pl.pallas_call(
        functools.partial(place_kernel, q_owner.shape[0]),
        out_shape=jax.ShapeDtypeStruct((size, size), jnp.bfloat16),
        in_specs=[pl.BlockSpec(memory_space=pltpu.SMEM), pl.BlockSpec(memory_space=pl.ANY)],
        out_specs=pl.BlockSpec(memory_space=pltpu.VMEM),
        compiler_params=pltpu.CompilerParams(vmem_limit_bytes=LIMIT),
        name="place",
    )(q_owner, after)


def order_kernel(peers, halves, *refs):
    shares, (place, out, held, ready, sems) = refs[:-5], refs[-5:]
    rows = held.shape[0] // len(peers)
    for j, half, share in zip(peers, halves, shares):
        held[j * rows : (j + 1) * rows, :] = share[...] if half is None else share[half]
    half = held.shape[1] // 2
    copies = []
    for c in range(2):
        at = slice(c * half, (c + 1) * half)
        ready[:, at] = jnp.dot(place[...], held[:, at], preferred_element_type=jnp.float32).astype(jnp.bfloat16)
        copies.append(pltpu.make_async_copy(ready.at[:, at], out.at[:, at], sems.at[c]))
        copies[c].start()
    for copy in copies:
        copy.wait()


def order(place, shares):
    size, share = place.shape[0], shares[0][1].shape[-1]
    peers, shares, halves = zip(*shares)
    vmem = pl.BlockSpec(memory_space=pltpu.VMEM)
    return pl.pallas_call(
        functools.partial(order_kernel, peers, halves),
        out_shape=jax.ShapeDtypeStruct((size, share), jnp.bfloat16),
        in_specs=[vmem] * (1 + len(shares)),
        out_specs=pl.BlockSpec(memory_space=pl.ANY),
        scratch_shapes=[
            pltpu.VMEM((size, share), jnp.bfloat16),
            pltpu.VMEM((size, share), jnp.bfloat16),
            pltpu.SemaphoreType.DMA((2,)),
        ],
        compiler_params=pltpu.CompilerParams(vmem_limit_bytes=LIMIT),
        name="order",
    )(*shares, place)


def on_device(amplitudes, amp_tiles, integrals, cd_tiles, q_owner):
    peers = lax.axis_size("wide")
    devices = lax.axis_size("narrow")
    rows = amplitudes.shape[0]

    odd, even = tuple(range(1, devices, 2)), tuple(range(0, devices, 2))
    middle = even[1:]

    def swap(value, j):
        return lax.ppermute(value, "wide", [(w, w ^ j) for w in range(peers)])

    def swap_line(value, mask):
        return lax.ppermute(value, "narrow", [(n, n ^ mask) for n in range(devices)])

    def first_step(message):
        return swap_line(message, 1)

    def later_steps(kept, come, after=()):
        terms = {0: [(come, 0)]}
        for i, r in enumerate(middle):
            terms[r] = [(kept, i + 1), (come, odd.index(r ^ 1))]
        messages = []
        step = 1
        while 1 << step < devices:
            names = [r for r in sorted(terms) if r >> step & 1]
            messages += totals([terms.pop(r) for r in names], list(after))
            come = swap_line(messages[-1], 1 << step)
            for i, r in enumerate(names):
                terms[r ^ (1 << step)].append((come, i))
            step += 1
        return messages[0], terms[0]

    chips = peers // 2
    mine = (0, 1)
    near = [(2 * g, 2 * g + 1) for g in range(1, chips) if g & (g - 1) == 0]
    far = [(j,) for g in range(1, chips) if g & (g - 1) for j in (2 * g, 2 * g + 1)]

    def multiply(units, use, held=None, fetch=(), passed=(), after=(), limit=LIMIT):
        chosen = [lot[j] for unit in units for j in unit]
        outs, brought, passed = product(
            chosen, len(units), use, held, integrals, fetch, list(passed), list(after), limit
        )
        return dict(zip(units, outs)), *brought, passed

    lot = dict(enumerate(pick(amplitudes, amp_tiles, cd_tiles, q_owner)))
    for j in [1] + [j for unit in near for j in unit]:
        lot[j] = swap(lot[j], j)

    come, ready, sums = {}, {}, {}
    first, others = near[0], near[1:]
    all_odd, all_even = tuple(range(len(odd))), tuple(range(len(even)))
    away, odd_ints, _ = multiply([mine], all_odd, fetch=odd, limit=FIRST)
    come[mine] = first_step(away[mine])
    outs, even_ints, passed = multiply(near, all_odd, odd_ints, even, [lot[j] for j, in far], [away[mine]])
    lot.update((j, swap(value, j)) for (j,), value in zip(far, passed))
    away.update(outs)
    come.update((u, first_step(away[u])) for u in near)
    kept, _ = multiply([mine] + near, all_even, even_ints, after=[come[mine]])
    ready[mine], sums[mine] = later_steps(kept[mine], come[mine])
    place = place_of(q_owner, peers * rows, ready[mine])
    ready[first], sums[first] = later_steps(kept[first], come[first], [place])
    outs, _ = multiply(far, all_odd, odd_ints, after=[ready[first]])
    away.update(outs)
    come.update((u, first_step(away[u])) for u in far)
    last = away[far[0]]
    for u in others:
        ready[u], sums[u] = later_steps(kept[u], come[u], [last])
        last = ready[u]
    outs, _ = multiply(far, all_even, even_ints, after=[last, sums[mine][-1][0]])
    kept.update(outs)

    shares = {}

    def close(u, after):
        terms = [[(kept[u], 0)] + sums[u]]
        if u == mine:
            halves = totals(terms, after, halves=True)
            shares[0], shares[1] = (halves[0], None), (swap(halves[1], 1), None)
            return halves[1]
        whole, = totals(terms, after)
        j = u[0]
        got = swap(whole.reshape(len(u), rows, -1), j)
        shares[j] = got, 0
        if len(u) == 2:
            shares[j + 1] = swap(got[1], 1), None
        return whole

    last = close(first, [kept[far[0]]])
    for u in far:
        ready[u], sums[u] = later_steps(kept[u], come[u], [last])
        last = ready[u]
    last = close(mine, [last])
    for u in others:
        last = close(u, [last, shares[first[0]][0]])
    for u in far:
        last = close(u, [last])
    return order(place, [(j, *shares[j]) for u in far + near + [mine] for j in u]).reshape(rows, peers, -1)


def solution(mesh):
    placed = (P("wide", None, "narrow"), P(), P("wide", None, None, "narrow"), P(), P())
    return jax.shard_map(
        on_device, mesh=mesh, in_specs=placed, out_specs=P("wide", None, "narrow"), check_vma=False
    )
```

```python
import functools

import jax
import jax.numpy as jnp
from jax import lax
from jax.experimental import pallas as pl
from jax.experimental.pallas import tpu as pltpu
from jax.sharding import PartitionSpec as P

PART = 512
AHEAD = 4
COST = 1
LIMIT = 30 << 20
FIRST = 40 << 20


def pick_kernel(peers, wants, tables_from, amps, *refs):
    outs, (tables, held, slots, sem) = refs[:peers], refs[peers:]
    fetch = pltpu.make_async_copy(tables_from, tables, sem)
    fetch.start()
    width = amps.shape[1]
    for t in range(width):
        held[t] = amps[:, t, :]
    held[width] = jnp.zeros_like(held[width])
    fetch.wait()
    me = lax.axis_index("wide")

    def look(q, carry):
        peer = tables[width + wants, q] ^ me
        for k in range(wants):
            slot = jnp.int32(width)
            for t in range(width):
                slot = jnp.where(tables[t, me] == tables[width + k, q], t, slot)
            slots[peer, k] = slot
        return carry

    lax.fori_loop(0, peers, look, 0)
    for j in range(peers):
        for k in range(wants):
            outs[j][k] = held[slots[j, k]]


def pick(amplitudes, amp_tiles, cd_tiles, q_owner):
    rows, width, depth = amplitudes.shape
    peers, wants = cd_tiles.shape
    tables = jnp.concatenate([amp_tiles.T, cd_tiles.T, q_owner[None]], axis=0)
    vmem = pl.BlockSpec(memory_space=pltpu.VMEM)
    return pl.pallas_call(
        functools.partial(pick_kernel, peers, wants),
        out_shape=[jax.ShapeDtypeStruct((wants, rows, depth), jnp.bfloat16)] * peers,
        in_specs=[pl.BlockSpec(memory_space=pl.ANY), vmem],
        out_specs=[vmem] * peers,
        scratch_shapes=[
            pltpu.SMEM(tables.shape, jnp.int32),
            pltpu.VMEM((width + 1, rows, depth), jnp.bfloat16),
            pltpu.SMEM((peers, wants), jnp.int32),
            pltpu.SemaphoreType.DMA,
        ],
        compiler_params=pltpu.CompilerParams(vmem_limit_bytes=LIMIT),
        name="pick",
    )(tables, amplitudes)


def product_kernel(plan, *refs):
    refs = list(refs[plan["after"] :])
    picked = [refs.pop(0) for _ in range(plan["count"])]
    held = refs.pop(0) if plan["held"] else None
    ints = refs.pop(0) if plan["fetch"] else None
    del refs[: plan["passed"]]
    outs = [refs.pop(0) for _ in range(plan["chunks"])]
    brought = refs.pop(0) if plan["fetch"] else None
    left, sems = refs[-2:]
    source = held if plan["held"] else brought
    _, wants, share, depth = source.shape
    part = min(PART, share)
    blocks = [(s, at, part) for s in range(len(plan["fetch"])) for at in range(0, share, part)]
    def copies(n):
        s, at, size = blocks[n]
        start = pl.multiple_of((lax.axis_index("narrow") ^ plan["fetch"][s]) * share, share) + at
        return [
            pltpu.make_async_copy(
                ints.at[0, k, pl.ds(start, size), :], brought.at[s, k, pl.ds(at, size), :], sems.at[n, k]
            )
            for k in range(wants)
        ]

    def start(n):
        if n < len(blocks):
            for copy in copies(n):
                copy.start()

    def wait(n):
        for copy in copies(n):
            copy.wait()

    ahead = len(blocks) if plan["held"] else AHEAD
    for n in range(ahead):
        start(n)
    rows = picked[0].shape[1]
    for i, ref in enumerate(picked):
        for k in range(wants):
            left[k, i * rows : (i + 1) * rows, :] = ref[k]

    each = len(picked) * rows // len(outs)

    def block(o, s, start, size):
        at = slice(start, start + size)
        total = None
        for k in range(wants):
            term = lax.dot_general(
                left[k], source[s, k, at, :], (((1,), (1,)), ((), ())), preferred_element_type=jnp.float32
            )
            total = term if total is None else total + term
        total = total.astype(jnp.bfloat16)
        for c, out in enumerate(outs):
            out[o, :, at] = total[c * each : (c + 1) * each]

    if plan["held"]:

        @pl.loop(0, len(plan["use"]))
        def _(o):
            for at in range(0, share, part):
                block(o, plan["use"][0] + o, at, part)

        for n in range(len(blocks)):
            wait(n)
    else:
        for n, (s, at, size) in enumerate(blocks):
            wait(n)
            start(n + ahead)
            block(s, s, at, size)


def product(picked, chunks, use, held, ints, fetch, passed, after, limit):
    _, wants, pairs, depth = ints.shape
    rows = picked[0].shape[1]
    share = pairs // lax.axis_size("narrow")
    count, shares = len(picked), len(use)
    plan = dict(
        count=count,
        chunks=chunks,
        use=use,
        held=held is not None,
        fetch=fetch,
        passed=len(passed),
        after=len(after),
    )
    vmem, any_space = pl.BlockSpec(memory_space=pltpu.VMEM), pl.BlockSpec(memory_space=pl.ANY)
    resident = ([held] if held is not None else []) + ([ints] if fetch else [])
    first_passed = len(after) + count + len(resident)
    outs = pl.pallas_call(
        functools.partial(product_kernel, plan),
        out_shape=[jax.ShapeDtypeStruct((shares, count * rows // chunks, share), jnp.bfloat16)] * chunks
        + [jax.ShapeDtypeStruct((len(fetch), wants, share, depth), jnp.bfloat16)] * bool(fetch)
        + [jax.ShapeDtypeStruct(p.shape, p.dtype) for p in passed],
        in_specs=[any_space] * len(after)
        + [vmem] * (count + (held is not None))
        + [any_space] * (bool(fetch) + len(passed)),
        out_specs=[vmem] * (chunks + bool(fetch)) + [any_space] * len(passed),
        input_output_aliases={first_passed + i: chunks + bool(fetch) + i for i in range(len(passed))},
        scratch_shapes=[
            pltpu.VMEM((wants, count * rows, depth), jnp.bfloat16),
            pltpu.SemaphoreType.DMA((1 + len(fetch) * max(1, share // PART), wants)),
        ],
        compiler_params=pltpu.CompilerParams(vmem_limit_bytes=limit),
        cost_estimate=pl.CostEstimate(
            flops=2 * 256 * wants * depth * share * shares // COST,
            bytes_accessed=2 * wants * depth * share * shares // COST,
            transcendentals=0,
        ),
        name="product",
    )(*after, *picked, *resident, *passed)
    return outs[:chunks], outs[chunks : chunks + bool(fetch)], outs[chunks + bool(fetch) :]


def total_kernel(places, halves, *refs):
    outs = refs[len(refs) - (2 if halves else 1) :]
    at = 0
    for o, own_places in enumerate(places):
        total = None
        for place in own_places:
            term = refs[at][place].astype(jnp.float32)
            total = term if total is None else total + term
            at += 1
        total = total.astype(jnp.bfloat16)
        if halves:
            rows = outs[0].shape[0]
            outs[0][...], outs[1][...] = total[:rows], total[rows:]
        else:
            outs[0][o] = total


def totals(lists, after, halves=False):
    terms = [term for terms in lists for term in terms]
    _, rows, share = terms[0][0].shape
    vmem, any_space = pl.BlockSpec(memory_space=pltpu.VMEM), pl.BlockSpec(memory_space=pl.ANY)
    shape = [(rows // 2, share)] * 2 if halves else [(len(lists), rows, share)]
    return pl.pallas_call(
        functools.partial(total_kernel, [[place for _, place in terms] for terms in lists], halves),
        out_shape=[jax.ShapeDtypeStruct(one, jnp.bfloat16) for one in shape],
        in_specs=[vmem] * len(terms) + [any_space] * len(after),
        out_specs=[vmem] * len(shape),
        compiler_params=pltpu.CompilerParams(vmem_limit_bytes=LIMIT),
        name="totals",
    )(*[array for array, _ in terms], *after)


def place_kernel(peers, q_owner, after, place):
    size = place.shape[0]
    me = lax.axis_index("wide")
    row = lax.broadcasted_iota(jnp.int32, (size, size), 0)
    column = lax.broadcasted_iota(jnp.int32, (size, size), 1)
    source = row // peers
    for q in range(peers):
        source += jnp.where(row % peers == q, (q_owner[q] ^ me) * (size // peers), 0)
    place[...] = (source == column).astype(jnp.bfloat16)


def place_of(q_owner, size, after):
    return pl.pallas_call(
        functools.partial(place_kernel, q_owner.shape[0]),
        out_shape=jax.ShapeDtypeStruct((size, size), jnp.bfloat16),
        in_specs=[pl.BlockSpec(memory_space=pltpu.SMEM), pl.BlockSpec(memory_space=pl.ANY)],
        out_specs=pl.BlockSpec(memory_space=pltpu.VMEM),
        compiler_params=pltpu.CompilerParams(vmem_limit_bytes=LIMIT),
        name="place",
    )(q_owner, after)


def order_kernel(peers, halves, *refs):
    shares, (place, out, held, ready, sems) = refs[:-5], refs[-5:]
    rows = held.shape[0] // len(peers)
    for j, half, share in zip(peers, halves, shares):
        held[j * rows : (j + 1) * rows, :] = share[...] if half is None else share[half]
    half = held.shape[1] // 2
    copies = []
    for c in range(2):
        at = slice(c * half, (c + 1) * half)
        ready[:, at] = jnp.dot(place[...], held[:, at], preferred_element_type=jnp.float32).astype(jnp.bfloat16)
        copies.append(pltpu.make_async_copy(ready.at[:, at], out.at[:, at], sems.at[c]))
        copies[c].start()
    for copy in copies:
        copy.wait()


def order(place, shares):
    size, share = place.shape[0], shares[0][1].shape[-1]
    peers, shares, halves = zip(*shares)
    vmem = pl.BlockSpec(memory_space=pltpu.VMEM)
    return pl.pallas_call(
        functools.partial(order_kernel, peers, halves),
        out_shape=jax.ShapeDtypeStruct((size, share), jnp.bfloat16),
        in_specs=[vmem] * (1 + len(shares)),
        out_specs=pl.BlockSpec(memory_space=pl.ANY),
        scratch_shapes=[
            pltpu.VMEM((size, share), jnp.bfloat16),
            pltpu.VMEM((size, share), jnp.bfloat16),
            pltpu.SemaphoreType.DMA((2,)),
        ],
        compiler_params=pltpu.CompilerParams(vmem_limit_bytes=LIMIT),
        name="order",
    )(*shares, place)


def on_device(amplitudes, amp_tiles, integrals, cd_tiles, q_owner):
    peers = lax.axis_size("wide")
    devices = lax.axis_size("narrow")
    rows = amplitudes.shape[0]

    odd, even = tuple(range(1, devices, 2)), tuple(range(0, devices, 2))
    middle = even[1:]

    def swap(value, j):
        return lax.ppermute(value, "wide", [(w, w ^ j) for w in range(peers)])

    def swap_line(value, mask):
        return lax.ppermute(value, "narrow", [(n, n ^ mask) for n in range(devices)])

    def first_step(message):
        return swap_line(message, 1)

    def later_steps(kept, come, after=()):
        terms = {0: [(come, 0)]}
        for i, r in enumerate(middle):
            terms[r] = [(kept, i + 1), (come, odd.index(r ^ 1))]
        messages = []
        step = 1
        while 1 << step < devices:
            names = [r for r in sorted(terms) if r >> step & 1]
            messages += totals([terms.pop(r) for r in names], list(after))
            come = swap_line(messages[-1], 1 << step)
            for i, r in enumerate(names):
                terms[r ^ (1 << step)].append((come, i))
            step += 1
        return messages[0], terms[0]

    chips = peers // 2
    mine = (0, 1)
    near = [(2 * g, 2 * g + 1) for g in range(1, chips) if g & (g - 1) == 0]
    far = [(j,) for g in range(1, chips) if g & (g - 1) for j in (2 * g, 2 * g + 1)]

    def multiply(units, use, held=None, fetch=(), passed=(), after=(), limit=LIMIT):
        chosen = [lot[j] for unit in units for j in unit]
        outs, brought, passed = product(
            chosen, len(units), use, held, integrals, fetch, list(passed), list(after), limit
        )
        return dict(zip(units, outs)), *brought, passed

    lot = dict(enumerate(pick(amplitudes, amp_tiles, cd_tiles, q_owner)))
    for j in [1] + [j for unit in near for j in unit]:
        lot[j] = swap(lot[j], j)

    come, ready, sums = {}, {}, {}
    first, others = near[0], near[1:]
    all_odd, all_even = tuple(range(len(odd))), tuple(range(len(even)))
    away, odd_ints, _ = multiply([mine], all_odd, fetch=odd, limit=FIRST)
    come[mine] = first_step(away[mine])
    outs, even_ints, passed = multiply(near, all_odd, odd_ints, even, [lot[j] for j, in far], [away[mine]])
    lot.update((j, swap(value, j)) for (j,), value in zip(far, passed))
    away.update(outs)
    come.update((u, first_step(away[u])) for u in near)
    kept, _ = multiply([mine] + near, all_even, even_ints, after=[come[mine]])
    ready[mine], sums[mine] = later_steps(kept[mine], come[mine])
    place = place_of(q_owner, peers * rows, ready[mine])
    ready[first], sums[first] = later_steps(kept[first], come[first], [place])
    outs, _ = multiply(far, all_odd, odd_ints, after=[ready[first]])
    away.update(outs)
    come.update((u, first_step(away[u])) for u in far)
    last = away[far[0]]
    for u in others:
        ready[u], sums[u] = later_steps(kept[u], come[u], [last])
        last = ready[u]
    outs, _ = multiply(far, all_even, even_ints, after=[last, sums[mine][-1][0]])
    kept.update(outs)

    shares = {}

    def close(u, after):
        terms = [[(kept[u], 0)] + sums[u]]
        if u == mine:
            halves = totals(terms, after, halves=True)
            shares[0], shares[1] = (halves[0], None), (swap(halves[1], 1), None)
            return halves[1]
        whole, = totals(terms, after)
        j = u[0]
        got = swap(whole.reshape(len(u), rows, -1), j)
        shares[j] = got, 0
        if len(u) == 2:
            shares[j + 1] = swap(got[1], 1), None
        return whole

    last = close(first, [kept[far[0]]])
    for u in far:
        ready[u], sums[u] = later_steps(kept[u], come[u], [last])
        last = ready[u]
    last = close(mine, [last])
    for u in others:
        last = close(u, [last, shares[first[0]][0]])
    for u in far:
        last = close(u, [last])
    return order(place, [(j, *shares[j]) for u in far + near + [mine] for j in u]).reshape(rows, peers, -1)


def solution(mesh):
    placed = (P("wide", None, "narrow"), P(), P("wide", None, None, "narrow"), P(), P())
    return jax.shard_map(
        on_device, mesh=mesh, in_specs=placed, out_specs=P("wide", None, "narrow"), check_vma=False
    )
```
